32 devices in a mesh: dp: 16 (over z, y, x), fsdp: 2 (over core).
Axes of the slice: x: 2, y: 2, z: 4, core: 2. Of those that a mesh axis runs over, the one named last changes fastest.
Arguments:
- tokens: bfloat16 [256, 196, 768], P(('dp', 'fsdp')), may hold values from -6 to 6
- tissue: int32 [256, 196], P(('dp', 'fsdp')), may hold values from 0 to 1, as said below
- norm1_gain: bfloat16 [768], P('fsdp'), may hold values from 0.25 to 1.75
- norm1_shift: bfloat16 [768], P('fsdp'), may hold values from -1.75 to 1.75
- qkv_matrix: bfloat16 [768, 2304], P('fsdp'), may hold values from -0.21875 to 0.21875
- qkv_shift: bfloat16 [1536], P('fsdp'), may hold values from -3 to 3
- proj_matrix: bfloat16 [768, 768], P('fsdp'), may hold values from -0.875 to 0.875
- proj_shift: bfloat16 [768], P('fsdp'), may hold values from -1.75 to 1.75
- norm2_gain: bfloat16 [768], P('fsdp'), may hold values from 0.25 to 1.75
- norm2_shift: bfloat16 [768], P('fsdp'), may hold values from -1.75 to 1.75
- up_matrix: bfloat16 [768, 3072], P('fsdp'), may hold values from -0.21875 to 0.21875
- up_shift: bfloat16 [3072], P('fsdp'), may hold values from -3 to 3
- down_matrix: bfloat16 [3072, 768], P('fsdp'), may hold values from -0.109375 to 0.109375
- down_shift: bfloat16 [768], P('fsdp'), may hold values from -1.75 to 1.75
- cotangent: bfloat16 [256, 196, 768], P(('dp', 'fsdp')), may hold values from -6 to 6
Outputs:
- out_tokens: bfloat16 [256, 196, 768], P(('dp', 'fsdp'))
- tokens_grad: bfloat16 [256, 196, 768], P(('dp', 'fsdp'))
- norm1_gain_grad: float32 [768], P('fsdp')
- norm1_shift_grad: float32 [768], P('fsdp')
- qkv_matrix_grad: float32 [768, 2304], P('fsdp')
- qkv_shift_grad: float32 [1536], P('fsdp')
- proj_matrix_grad: float32 [768, 768], P('fsdp')
- proj_shift_grad: float32 [768], P('fsdp')
- norm2_gain_grad: float32 [768], P('fsdp')
- norm2_shift_grad: float32 [768], P('fsdp')
- up_matrix_grad: float32 [768, 3072], P('fsdp')
- up_shift_grad: float32 [3072], P('fsdp')
- down_matrix_grad: float32 [3072, 768], P('fsdp')
- down_shift_grad: float32 [768], P('fsdp')
The draws below stay inside these ranges and needn't reach their ends.
Inputs may be any that keep to these rules, and one draw needn't show every extreme that they name: `tissue`: each image has at least one patch slot of value 1.
All inputs are finite; a program needn't handle non-finite values.
Results may differ from the reference program's by a relative error of at most 0.02.
Values may be sent and summed in bfloat16 or wider, within the bound.
A program may use at most 256 MiB of HBM per device.

```python
import math
import jax
import jax.numpy as jnp
from jax import lax

D = 768
HEADS = 12
FF = 3072
P_SIZE = 196
IMG_DEV = 8
IMAGES = 256
N_FSDP = 2


def draw_tissue(key, part):
    key = jax.random.fold_in(key, 7)
    count_key, order_key = jax.random.split(key)
    tissue_count = jax.random.randint(count_key, (IMAGES, 1), 1, P_SIZE + 1)
    image_keys = jax.random.split(order_key, IMAGES)
    order_rows = jax.vmap(lambda image_key: jax.random.permutation(image_key, P_SIZE))(image_keys)
    return (order_rows < tissue_count).astype(jnp.int32)


def steps_of(own_key, extent, cuts, low, high):
    factor_of = 1.0
    for dim, shards_of in cuts:
        steps = jax.random.uniform(jax.random.fold_in(jax.random.fold_in(own_key, 6), dim), (shards_of,), jnp.float32, low / len(cuts), high / len(cuts))
        factor_of = factor_of * jnp.repeat(jnp.exp(steps), extent[dim] // shards_of).reshape((-1,) + (1,) * (len(extent) - 1 - dim))
    return factor_of


def normal_values(own_key, dims, width, reach, shards=(), dtype=jnp.bfloat16):
    entries = width * jax.random.normal(own_key, dims, jnp.float32)
    if shards:
        entries = entries * steps_of(own_key, dims, shards, -0.22, 0.18)
    return jnp.clip(entries, -reach, reach).astype(dtype)


def setup_inputs(seed: int = 0) -> dict:
    arg_keys = jax.random.split(jax.random.key(seed), 16)
    return {
        "tokens": normal_values(arg_keys[0], (IMAGES, P_SIZE, D), 1.0, 6.0, ((0, 32),)),
        "tissue": draw_tissue(jax.random.fold_in(arg_keys[15], 71), 0),
        "norm1_gain": jnp.clip(1.0 + 0.15 * jax.random.normal(arg_keys[2], (D,), jnp.float32), 0.25, 1.75).astype(jnp.bfloat16),
        "norm1_shift": normal_values(arg_keys[3], (D,), 0.3, 1.75, ((0, 2),)),
        "qkv_matrix": normal_values(arg_keys[4], (D, 3 * D), D ** -0.5, 0.21875, ((0, 2),)),
        "qkv_shift": normal_values(arg_keys[5], (2 * D,), 0.5, 3.0, ((0, 2),)),
        "proj_matrix": normal_values(arg_keys[6], (D, D), (D // 16) ** -0.5, 0.875, ((0, 2),)),
        "proj_shift": normal_values(arg_keys[7], (D,), 0.3, 1.75, ((0, 2),)),
        "norm2_gain": jnp.clip(1.0 + 0.15 * jax.random.normal(arg_keys[8], (D,), jnp.float32), 0.25, 1.75).astype(jnp.bfloat16),
        "norm2_shift": normal_values(arg_keys[9], (D,), 0.3, 1.75, ((0, 2),)),
        "up_matrix": normal_values(arg_keys[10], (D, FF), D ** -0.5, 0.21875, ((0, 2),)),
        "up_shift": normal_values(arg_keys[11], (FF,), 0.5, 3.0, ((0, 2),)),
        "down_matrix": normal_values(arg_keys[12], (FF, D), FF ** -0.5, 0.109375, ((0, 2),)),
        "down_shift": normal_values(arg_keys[13], (D,), 0.3, 1.75, ((0, 2),)),
        "cotangent": normal_values(arg_keys[14], (IMAGES, P_SIZE, D), 1.0, 6.0, ((0, 32),)),
    }


@jax.custom_vjp
def low(v):
    return lax.optimization_barrier(v.astype(jnp.bfloat16)).astype(jnp.float32)

@jax.custom_vjp
def low_back(v):
    return v

def low_keep(v):
    return (low(v), None)

def low_pass(kept, grad):
    return (grad,)

def back_keep(v):
    return (v, None)

def back_low(kept, grad):
    return (low(grad),)
low.defvjp(low_keep, low_pass)
low_back.defvjp(back_keep, back_low)
norm_eps = 1e-06

def layer_norm(features_in, gain_row, shift_row):
    row_mean = lax.optimization_barrier(jnp.mean(features_in, axis=-1, keepdims=True))
    centred = features_in - row_mean
    row_var = lax.optimization_barrier(jnp.mean(centred * centred, axis=-1, keepdims=True))
    return centred * lax.rsqrt(row_var + norm_eps) * gain_row + shift_row

def project(rows_in, matrix):
    return jnp.einsum('bpd,de->bpe', rows_in, matrix, precision=lax.Precision.HIGHEST)

def forward_block(inputs, tissue_rows, weights):
    norm1_gain, norm1_shift, qkv_matrix, qkv_shift, proj_matrix, proj_shift, norm2_gain, norm2_shift, up_matrix, up_shift, down_matrix, down_shift = weights
    images, patches, features = inputs.shape
    head_dim = features // HEADS
    first_in = low(layer_norm(inputs, norm1_gain, norm1_shift))
    zeros_key = jnp.zeros((features,), jnp.float32)
    shift_all = jnp.concatenate([qkv_shift[:features], zeros_key, qkv_shift[features:]])
    qkv_rows = low(low_back(project(first_in, qkv_matrix) + shift_all))
    qkv_split = qkv_rows.reshape(images, patches, 3, HEADS, head_dim)
    queries = qkv_split[:, :, 0]
    key_rows = qkv_split[:, :, 1]
    value_rows = qkv_split[:, :, 2]
    score_scale = 1.0 / math.sqrt(head_dim)
    raw_scores = low_back(jnp.einsum('bqhd,bkhd->bhqk', queries, key_rows, precision=lax.Precision.HIGHEST) * score_scale)
    key_valid = tissue_rows > 0
    scores = jnp.where(key_valid[:, None, None, :], raw_scores, -1e+30)
    row_max = lax.optimization_barrier(jnp.max(scores, axis=-1, keepdims=True))
    shifted_exp = jnp.exp(scores - row_max)
    softmax = shifted_exp / lax.optimization_barrier(jnp.sum(shifted_exp, axis=-1, keepdims=True))
    mixed_heads = low_back(jnp.einsum('bhqk,bkhd->bqhd', low(softmax), value_rows, precision=lax.Precision.HIGHEST))
    weight_rows = tissue_rows.astype(jnp.float32)[:, :, None, None]
    heads_out = low((mixed_heads * weight_rows).reshape(images, patches, features))
    residual = inputs + low_back(project(heads_out, proj_matrix) + proj_shift)
    second_in = low(layer_norm(residual, norm2_gain, norm2_shift))
    hidden = low_back(project(second_in, up_matrix) + up_shift)
    active = low(jax.nn.gelu(hidden, approximate=False))
    return residual + low_back(project(active, down_matrix) + down_shift)

def reference(tokens, tissue, norm1_gain, norm1_shift, qkv_matrix, qkv_shift, proj_matrix, proj_shift, norm2_gain, norm2_shift, up_matrix, up_shift, down_matrix, down_shift, cotangent):
    weights = tuple((member.astype(jnp.float32) for member in (norm1_gain, norm1_shift, qkv_matrix, qkv_shift, proj_matrix, proj_shift, norm2_gain, norm2_shift, up_matrix, up_shift, down_matrix, down_shift)))
    group_size = IMG_DEV * N_FSDP
    group_count = IMAGES // group_size
    grouped = tokens.astype(jnp.float32).reshape(group_count, group_size, P_SIZE, D)
    tissue_groups = tissue.reshape(group_count, group_size, P_SIZE)

    def forward(grouped_in, weight_set):
        checked = jax.checkpoint(forward_block)
        return lax.map(lambda pair_in: checked(pair_in[0], pair_in[1], weight_set), (grouped_in, tissue_groups))
    outputs, pull_back = jax.vjp(forward, grouped, weights)
    grad_tokens, grad_weights = pull_back(cotangent.astype(jnp.float32).reshape(group_count, group_size, P_SIZE, D))
    return (outputs.reshape(IMAGES, P_SIZE, D).astype(jnp.bfloat16), grad_tokens.reshape(IMAGES, P_SIZE, D).astype(jnp.bfloat16), grad_weights[0], grad_weights[1], grad_weights[2], grad_weights[3], grad_weights[4], grad_weights[5], grad_weights[6], grad_weights[7], grad_weights[8], grad_weights[9], grad_weights[10], grad_weights[11])
```

```python
import functools

import jax
import jax.numpy as jnp
from jax import lax
from jax.experimental import pallas as pl
from jax.experimental.pallas import tpu as pltpu
from jax.sharding import PartitionSpec as P

HEADS = 12
EPS = 1e-06
BF = jnp.bfloat16
F32 = jnp.float32
MESH = pl.DeviceIdType.MESH
ERF = (0.254829592, -0.284496736, 1.421413741, -1.453152027, 1.061405429)


def dot(a, b, ca, cb):
    return lax.dot_general(a, b, (((ca,), (cb,)), ((), ())), preferred_element_type=F32)


def aligned(start, size, step):
    if isinstance(start, int):
        return pl.ds(start, size)
    return pl.ds(pl.multiple_of(start, step), size)


def gelu_both(h):
    t = 1.0 / (1.0 + (0.3275911 * 0.7071067811865476) * jnp.abs(h))
    e = jnp.exp(-0.5 * h * h)
    tail = t * (ERF[0] + t * (ERF[1] + t * (ERF[2] + t * (ERF[3] + t * ERF[4])))) * (0.5 * e)
    cdf = jnp.where(h >= 0, 1.0 - tail, tail)
    return h * cdf, cdf + h * e * 0.3989422804014327


def normalized(v):
    mean = jnp.mean(v, axis=-1, keepdims=True)
    centred = v - mean
    var = jnp.mean(centred * centred, axis=-1, keepdims=True)
    rstd = lax.rsqrt(var + EPS)
    return centred * rstd, rstd


def head_masks(scale):
    lane = lax.broadcasted_iota(jnp.int32, (1, 128), 1)
    return [
        jnp.where(lane < 64, scale, 0.0).astype(BF),
        jnp.where(lane >= 64, scale, 0.0).astype(BF),
    ]


def front_kernel(
    x_hbm, cot_hbm, tissue, g1, b1, qkv_w_hbm, qkv_b, proj_w_hbm, proj_b, g2, b2,
    xp_o, cotp_o, first_o, qkv_o, pt_o, ho_o, res_o, s2_o, tb_o,
    x3, cot3, xp, cotp, first, qkv_w, qkv, pt, ho, proj_w, res, s2, tb, sem, osem, psem,
):
    images, slots, width = x3.shape
    padded = xp.shape[0] // images
    scores_w = pt.shape[-1]

    loads = {
        "x": pltpu.make_async_copy(x_hbm, x3, sem.at[0]),
        "qkv_w": pltpu.make_async_copy(qkv_w_hbm, qkv_w, sem.at[1]),
        "proj_w": pltpu.make_async_copy(proj_w_hbm, proj_w, sem.at[2]),
        "cot": pltpu.make_async_copy(cot_hbm, cot3, sem.at[3]),
    }
    for copy in loads.values():
        copy.start()
    stores = []

    def store(n, src, dst):
        copy = pltpu.make_async_copy(src, dst, osem.at[n])
        copy.start()
        stores.append(copy)

    pad_rows = jnp.zeros((padded - slots, width), BF)
    loads["x"].wait()

    @pl.loop(0, images)
    def _(i):
        rows = aligned(i * padded, padded, 16)
        block = jnp.concatenate([x3[i], pad_rows], axis=0)
        xp[rows] = block
        n, _ = normalized(block.astype(F32))
        first[rows] = (n * g1[...] + b1[...]).astype(BF)
        t_row = jnp.concatenate(
            [tissue[i].astype(F32), jnp.zeros((1, padded - slots), F32)], axis=1
        )
        tb[i] = jnp.broadcast_to(t_row, (128, padded)).T

    store(0, xp, xp_o)
    store(1, first, first_o)
    store(2, tb, tb_o)
    loads["qkv_w"].wait()
    for part in range(3):
        cols = slice(part * width, (part + 1) * width)
        prod = dot(first[...], qkv_w[:, cols], 1, 0)
        if part == 0:
            prod = prod + qkv_b[:, :width]
        if part == 2:
            prod = prod + qkv_b[:, width:]
        qkv[:, cols] = prod.astype(BF)
    store(3, qkv, qkv_o)

    scaled = head_masks(0.125)
    ones = head_masks(1.0)

    @pl.loop(0, images)
    def _(i):
        rows = aligned(i * padded, padded, 16)
        slot = lax.rem(i, 2)
        out = pltpu.make_async_copy(pt.at[slot], pt_o.at[i], psem.at[slot])

        @pl.when(i >= 2)
        def _():
            out.wait()

        t = tb[i]
        valid = jnp.concatenate([t, t[:, : scores_w - 128]], axis=1) > 0
        for pair in range(HEADS // 2):
            cols = [slice(b * width + pair * 128, b * width + pair * 128 + 128) for b in range(3)]
            q, k, v = qkv[rows, cols[0]], qkv[rows, cols[1]], qkv[rows, cols[2]]
            mixed = None
            for h in range(2):
                st = jnp.where(valid, dot(k * scaled[h], q, 1, 1), -1e30)
                e = jnp.exp(st - jnp.max(st, axis=0, keepdims=True))
                probs = (e * (1.0 / jnp.sum(e, axis=0, keepdims=True))).astype(BF)
                pt[slot, pair * 2 + h] = probs
                part = dot(probs, v * ones[h], 0, 0)
                mixed = part if mixed is None else mixed + part
            ho[rows, cols[0]] = (mixed * t).astype(BF)
        out.start()

    store(4, ho, ho_o)
    loads["proj_w"].wait()
    res[...] = dot(ho[...], proj_w[...], 1, 0)

    @pl.loop(0, images)
    def _(i):
        rows = aligned(i * padded, padded, 16)
        total = xp[rows].astype(F32) + res[rows] + proj_b[...]
        res[rows] = total
        n, _ = normalized(total)
        s2[rows] = (n * g2[...] + b2[...]).astype(BF)

    store(5, s2, s2_o)
    store(6, res, res_o)
    loads["cot"].wait()

    @pl.loop(0, images)
    def _(i):
        cotp[aligned(i * padded, padded, 16)] = jnp.concatenate([cot3[i], pad_rows], axis=0)

    store(7, cotp, cotp_o)
    for slot in range(2):
        pltpu.make_async_copy(pt.at[slot], pt_o.at[0], psem.at[slot]).wait()
    for copy in stores:
        copy.wait()


def front(tokens, cot, tissue, vec, qkv_w, proj_w):
    images, slots, width = tokens.shape
    padded = -(-slots // 16) * 16
    rows = images * padded
    vm = pl.BlockSpec(memory_space=pltpu.VMEM)
    hbm = pl.BlockSpec(memory_space=pl.ANY)
    sds = jax.ShapeDtypeStruct
    return pl.pallas_call(
        front_kernel,
        out_shape=[
            sds((rows, width), BF),
            sds((rows, width), BF),
            sds((rows, width), BF),
            sds((rows, 3 * width), BF),
            sds((images, HEADS, padded, padded), BF),
            sds((rows, width), BF),
            sds((rows, width), F32),
            sds((rows, width), BF),
            sds((images, padded, 128), F32),
        ],
        in_specs=[hbm, hbm, vm, vm, vm, hbm, vm, hbm, vm, vm, vm],
        out_specs=[hbm] * 9,
        scratch_shapes=[
            pltpu.VMEM((images, slots, width), BF),
            pltpu.VMEM((images, slots, width), BF),
            pltpu.VMEM((rows, width), BF),
            pltpu.VMEM((rows, width), BF),
            pltpu.VMEM((rows, width), BF),
            pltpu.VMEM((width, 3 * width), BF),
            pltpu.VMEM((rows, 3 * width), BF),
            pltpu.VMEM((2, HEADS, padded, padded), BF),
            pltpu.VMEM((rows, width), BF),
            pltpu.VMEM((width, width), BF),
            pltpu.VMEM((rows, width), F32),
            pltpu.VMEM((rows, width), BF),
            pltpu.VMEM((images, padded, 128), F32),
            pltpu.SemaphoreType.DMA((4,)),
            pltpu.SemaphoreType.DMA((8,)),
            pltpu.SemaphoreType.DMA((2,)),
        ],
        compiler_params=pltpu.CompilerParams(vmem_limit_bytes=56 << 20),
        cost_estimate=pl.CostEstimate(flops=13_000_000_000, bytes_accessed=40_000_000, transcendentals=0),
        name="front",
    )(
        tokens, cot, tissue.reshape(images, 1, slots), vec["norm1_gain"], vec["norm1_shift"], qkv_w,
        vec["qkv_shift"], proj_w, vec["proj_shift"], vec["norm2_gain"], vec["norm2_shift"],
    )


OFFSETS = (0, 1, 4, 6, 7, 8, 9, 10, 12, 16)
TICKS = 4


class Exchange:
    def __init__(self, r):
        self.r = r
        self.dp = lax.axis_index("dp")
        self.core = lax.axis_index("fsdp")
        self.pending = []
        self.now = 0
        self.finals = []

    def side(self, bit):
        return (self.dp // bit) % 2

    def peer(self, bit):
        return (self.dp + bit * (1 - 2 * self.side(bit)), self.core)

    def other_core(self):
        return (self.dp, 1 - self.core)

    def greet(self):
        barrier = pltpu.get_barrier_semaphore()
        peers = [self.other_core()] + [self.peer(bit) for bit in (1, 2, 4, 8)]
        for peer in peers:
            pl.semaphore_signal(barrier, inc=1, device_id=peer, device_id_type=MESH)
        pl.semaphore_wait(barrier, len(peers))

    @staticmethod
    def bit_of(turn, k):
        if k == 3:
            return 8
        idx = (turn + k) % 3
        return 1 + idx + (idx * (idx - 1)) // 2

    def d_regions(self, u):
        start, size, out = 0, 256, []
        for k in range(4):
            bit = self.bit_of(u, k)
            side = self.side(bit)
            size //= 2
            out.append((bit, start + side * size, start + (1 - side) * size, size))
            start = start + side * size
        return out

    def d_copy(self, e, u):
        r = self.r
        sems = dict(send_sem=r.d_send.at[e, u], recv_sem=r.d_recv.at[e, u], device_id_type=MESH)
        if e == 0:
            src = r.d_stage.at[aligned((1 - self.core) * 256, 256, 256)]
            return pltpu.make_async_remote_copy(
                src_ref=src, dst_ref=r.d_core.at[u % 2], device_id=self.other_core(), **sems
            )
        k = e - 1 if e <= 4 else 8 - e
        bit, kept, sent, size = self.d_regions(u)[k]
        if e <= 4:
            src, dst = r.d_work.at[u % 2, aligned(sent, size, 16)], r.d_in[k].at[u]
        else:
            src = dst = r.d_total.at[aligned(u * 256 + kept, size, 16)]
        return pltpu.make_async_remote_copy(
            src_ref=src, dst_ref=dst, device_id=self.peer(bit), **sems
        )

    def d_event(self, e, u):
        r = self.r
        if e >= 1:
            self.d_copy(e - 1, u).wait()
        if e == 1:
            r.d_work[u % 2] = r.d_stage[aligned(self.core * 256, 256, 256)] + r.d_core[u % 2]
        elif 2 <= e <= 5:
            _, kept, _, size = self.d_regions(u)[e - 2]
            summed = r.d_work[u % 2, aligned(kept, size, 16)] + r.d_in[e - 2][u]
            if e < 5:
                r.d_work[u % 2, aligned(kept, size, 16)] = summed
            else:
                r.d_total[aligned(u * 256 + kept, size, 16)] = summed
        if e == 9:
            rows = aligned(u * 256, 256, 256)
            pltpu.make_async_copy(r.d_total.at[rows], r.d_out.at[rows], r.d_done.at[u]).start()
        else:
            self.d_copy(e, u).start()

    def u_blocks(self, u):
        width = self.r.width
        if not isinstance(u, int) or u < 6:
            return u * 256, 2 * width + u * 256
        tail = [4 * width + b * width + g * 256 for g in range(3) for b in range(3)]
        tail = [7 * width, 7 * width + 256, 7 * width + 512] + tail
        return tail[2 * (u - 6)], tail[2 * (u - 6) + 1]

    def u_regions(self, u):
        height = self.r.width // 2
        bits = [self.bit_of(u + 1, k) for k in range(4)]
        sides = [self.side(bit) for bit in bits]
        block, col, row = sides[0], sides[1] * 128, 0
        out = [
            (bits[0], (0, height, block, 0, 256), (0, height, 1 - block, 0, 256)),
            (bits[1], (0, height, block, col, 128), (0, height, block, 128 - col, 128)),
        ]
        for k in (2, 3):
            height //= 2
            kept, sent = row + sides[k] * height, row + (1 - sides[k]) * height
            out.append((bits[k], (kept, height, block, col, 128), (sent, height, block, col, 128)))
            row = kept
        return out

    @staticmethod
    def u_work(region):
        row, rows, block, col, cols = region
        return aligned(row, rows, 32), aligned(block * 256 + col, cols, 128)

    def u_place(self, u, region):
        row, rows, block, col, cols = region
        first, second = self.u_blocks(u)
        return aligned(row, rows, 32), aligned(first + block * (second - first) + col, cols, 128)

    def u_copy(self, e, u):
        r = self.r
        sems = dict(send_sem=r.u_send.at[e, u], recv_sem=r.u_recv.at[e, u], device_id_type=MESH)
        half = r.width // 2
        if e == 0:
            src = r.u_stage.at[u % 3, aligned((1 - self.core) * half, half, half)]
            return pltpu.make_async_remote_copy(
                src_ref=src, dst_ref=r.u_core.at[u % 3], device_id=self.other_core(), **sems
            )
        k = e - 1 if e <= 4 else 8 - e
        bit, kept, sent = self.u_regions(u)[k]
        if e <= 4:
            rows, cols = self.u_work(sent)
            src, dst = r.u_work.at[u % 4, rows, cols], r.u_in[k].at[u % 6]
        else:
            src = dst = r.u_total.at[self.u_place(u, kept)]
        return pltpu.make_async_remote_copy(
            src_ref=src, dst_ref=dst, device_id=self.peer(bit), **sems
        )

    def u_event(self, e, u):
        r = self.r
        half = r.width // 2
        if e >= 1:
            self.u_copy(e - 1, u).wait()
        if e == 1:
            r.u_work[u % 4] = r.u_stage[u % 3, aligned(self.core * half, half, half)] + r.u_core[u % 3]
        elif 2 <= e <= 5:
            _, kept, _ = self.u_regions(u)[e - 2]
            rows, cols = self.u_work(kept)
            summed = r.u_work[u % 4, rows, cols] + r.u_in[e - 2][u % 6]
            if e < 5:
                r.u_work[u % 4, rows, cols] = summed
            else:
                r.u_total[self.u_place(u, kept)] = summed
        if e == 9:
            for copy in self.u_outs(u):
                copy.start()
        else:
            self.u_copy(e, u).start()

    def u_outs(self, u):
        r = self.r
        return [
            pltpu.make_async_copy(
                r.u_total.at[:, aligned(col, 256, 256)],
                r.u_out.at[:, aligned(col, 256, 256)],
                r.u_done.at[n, u],
            )
            for n, col in enumerate(self.u_blocks(u))
        ]

    def v_copy(self, e):
        r = self.r
        peer = self.other_core() if e == 0 else self.peer(1 << (e - 1))
        return pltpu.make_async_remote_copy(
            src_ref=r.v_sum.at[e], dst_ref=r.v_in.at[e], send_sem=r.v_send.at[e],
            recv_sem=r.v_recv.at[e], device_id=peer, device_id_type=MESH,
        )

    def v_event(self, e, u=0):
        r = self.r
        if e >= 1:
            self.v_copy(e - 1).wait()
            r.v_sum[e] = r.v_sum[e - 1] + r.v_in[e - 1]
        if e < 5:
            self.v_copy(e).start()

    def loop_tick(self, c, j):
        for base, event in ((2, self.d_event), (3, self.u_event)):
            for e in range(9, 0, -1):
                back = base + OFFSETS[e] - j
                if back % TICKS == 0 and back // TICKS < 6:
                    d = back // TICKS

                    @pl.when(c >= d)
                    def _(event=event, e=e, d=d):
                        event(e, c - d)

    def after_loop(self, chunks):
        self.now = chunks * TICKS - 1
        for base, event in ((2, self.d_event), (3, self.u_event)):
            for u in range(chunks):
                for e in range(1, 10):
                    due = u * TICKS + base + OFFSETS[e]
                    if due > self.now:
                        self.pending.append((due, e, event, u))

    def begin_tail(self, u):
        self.u_event(0, u)
        for e in range(1, 10):
            self.pending.append((self.now + OFFSETS[e], e, self.u_event, u))

    def begin_vec(self):
        self.v_event(0)
        for e in range(1, 6):
            self.pending.append((self.now + e, e, self.v_event, 0))

    def tick(self):
        self.now += 1
        due = sorted((p for p in self.pending if p[0] <= self.now), key=lambda p: p[0])
        for p in due:
            self.run(p)

    def run(self, p):
        if p not in self.pending:
            return
        _, e, event, u = p
        if event == self.u_event and e == 1:
            for q in list(self.pending):
                if q[2] == self.u_event and (q[3] <= u - 6 or (q[3] <= u - 4 and q[1] <= 5)):
                    self.run(q)
        self.pending.remove(p)
        event(e, u)

    def drain(self):
        while self.pending:
            self.tick()
        for u in range(6):
            rows = aligned(u * 256, 256, 256)
            pltpu.make_async_copy(self.r.d_total.at[rows], self.r.d_out.at[rows], self.r.d_done.at[u]).wait()
        for u in range(12):
            for copy in self.u_outs(u):
                copy.wait()


class Local:
    def __init__(self, r):
        self.r = r
        self.copies = []

    def greet(self):
        pass

    def d_store(self, u):
        r = self.r
        outs = []
        for half in range(2):
            rows = aligned(half * 2 * r.width + u * 256, 256, 256)
            outs.append(
                pltpu.make_async_copy(r.d_stage.at[half * 256 : half * 256 + 256], r.d_out.at[rows], r.d_done.at[half])
            )
        return outs

    def d_event(self, e, u):
        for copy in self.d_store(u):
            copy.start()
        for copy in self.d_store(u):
            copy.wait()

    def u_event(self, e, u):
        r = self.r
        for n, col in enumerate(Exchange.u_blocks(self, u)):
            copy = pltpu.make_async_copy(
                r.u_stage.at[u % 3, :, n * 256 : n * 256 + 256],
                r.u_out.at[:, aligned(col, 256, 256)],
                r.u_done.at[n],
            )
            copy.start()
            copy.wait()

    def loop_tick(self, c, j):
        pass

    def after_loop(self, chunks):
        pass

    def begin_tail(self, u):
        self.u_event(0, u)

    def begin_vec(self):
        pass

    def tick(self):
        pass

    def drain(self):
        pass


class Refs:
    def __init__(self, names, refs):
        self.__dict__.update(zip(names, refs, strict=True))


def back_kernel(names, exchange, *refs):
    r = Refs(names, refs)
    rows_all, width = r.gs.shape
    r.width = width
    images = r.tb_hbm.shape[0]
    padded = rows_all // images
    chunks = r.up_b.shape[1] // 512
    if exchange:
        r.d_in = [r.d_in0, r.d_in1, r.d_in2, r.d_in3]
        r.u_in = [r.u_in0, r.u_in1, r.u_in2, r.u_in3]
    net = Exchange(r) if exchange else Local(r)

    def load(n, src, dst):
        copy = pltpu.make_async_copy(src, dst, r.load_sem.at[n])
        copy.start()
        return copy

    early = [load(0, r.s2_hbm, r.s), load(1, r.cot_hbm, r.cot), load(2, r.res_hbm, r.acc)]
    for b in range(4):
        src = r.up_hbm.at[:, b * width : (b + 1) * width]
        early.append(load(3 + b, src, r.w.at[b * width : (b + 1) * width]))
    early.append(load(7, r.down_hbm, r.w.at[4 * width : 8 * width]))
    late = [load(8, r.ho_hbm, r.h), load(10, r.tb_hbm, r.tb)]
    net.greet()
    r.gs[...] = jnp.zeros_like(r.gs)
    r.vec[...] = jnp.zeros_like(r.vec)
    for copy in early:
        copy.wait()

    def pt_copy(it, slot):
        g, half = it // 2, it % 2
        count = images // 2
        return pltpu.make_async_copy(
            r.pt_hbm.at[half * count : (half + 1) * count, g * 4 : g * 4 + 4],
            r.pt.at[slot],
            r.pt_sem.at[slot],
        )

    pt_copy(0, 0).start()

    @pl.loop(0, chunks)
    def _(c):
        half_cols = []
        block, col = c // 3, (c % 3) * 256
        for half in range(2):
            up_rows = aligned((2 * half + block) * width, width, width)
            down_rows = aligned(4 * width + half * 2 * width + c * 256, 256, 256)
            half_cols.append((up_rows, aligned(col, 256, 256), down_rows))
        for half in range(2):
            up_rows, up_cols, down_rows = half_cols[half]
            at = slice(half * 256, half * 256 + 256)
            bias = r.up_b[:, aligned(half * 2 * width + c * 256, 256, 256)]
            hidden = dot(r.s[...], r.w[up_rows, up_cols], 1, 0) + bias
            g_active = dot(r.cot[...], r.w[down_rows], 1, 1)
            active, slope = gelu_both(hidden)
            r.a[:, at] = active.astype(BF)
            g_hidden = (g_active * slope).astype(BF)
            r.b[:, at] = g_hidden
            sums = jnp.sum(g_hidden.astype(F32), axis=0, keepdims=True)
            r.vec[pl.ds(8 + 2 * half + block, 1), up_cols] = sums
        net.loop_tick(c, 0)
        for n in range(width // 256):
            at = slice(n * 256, n * 256 + 256)
            parts = []
            for half in range(2):
                up_rows, up_cols, down_rows = half_cols[half]
                left = slice(half * 256, half * 256 + 256)
                start = (2 * half + block) * width + n * 256
                parts.append(
                    (
                        dot(r.a[:, left], r.w[down_rows, at], 1, 0),
                        dot(r.b[:, left], r.w[aligned(start, 256, 256), up_cols], 1, 1),
                    )
                )
            r.acc[:, at] += parts[0][0] + parts[1][0]
            r.gs[:, at] += parts[0][1] + parts[1][1]
        net.loop_tick(c, 1)
        r.d_stage[...] = dot(r.a[:, :512], r.cot[...], 0, 0).astype(BF)
        net.d_event(0, c)
        net.loop_tick(c, 2)
        r.u_stage[c % 3] = dot(r.s[...], r.b[:, :512], 0, 0).astype(BF)
        net.u_event(0, c)
        net.loop_tick(c, 3)

    net.after_loop(chunks)
    late2 = []
    for b in range(3):
        src = r.qkv_hbm.at[:, b * width : (b + 1) * width]
        late2.append(load(3 + b, src, r.w.at[b * rows_all : (b + 1) * rows_all]))
    proj_rows = slice(3 * rows_all, 3 * rows_all + width)
    late2.append(load(6, r.proj_hbm, r.w.at[proj_rows]))
    late2.append(load(0, r.first_hbm, r.s))

    def res_copy(i, slot):
        return pltpu.make_async_copy(
            r.res_hbm.at[aligned(i * padded, padded, 16)], r.res.at[slot], r.res_sem.at[slot]
        )

    res_copy(0, 0).start()
    r.b[...] = (r.acc[...] + r.down_b[...]).astype(BF)
    out_copy = pltpu.make_async_copy(r.b, r.out_o, r.load_sem.at[7])
    out_copy.start()
    net.tick()

    def add_vec(n, value):
        r.vec[n : n + 1] += jnp.sum(value, axis=0, keepdims=True)

    @pl.loop(0, images)
    def _(i):
        slot = lax.rem(i, 2)
        res_copy(i, slot).wait()

        @pl.when(i + 1 < images)
        def _():
            res_copy(i + 1, 1 - slot).start()

        rows = aligned(i * padded, padded, 16)
        n, rstd = normalized(r.res[slot])
        grad = r.gs[rows]
        cot = r.cot[rows].astype(F32)
        add_vec(0, cot)
        add_vec(1, grad * n)
        add_vec(2, grad)
        t = grad * r.g2[...]
        centre = t - jnp.mean(t, axis=-1, keepdims=True) - n * jnp.mean(t * n, axis=-1, keepdims=True)
        g_res = cot + rstd * centre
        r.gs[rows] = g_res
        low = g_res.astype(BF)
        r.a[rows] = low
        add_vec(3, low.astype(F32))

    net.tick()
    for copy in late + late2:
        copy.wait()
    qkv_at = [r.cot.at[:width], r.cot.at[width : 2 * width], r.w.at[proj_rows]]
    qkv_src = [r.qkv_w_hbm.at[:, b * width : (b + 1) * width] for b in range(3)]
    qkv_loads = [load(3 + b, qkv_src[b], qkv_at[b]) for b in range(2)]
    for n in range(3):
        at = slice(n * 256, n * 256 + 256)
        p_grad = dot(r.h[...], r.a[:, at], 0, 0).astype(BF)
        r.u_stage[n // 2, :, n % 2 * 256 : n % 2 * 256 + 256] = p_grad
    net.begin_tail(6)
    net.tick()
    out_copy.wait()
    x_copy = load(8, r.x_hbm, r.h)
    for n in range(3):
        proj_at = slice(3 * rows_all + n * 256, 3 * rows_all + n * 256 + 256)
        g_heads = dot(r.a[...], r.w[proj_at], 1, 1)
        for i in range(images):
            rows = slice(i * padded, (i + 1) * padded)
            t = jnp.concatenate([r.tb[i]] * 2, axis=1)
            r.b[rows, n * 256 : n * 256 + 256] = (g_heads[rows] * t).astype(BF)
    qkv_loads.append(load(5, qkv_src[2], qkv_at[2]))
    net.tick()

    scaled = head_masks(0.125)
    ones = head_masks(1.0)
    stage = 1
    filled = 1
    for g in range(3):
        for half in range(2):
            it = 2 * g + half
            slot = it % 2
            pt_copy(it, slot).wait()
            if it < 5:
                pt_copy(it + 1, 1 - slot).start()
            for n in range(images // 2):
                i = half * (images // 2) + n
                for p in range(2):
                    cols = slice((2 * g + p) * 128, (2 * g + p + 1) * 128)
                    at = [slice(b * rows_all + i * padded, b * rows_all + (i + 1) * padded) for b in range(3)]
                    q, k, v = r.w[at[0], cols], r.w[at[1], cols], r.w[at[2], cols]
                    gh = r.b[i * padded : (i + 1) * padded, cols]
                    gq = gk = gv = None
                    for h in range(2):
                        low = r.pt[slot, n, 2 * p + h]
                        probs = low.astype(F32)
                        g_probs = dot(v * ones[h], gh, 1, 1)
                        row_dot = jnp.sum(probs * g_probs, axis=0, keepdims=True)
                        g_scores = (probs * (g_probs - row_dot)).astype(BF)
                        parts = (
                            dot(g_scores, k * scaled[h], 0, 0),
                            dot(g_scores, q * scaled[h], 1, 0),
                            dot(low, gh * ones[h], 1, 0),
                        )
                        gq, gk, gv = parts if gq is None else (gq + parts[0], gk + parts[1], gv + parts[2])
                    r.w[at[0], cols] = gq.astype(BF)
                    r.w[at[1], cols] = gk.astype(BF)
                    r.w[at[2], cols] = gv.astype(BF)
            net.tick()
        cols = slice(g * 256, (g + 1) * 256)
        for b in range(3):
            grads = r.w[b * rows_all : (b + 1) * rows_all, cols]
            r.u_stage[stage, :, filled * 256 : (filled + 1) * 256] = dot(r.s[...], grads, 0, 0).astype(BF)
            if b != 1:
                r.vec[4 + b // 2 : 5 + b // 2, cols] = jnp.sum(grads.astype(F32), axis=0, keepdims=True)
            filled += 1
            if filled == 2:
                net.begin_tail(6 + (3 * g + b + 3) // 2)
                stage, filled = (stage + 1) % 3, 0
        net.tick()

    x_copy.wait()
    for b in range(3):
        qkv_loads[b].wait()
        part = dot(r.w[b * rows_all : (b + 1) * rows_all], qkv_at[b][...], 1, 1)
        if b == 0:
            r.acc[...] = part
        else:
            r.acc[...] += part
        net.tick()

    @pl.loop(0, images)
    def _(i):
        rows = aligned(i * padded, padded, 16)
        n, rstd = normalized(r.h[rows].astype(F32))
        grad = r.acc[rows]
        add_vec(6, grad * n)
        add_vec(7, grad)
        t = grad * r.g1[...]
        centre = t - jnp.mean(t, axis=-1, keepdims=True) - n * jnp.mean(t * n, axis=-1, keepdims=True)
        r.a[rows] = (r.gs[rows] + rstd * centre).astype(BF)

    dx_copy = pltpu.make_async_copy(r.a, r.dx_o, r.load_sem.at[9])
    dx_copy.start()
    if exchange:
        r.v_sum[0] = r.vec[...]
    net.tick()
    net.begin_vec()
    net.drain()
    r.vec_o[...] = r.v_sum[5] if exchange else r.vec[...]
    dx_copy.wait()


def back(exchange, s2, res, cot, up, down, ho, proj_w, qkv, pt, first, qkv_w, x, tb, vec):
    rows, width = s2.shape
    images, padded = tb.shape[:2]
    hidden = up.shape[1]
    vm = pl.BlockSpec(memory_space=pltpu.VMEM)
    hbm = pl.BlockSpec(memory_space=pl.ANY)
    sds = jax.ShapeDtypeStruct
    half = width // 2
    if exchange:
        d_shape, u_shape = (hidden // 2, width), (half, 2 * hidden)
    else:
        d_shape, u_shape = (hidden, width), (width, 2 * hidden)
    ins = dict(
        s2_hbm=s2, res_hbm=res, cot_hbm=cot, up_hbm=up, down_hbm=down, ho_hbm=ho, proj_hbm=proj_w,
        qkv_hbm=qkv, pt_hbm=pt, first_hbm=first, qkv_w_hbm=qkv_w, x_hbm=x, tb_hbm=tb,
        up_b=vec["up_shift"], down_b=vec["down_shift"], g1=vec["norm1_gain"], g2=vec["norm2_gain"],
    )
    outs = dict(
        out_o=sds((rows, width), BF), dx_o=sds((rows, width), BF), d_out=sds(d_shape, BF),
        u_out=sds(u_shape, BF), vec_o=sds((16, width), F32),
    )
    dma = pltpu.SemaphoreType.DMA
    scratch = dict(
        s=pltpu.VMEM((rows, width), BF), cot=pltpu.VMEM((rows, width), BF), a=pltpu.VMEM((rows, width), BF),
        b=pltpu.VMEM((rows, width), BF), h=pltpu.VMEM((rows, width), BF), w=pltpu.VMEM((8 * width, width), BF),
        acc=pltpu.VMEM((rows, width), F32), gs=pltpu.VMEM((rows, width), F32),
        res=pltpu.VMEM((2, padded, width), F32),
        tb=pltpu.VMEM((images, padded, 128), F32), pt=pltpu.VMEM((2, images // 2, 4, padded, padded), BF),
        vec=pltpu.VMEM((16, width), F32), d_stage=pltpu.VMEM((512, width), BF),
        u_stage=pltpu.VMEM((3, width, 512), BF), load_sem=dma((11,)), res_sem=dma((2,)), pt_sem=dma((2,)),
    )
    if exchange:
        scratch.update(
            d_total=pltpu.VMEM(d_shape, BF), u_total=pltpu.VMEM(u_shape, BF),
            d_core=pltpu.VMEM((2, 256, width), BF), u_core=pltpu.VMEM((3, half, 512), BF),
            d_in0=pltpu.VMEM((6, 128, width), BF), d_in1=pltpu.VMEM((6, 64, width), BF),
            d_in2=pltpu.VMEM((6, 32, width), BF), d_in3=pltpu.VMEM((6, 16, width), BF),
            u_in0=pltpu.VMEM((6, half, 256), BF), u_in1=pltpu.VMEM((6, half, 128), BF),
            u_in2=pltpu.VMEM((6, half // 2, 128), BF), u_in3=pltpu.VMEM((6, half // 4, 128), BF),
            d_work=pltpu.VMEM((2, 256, width), BF), u_work=pltpu.VMEM((4, half, 512), BF),
            v_sum=pltpu.VMEM((6, 16, width), F32), v_in=pltpu.VMEM((5, 16, width), F32),
            d_send=dma((9, 6)), d_recv=dma((9, 6)), u_send=dma((9, 12)), u_recv=dma((9, 12)),
            v_send=dma((5,)), v_recv=dma((5,)), d_done=dma((6,)), u_done=dma((2, 12)),
        )
    else:
        scratch.update(d_done=dma((2,)), u_done=dma((2,)))
    small = {"up_b", "down_b", "g1", "g2"}
    params = dict(vmem_limit_bytes=63 << 20)
    if exchange:
        params.update(collective_id=1, has_side_effects=True)
    names = [*ins, *outs, *scratch]
    return pl.pallas_call(
        functools.partial(back_kernel, names, exchange),
        out_shape=list(outs.values()),
        in_specs=[vm if name in small else hbm for name in ins],
        out_specs=[hbm] * 4 + [vm],
        scratch_shapes=list(scratch.values()),
        compiler_params=pltpu.CompilerParams(**params),
        cost_estimate=pl.CostEstimate(flops=60_000_000_000, bytes_accessed=60_000_000, transcendentals=0),
        name="back",
    )(*ins.values())


def on_device(n_dp, n_fsdp, *args):
    names = (
        "tokens", "tissue", "norm1_gain", "norm1_shift", "qkv_matrix", "qkv_shift", "proj_matrix", "proj_shift",
        "norm2_gain", "norm2_shift", "up_matrix", "up_shift", "down_matrix", "down_shift", "cotangent",
    )
    arg = dict(zip(names, args, strict=True))
    images, slots, width = arg["tokens"].shape
    whole = {}
    for name in ("qkv_matrix", "proj_matrix", "up_matrix", "down_matrix"):
        whole[name] = lax.all_gather(arg[name], "fsdp", axis=0, tiled=True)
    vectors = [name for name in names if arg[name].ndim == 1]
    packed = lax.all_gather(jnp.concatenate([arg[name] for name in vectors]), "fsdp", axis=0)
    vec, at = {}, 0
    for name in vectors:
        size = arg[name].shape[0]
        vec[name] = packed[:, at : at + size].reshape(1, -1).astype(F32)
        at += size
    xp, cotp, first, qkv, pt, ho, res, s2, tb = front(
        arg["tokens"], arg["cotangent"], arg["tissue"], vec, whole["qkv_matrix"], whole["proj_matrix"]
    )
    exchange = n_dp == 16 and n_fsdp == 2
    out_p, dx_p, d_sum, u_sum, v_sum = back(
        exchange, s2, res, cotp, whole["up_matrix"], whole["down_matrix"], ho, whole["proj_matrix"], qkv, pt,
        first, whole["qkv_matrix"], xp, tb, vec,
    )
    hidden = arg["up_matrix"].shape[1]
    if not exchange:
        d_sum = lax.psum_scatter(d_sum, "fsdp", scatter_dimension=0, tiled=True)
        u_sum = lax.psum_scatter(u_sum, "fsdp", scatter_dimension=0, tiled=True)
        d_sum, u_sum = lax.psum((d_sum, u_sum), "dp")
        v_sum = lax.psum(v_sum, ("dp", "fsdp"))

    def own(v):
        size = v.shape[0] // n_fsdp
        return lax.dynamic_slice(v, (lax.axis_index("fsdp") * size,), (size,))

    def unpad(rows):
        return rows.reshape(images, -1, width)[:, :slots]

    return (
        unpad(out_p),
        unpad(dx_p),
        own(v_sum[6]),
        own(v_sum[7]),
        u_sum[:, hidden : hidden + 3 * width].astype(F32),
        own(v_sum[4:6].reshape(-1)),
        u_sum[:, hidden + 3 * width :].astype(F32),
        own(v_sum[3]),
        own(v_sum[1]),
        own(v_sum[2]),
        u_sum[:, :hidden].astype(F32),
        own(v_sum[8:12].reshape(-1)),
        d_sum.astype(F32),
        own(v_sum[0]),
    )


def solution(mesh):
    rows = P(("dp", "fsdp"), None, None)
    vec, mat = P("fsdp"), P("fsdp", None)
    weights = (vec, vec, mat, vec, mat, vec, vec, vec, mat, vec, mat, vec)
    return jax.shard_map(
        functools.partial(on_device, mesh.shape["dp"], mesh.shape["fsdp"]),
        mesh=mesh,
        in_specs=(rows, P(("dp", "fsdp"), None)) + weights + (rows,),
        out_specs=(rows, rows) + weights,
        check_vma=False,
    )
```

```python
import functools

import jax
import jax.numpy as jnp
from jax import lax
from jax.experimental import pallas as pl
from jax.experimental.pallas import tpu as pltpu
from jax.sharding import PartitionSpec as P

HEADS = 12
EPS = 1e-06
BF = jnp.bfloat16
F32 = jnp.float32
MESH = pl.DeviceIdType.MESH
ERF = (0.254829592, -0.284496736, 1.421413741, -1.453152027, 1.061405429)


def dot(a, b, ca, cb):
    return lax.dot_general(a, b, (((ca,), (cb,)), ((), ())), preferred_element_type=F32)


def aligned(start, size, step):
    if isinstance(start, int):
        return pl.ds(start, size)
    return pl.ds(pl.multiple_of(start, step), size)


def gelu_both(h):
    t = 1.0 / (1.0 + (0.3275911 * 0.7071067811865476) * jnp.abs(h))
    e = jnp.exp(-0.5 * h * h)
    tail = t * (ERF[0] + t * (ERF[1] + t * (ERF[2] + t * (ERF[3] + t * ERF[4])))) * (0.5 * e)
    cdf = jnp.where(h >= 0, 1.0 - tail, tail)
    return h * cdf, cdf + h * e * 0.3989422804014327


def normalized(v):
    mean = jnp.mean(v, axis=-1, keepdims=True)
    centred = v - mean
    var = jnp.mean(centred * centred, axis=-1, keepdims=True)
    rstd = lax.rsqrt(var + EPS)
    return centred * rstd, rstd


VECTORS = (
    "norm1_gain", "norm1_shift", "qkv_shift", "proj_shift", "norm2_gain", "norm2_shift", "up_shift", "down_shift",
)


def unpack(vecs, width, hidden):
    cores = vecs.shape[0]
    sizes = dict(qkv_shift=2 * width, up_shift=hidden)
    out, at = {}, 0
    for name in VECTORS:
        size = sizes.get(name, width) // cores
        out[name] = jnp.concatenate([vecs[core, 0:1, at : at + size] for core in range(cores)], axis=1)
        at += size
    return out


def head_masks(scale):
    lane = lax.broadcasted_iota(jnp.int32, (1, 128), 1)
    return [
        jnp.where(lane < 64, scale, 0.0).astype(BF),
        jnp.where(lane >= 64, scale, 0.0).astype(BF),
    ]


def front_kernel(
    remote, x_hbm, cot_hbm, tissue, packed, qkv_s, proj_s, up_s, down_s,
    n1_o, r1_o, cotp_o, first_o, qkv_o, pt_o, ho_o, res_o, s2_o, n2_o, r2_o, tb_o, qkv_wo, proj_wo, up_wo, down_wo,
    vecs_o, x3, cot3, xp, cotp, first, qkv_w, qkv, pt, ho, proj_w, res, s2, tb, n1, r1, n2, r2, vecs, g1, b1, qkv_b,
    proj_b, g2, b2, sem, osem, psem, send_sem, recv_sem, *ff_w,
):
    images, slots, width = x3.shape
    padded = xp.shape[0] // images
    scores_w = pt.shape[-1]
    hidden = up_s.shape[1]

    loads = {
        "x": pltpu.make_async_copy(x_hbm, x3, sem.at[0]),
        "cot": pltpu.make_async_copy(cot_hbm, cot3, sem.at[3]),
    }
    loads["x"].start()
    sends = {}
    if remote:
        up, down = ff_w
        dp, core = lax.axis_index("dp"), lax.axis_index("fsdp")
        barrier = pltpu.get_barrier_semaphore()
        pl.semaphore_signal(barrier, inc=1, device_id=(dp, 1 - core), device_id_type=MESH)
        pl.semaphore_wait(barrier, 1)
        parts = (("vecs", packed, vecs), ("qkv_w", qkv_s, qkv_w), ("proj_w", proj_s, proj_w), ("up", up_s, up), ("down", down_s, down))
        for n, (name, src, dst) in enumerate(parts):
            if name == "vecs":
                here = dst.at[core]
            else:
                share = src.shape[0]
                here = dst.at[aligned(core * share, share, share)]
            sends[name] = pltpu.make_async_remote_copy(
                src_ref=src, dst_ref=here, send_sem=send_sem.at[n], recv_sem=recv_sem.at[n],
                device_id=(dp, 1 - core), device_id_type=MESH,
            )
            sends[name].start()
            loads[name] = pltpu.make_async_copy(src, here, sem.at[4 + n])
            loads[name].start()
    else:
        loads["vecs"] = pltpu.make_async_copy(packed, vecs, sem.at[4])
        loads["qkv_w"] = pltpu.make_async_copy(qkv_s, qkv_w, sem.at[1])
        loads["proj_w"] = pltpu.make_async_copy(proj_s, proj_w, sem.at[2])
        for name in ("vecs", "qkv_w", "proj_w"):
            loads[name].start()
    loads["cot"].start()

    def arrive(name):
        loads[name].wait()
        if remote:
            sends[name].wait()

    arrive("vecs")
    vec = unpack(vecs, width, hidden)
    for ref, name in (
        (g1, "norm1_gain"), (b1, "norm1_shift"), (qkv_b, "qkv_shift"), (proj_b, "proj_shift"), (g2, "norm2_gain"), (b2, "norm2_shift"),
    ):
        ref[...] = vec[name]
    stores = []

    def store(n, src, dst):
        copy = pltpu.make_async_copy(src, dst, osem.at[n])
        copy.start()
        stores.append(copy)

    pad_rows = jnp.zeros((padded - slots, width), BF)
    loads["x"].wait()

    @pl.loop(0, images)
    def _(i):
        rows = aligned(i * padded, padded, 16)
        block = jnp.concatenate([x3[i], pad_rows], axis=0)
        xp[rows] = block
        n, rstd = normalized(block.astype(F32))
        n1[rows] = n.astype(BF)
        r1[i] = jnp.broadcast_to(rstd, (padded, 128))
        first[rows] = (n * g1[...] + b1[...]).astype(BF)
        t_row = jnp.concatenate(
            [tissue[pl.ds(i, 1)].astype(F32), jnp.zeros((1, padded - slots), F32)], axis=1
        )
        tb[i] = jnp.broadcast_to(t_row, (128, padded)).T

    store(0, n1, n1_o)
    store(8, r1, r1_o)
    store(1, first, first_o)
    store(2, tb, tb_o)
    arrive("qkv_w")
    if remote:
        store(11, qkv_w, qkv_wo)
        store(12, vecs, vecs_o)
    for part in range(3):
        cols = slice(part * width, (part + 1) * width)
        prod = dot(first[...], qkv_w[:, cols], 1, 0)
        if part == 0:
            prod = prod + qkv_b[:, :width]
        if part == 2:
            prod = prod + qkv_b[:, width:]
        qkv[:, cols] = prod.astype(BF)
    store(3, qkv, qkv_o)

    scaled = head_masks(0.125)
    ones = head_masks(1.0)

    @pl.loop(0, images)
    def _(i):
        rows = aligned(i * padded, padded, 16)
        slot = lax.rem(i, 2)
        out = pltpu.make_async_copy(pt.at[slot], pt_o.at[i], psem.at[slot])

        @pl.when(i >= 2)
        def _():
            out.wait()

        t = tb[i]
        valid = jnp.concatenate([t, t[:, : scores_w - 128]], axis=1) > 0
        for pair in range(HEADS // 2):
            cols = [slice(b * width + pair * 128, b * width + pair * 128 + 128) for b in range(3)]
            q, k, v = qkv[rows, cols[0]], qkv[rows, cols[1]], qkv[rows, cols[2]]
            mixed = None
            for h in range(2):
                st = jnp.where(valid, dot(k * scaled[h], q, 1, 1), -1e30)
                e = jnp.exp(st - jnp.max(st, axis=0, keepdims=True))
                probs = (e * (1.0 / jnp.sum(e, axis=0, keepdims=True))).astype(BF)
                pt[slot, pair * 2 + h] = probs
                part = dot(probs, v * ones[h], 0, 0)
                mixed = part if mixed is None else mixed + part
            ho[rows, cols[0]] = (mixed * t).astype(BF)
        out.start()

    store(4, ho, ho_o)
    arrive("proj_w")
    if remote:
        store(13, proj_w, proj_wo)
    res[...] = dot(ho[...], proj_w[...], 1, 0)

    @pl.loop(0, images)
    def _(i):
        rows = aligned(i * padded, padded, 16)
        total = xp[rows].astype(F32) + res[rows] + proj_b[...]
        res[rows] = total
        n, rstd = normalized(total)
        n2[rows] = n.astype(BF)
        r2[i] = jnp.broadcast_to(rstd, (padded, 128))
        s2[rows] = (n * g2[...] + b2[...]).astype(BF)

    if remote:
        arrive("up")
        store(14, up, up_wo)
        arrive("down")
        store(15, down, down_wo)
    store(5, s2, s2_o)
    store(6, res, res_o)
    store(9, n2, n2_o)
    store(10, r2, r2_o)
    loads["cot"].wait()

    @pl.loop(0, images)
    def _(i):
        cotp[aligned(i * padded, padded, 16)] = jnp.concatenate([cot3[i], pad_rows], axis=0)

    store(7, cotp, cotp_o)
    for slot in range(2):
        pltpu.make_async_copy(pt.at[slot], pt_o.at[0], psem.at[slot]).wait()
    for copy in stores:
        copy.wait()


def front(remote, tokens, cot, tissue, packed, qkv_w, proj_w, up, down):
    images, slots, width = tokens.shape
    padded = -(-slots // 16) * 16
    rows = images * padded
    cores = 2 if remote else packed.shape[0]
    hidden = up.shape[1]
    vm = pl.BlockSpec(memory_space=pltpu.VMEM)
    hbm = pl.BlockSpec(memory_space=pl.ANY)
    sds = jax.ShapeDtypeStruct
    flat, col = sds((rows, width), BF), sds((images, padded, 128), F32)
    vecs_shape = (cores, 8, packed.shape[-1])
    outs = [
        flat, col, flat, flat, sds((rows, 3 * width), BF), sds((images, HEADS, padded, padded), BF), flat,
        sds((rows, width), F32), flat, flat, col, col, sds((width, 3 * width), BF), sds((width, width), BF),
        sds((width, hidden), BF), sds((hidden, width), BF), sds(vecs_shape, F32),
    ]
    flat_v, col_v = pltpu.VMEM((rows, width), BF), pltpu.VMEM((images, padded, 128), F32)
    row_v = pltpu.VMEM((1, width), F32)
    dma = pltpu.SemaphoreType.DMA
    params = dict(collective_id=2, has_side_effects=True) if remote else {}
    got = pl.pallas_call(
        functools.partial(front_kernel, remote),
        out_shape=outs,
        in_specs=[hbm, hbm, vm, vm if remote else hbm, hbm, hbm, hbm, hbm],
        out_specs=[hbm] * len(outs),
        scratch_shapes=[
            pltpu.VMEM((images, slots, width), BF), pltpu.VMEM((images, slots, width), BF), flat_v, flat_v, flat_v,
            pltpu.VMEM((width, 3 * width), BF), pltpu.VMEM((rows, 3 * width), BF),
            pltpu.VMEM((2, HEADS, padded, padded), BF), flat_v, pltpu.VMEM((width, width), BF),
            pltpu.VMEM((rows, width), F32), flat_v, col_v, flat_v, col_v, flat_v, col_v, pltpu.VMEM(vecs_shape, F32),
            row_v, row_v, pltpu.VMEM((1, 2 * width), F32), row_v, row_v, row_v, dma((9,)), dma((16,)), dma((2,)),
            dma((5,)), dma((5,)),
        ] + ([pltpu.VMEM((width, hidden), BF), pltpu.VMEM((hidden, width), BF)] if remote else []),
        compiler_params=pltpu.CompilerParams(vmem_limit_bytes=62 << 20, **params),
        cost_estimate=pl.CostEstimate(flops=13_000_000_000, bytes_accessed=40_000_000, transcendentals=0),
        name="front",
    )(tokens, cot, tissue, packed, qkv_w, proj_w, up, down)
    if not remote:
        got = [*got[:12], qkv_w, proj_w, up, down, packed]
    return got


D_TICKS = (
    (1, 2, 4, 6, 7, 8, 9, 10, 13, 15),
    (3, 4, 6, 8, 9, 10, 11, 13, 16, 19),
    (5, 6, 8, 10, 12, 14, 16, 18, 20, 23),
    (7, 8, 10, 13, 15, 17, 20, 22, 24, 27),
    (9, 10, 14, 17, 19, 21, 23, 24, 27, 35),
    (11, 12, 15, 17, 19, 21, 23, 25, 27, 36),
)
U_TICKS = (
    (1, 2, 4, 6, 7, 8, 10, 12, 14, 20),
    (3, 4, 6, 8, 10, 11, 13, 15, 16, 19),
    (5, 6, 8, 10, 11, 13, 15, 16, 20, 23),
    (7, 8, 10, 12, 14, 16, 19, 20, 22, 25),
    (9, 10, 13, 15, 17, 20, 22, 24, 26, 32),
    (11, 12, 15, 19, 20, 22, 24, 26, 28, 44),
    (15, 16, 21, 23, 25, 27, 30, 39, 52, 63),
    (19, 20, 23, 25, 27, 30, 40, 47, 54, 61),
    (19, 20, 23, 26, 28, 31, 42, 49, 59, 67),
    (22, 23, 27, 33, 43, 51, 57, 62, 66, 71),
    (25, 26, 34, 46, 53, 58, 65, 68, 70, 73),
    (25, 26, 29, 38, 48, 55, 60, 64, 69, 72),
)
V_TICKS = (30, 31, 34, 37, 40, 43)
WORK = 7


class Exchange:
    def __init__(self, r):
        self.r = r
        self.dp = lax.axis_index("dp")
        self.core = lax.axis_index("fsdp")
        self.due = self.plan()
        self.now = 0
        self.sides = {bit: (self.dp // bit) % 2 for bit in (1, 2, 4, 8)}
        self.peers = {bit: self.dp + bit * (1 - 2 * self.sides[bit]) for bit in (1, 2, 4, 8)}

    def other_core(self):
        return (self.dp, 1 - self.core)

    def greet(self):
        barrier = pltpu.get_barrier_semaphore()
        peers = [self.other_core()] + [(self.peers[bit], self.core) for bit in (1, 2, 4, 8)]
        for peer in peers:
            pl.semaphore_signal(barrier, inc=1, device_id=peer, device_id_type=MESH)
        pl.semaphore_wait(barrier, len(peers))

    def at_stage(self, turn, k):
        if k == 3:
            return self.sides[8], self.peers[8]
        bit = (1, 2, 4)[(turn + k) % 3]
        return self.sides[bit], self.peers[bit]

    def d_regions(self, u):
        start, size, out = 0, 256, []
        for k in range(4):
            side, peer = self.at_stage(u, k)
            size //= 2
            out.append((peer, start + side * size, start + (1 - side) * size, size))
            start = start + side * size
        return out

    def d_copy(self, e, u):
        r = self.r
        sems = dict(send_sem=r.d_send.at[e, u], recv_sem=r.d_recv.at[e, u], device_id_type=MESH)
        if e == 0:
            src = r.d_stage.at[u % 2, aligned((1 - self.core) * 256, 256, 256)]
            return pltpu.make_async_remote_copy(
                src_ref=src, dst_ref=r.d_core.at[u % 2], device_id=self.other_core(), **sems
            )
        k = e - 1 if e <= 4 else 8 - e
        peer, kept, sent, size = self.d_regions(u)[k]
        if e <= 4:
            src, dst = r.d_work.at[u, aligned(sent, size, 16)], r.d_in[k].at[u]
        else:
            src = dst = r.d_out.at[aligned(u * 256 + kept, size, 16)]
            if e == 5:
                src = r.d_work.at[u, aligned(kept, size, 16)]
        return pltpu.make_async_remote_copy(
            src_ref=src, dst_ref=dst, device_id=(peer, self.core), **sems
        )

    def d_event(self, e, u):
        r = self.r
        if e >= 1:
            self.d_copy(e - 1, u).wait()
        if e == 1:
            r.d_work[u] = r.d_stage[u % 2, aligned(self.core * 256, 256, 256)] + r.d_core[u % 2]
        elif 2 <= e <= 5:
            _, kept, _, size = self.d_regions(u)[e - 2]
            r.d_work[u, aligned(kept, size, 16)] += r.d_in[e - 2][u]
        if e == 5:
            self.d_own(u).start()
        if e == 6:
            self.d_own(u).wait()
        if e < 9:
            self.d_copy(e, u).start()

    def d_own(self, u):
        _, kept, _, size = self.d_regions(u)[3]
        return pltpu.make_async_copy(
            self.r.d_work.at[u, aligned(kept, size, 16)],
            self.r.d_out.at[aligned(u * 256 + kept, size, 16)],
            self.r.d_done.at[u],
        )

    def u_blocks(self, u):
        width = self.r.width
        if u < 6:
            return u * 256, 2 * width + u * 256
        tail = [4 * width + b * width + g * 256 for g in range(3) for b in range(3)]
        tail = [7 * width, 7 * width + 256, 7 * width + 512] + tail
        return tail[2 * (u - 6)], tail[2 * (u - 6) + 1]

    def u_regions(self, u):
        height = self.r.width // 2
        sides, peers = zip(*(self.at_stage(u + 2, k) for k in range(4)))
        block, col, row = sides[0], sides[1] * 128, 0
        out = [
            (peers[0], (0, height, block, 0, 256), (0, height, 1 - block, 0, 256)),
            (peers[1], (0, height, block, col, 128), (0, height, block, 128 - col, 128)),
        ]
        for k in (2, 3):
            height //= 2
            kept, sent = row + sides[k] * height, row + (1 - sides[k]) * height
            out.append((peers[k], (kept, height, block, col, 128), (sent, height, block, col, 128)))
            row = kept
        return out

    @staticmethod
    def u_work(region):
        row, rows, block, col, cols = region
        return aligned(row, rows, 32), aligned(block * 256 + col, cols, 128)

    def u_place(self, u, region):
        row, rows, block, col, cols = region
        first, second = self.u_blocks(u)
        return aligned(row, rows, 32), aligned(first + block * (second - first) + col, cols, 128)

    def u_copy(self, e, u):
        r = self.r
        sems = dict(send_sem=r.u_send.at[e, u], recv_sem=r.u_recv.at[e, u], device_id_type=MESH)
        half = r.width // 2
        if e == 0:
            src = r.u_stage.at[u % 2, aligned((1 - self.core) * half, half, half)]
            return pltpu.make_async_remote_copy(
                src_ref=src, dst_ref=r.u_core.at[u % 3], device_id=self.other_core(), **sems
            )
        k = e - 1 if e <= 4 else 8 - e
        peer, kept, sent = self.u_regions(u)[k]
        if e <= 4:
            rows, cols = self.u_work(sent)
            src, dst = r.u_work.at[u % WORK, rows, cols], r.u_in[k].at[u]
        else:
            src = dst = r.u_out.at[self.u_place(u, kept)]
            if e == 5:
                rows, cols = self.u_work(kept)
                src = r.u_work.at[u % WORK, rows, cols]
        return pltpu.make_async_remote_copy(
            src_ref=src, dst_ref=dst, device_id=(peer, self.core), **sems
        )

    def u_event(self, e, u):
        r = self.r
        half = r.width // 2
        if e >= 1:
            self.u_copy(e - 1, u).wait()
        if e == 1:
            r.u_work[u % WORK] = r.u_stage[u % 2, aligned(self.core * half, half, half)] + r.u_core[u % 3]
        elif 2 <= e <= 5:
            rows, cols = self.u_work(self.u_regions(u)[e - 2][1])
            r.u_work[u % WORK, rows, cols] += r.u_in[e - 2][u]
        if e == 5:
            self.u_own(u).start()
        if e == 6:
            self.u_own(u).wait()
        if e < 9:
            self.u_copy(e, u).start()

    def u_own(self, u):
        kept = self.u_regions(u)[3][1]
        rows, cols = self.u_work(kept)
        return pltpu.make_async_copy(
            self.r.u_work.at[u % WORK, rows, cols], self.r.u_out.at[self.u_place(u, kept)], self.r.u_done.at[u]
        )

    def v_copy(self, e):
        r = self.r
        peer = self.other_core() if e == 0 else (self.peers[1 << (e - 1)], self.core)
        return pltpu.make_async_remote_copy(
            src_ref=r.v_sum.at[e], dst_ref=r.v_in.at[e], send_sem=r.v_send.at[e],
            recv_sem=r.v_recv.at[e], device_id=peer, device_id_type=MESH,
        )

    def v_event(self, e, u=0):
        r = self.r
        if e >= 1:
            self.v_copy(e - 1).wait()
            r.v_sum[e] = r.v_sum[e - 1] + r.v_in[e - 1]
        if e < 5:
            self.v_copy(e).start()

    def plan(self):
        due = {}
        for event, table in ((self.d_event, D_TICKS), (self.u_event, U_TICKS), (self.v_event, (V_TICKS,))):
            for u, ticks in enumerate(table):
                for e, tick in enumerate(ticks):
                    due.setdefault(tick, []).append((-e, u, event))
        return due

    def run(self, tick):
        for e, u, event in sorted(self.due.pop(tick, []), key=lambda item: item[:2]):
            event(-e, u)

    def loop_tick(self, c, chunks, j):
        for k in range(chunks):
            if self.due.get(2 * k + j):

                @pl.when(c == k)
                def _(k=k):
                    self.run(2 * k + j)

        self.now = 2 * chunks - 1

    def tick(self):
        self.now += 1
        self.run(self.now)

    def tail(self, u):
        pass

    def drain(self):
        while self.due:
            self.tick()


class Local:
    def __init__(self, r):
        self.r = r
        self.copies = []

    def greet(self):
        pass

    def d_store(self, u):
        r = self.r
        outs = []
        for half in range(2):
            rows = aligned(half * 2 * r.width + u * 256, 256, 256)
            outs.append(
                pltpu.make_async_copy(r.d_stage.at[lax.rem(u, 2), half * 256 : half * 256 + 256], r.d_out.at[rows], r.d_done.at[half])
            )
        return outs

    def d_event(self, e, u):
        for copy in self.d_store(u):
            copy.start()
        for copy in self.d_store(u):
            copy.wait()

    def blocks(self, u):
        if isinstance(u, int):
            return Exchange.u_blocks(self, u)
        return u * 256, 2 * self.r.width + u * 256

    def u_event(self, e, u):
        r = self.r
        for n, col in enumerate(self.blocks(u)):
            copy = pltpu.make_async_copy(
                r.u_stage.at[lax.rem(u, 2), :, n * 256 : n * 256 + 256],
                r.u_out.at[:, aligned(col, 256, 256)],
                r.u_done.at[n],
            )
            copy.start()
            copy.wait()

    def loop_tick(self, c, chunks, j):
        if j == 1:
            self.d_event(0, c)
            self.u_event(0, c)

    def tick(self):
        pass

    def tail(self, u):
        self.u_event(0, u)

    def drain(self):
        pass


class Refs:
    def __init__(self, names, refs):
        self.__dict__.update(zip(names, refs, strict=True))


def back_kernel(names, exchange, *refs):
    r = Refs(names, refs)
    rows_all, width = r.gs.shape
    r.width = width
    images = r.tb_hbm.shape[0]
    padded = rows_all // images
    chunks = r.up_b.shape[1] // 512
    if exchange:
        r.d_in = [r.d_in0, r.d_in1, r.d_in2, r.d_in3]
        r.u_in = [r.u_in0, r.u_in1, r.u_in2, r.u_in3]
    net = Exchange(r) if exchange else Local(r)

    def load(n, src, dst):
        copy = pltpu.make_async_copy(src, dst, r.load_sem.at[n])
        copy.start()
        return copy

    early = [load(0, r.s2_hbm, r.s), load(1, r.cot_hbm, r.cot), load(2, r.res_hbm, r.acc)]
    for b in range(4):
        src = r.up_hbm.at[:, b * width : (b + 1) * width]
        early.append(load(3 + b, src, r.w.at[b * width : (b + 1) * width]))
    early.append(load(7, r.down_hbm, r.w.at[4 * width : 8 * width]))
    late = [load(8, r.ho_hbm, r.h), load(10, r.tb_hbm, r.tb), load(9, r.r2_hbm, r.r2)]
    net.greet()
    vec = unpack(r.vecs, width, r.up_b.shape[1])
    for ref, name in ((r.up_b, "up_shift"), (r.down_b, "down_shift"), (r.g1, "norm1_gain"), (r.g2, "norm2_gain")):
        ref[...] = vec[name]
    r.gs[...] = jnp.zeros_like(r.gs)
    r.vec[...] = jnp.zeros_like(r.vec)
    for copy in early:
        copy.wait()

    def pt_copy(it, slot):
        g, half = it // 2, it % 2
        count = images // 2
        return pltpu.make_async_copy(
            r.pt_hbm.at[half * count : (half + 1) * count, g * 4 : g * 4 + 4],
            r.pt.at[slot],
            r.pt_sem.at[slot],
        )

    pt_copy(0, 0).start()

    def part_of(c, half):
        upper = jnp.where(c >= 3, 1, 0)
        block = (2 * half + upper) * width
        cols = aligned((c - 3 * upper) * 256, 256, 256)
        down = aligned(4 * width + half * 2 * width + c * 256, 256, 256)
        return block, cols, down, 8 + 2 * half + upper

    def ff_in(c, half):
        block, cols, down, row = part_of(c, half)
        at = slice(half * 256, half * 256 + 256)
        bias = r.up_b[:, aligned(half * 2 * width + c * 256, 256, 256)]
        hidden = dot(r.s[...], r.w[aligned(block, width, width), cols], 1, 0) + bias
        g_active = dot(r.cot[...], r.w[down], 1, 1)
        active, slope = gelu_both(hidden)
        r.a[:, at] = active.astype(BF)
        g_hidden = (g_active * slope).astype(BF)
        r.b[:, at] = g_hidden
        r.vec[pl.ds(row, 1), cols] = jnp.sum(g_hidden.astype(F32), axis=0, keepdims=True)

    def ff_out(c):
        (block0, cols, down0, _), (block1, _, down1, _) = part_of(c, 0), part_of(c, 1)
        for n in range(width // 256):
            to = slice(n * 256, n * 256 + 256)
            up0, up1 = aligned(block0 + n * 256, 256, 256), aligned(block1 + n * 256, 256, 256)
            r.acc[:, to] += dot(r.a[:, :256], r.w[down0, to], 1, 0) + dot(r.a[:, 256:512], r.w[down1, to], 1, 0)
            r.gs[:, to] += dot(r.b[:, :256], r.w[up0, cols], 1, 1) + dot(r.b[:, 256:512], r.w[up1, cols], 1, 1)

    @pl.loop(0, chunks)
    def _(c):
        ff_in(c, 0)
        ff_in(c, 1)
        ff_out(c)
        net.loop_tick(c, chunks, 0)
        r.d_stage[lax.rem(c, 2)] = dot(r.a[:, :512], r.cot[...], 0, 0).astype(BF)
        r.u_stage[lax.rem(c, 2)] = dot(r.s[...], r.b[:, :512], 0, 0).astype(BF)
        net.loop_tick(c, chunks, 1)

    late2 = []
    for b in range(3):
        src = r.qkv_hbm.at[:, b * width : (b + 1) * width]
        late2.append(load(3 + b, src, r.w.at[b * rows_all : (b + 1) * rows_all]))
    proj_rows = slice(3 * rows_all, 3 * rows_all + width)
    late2.append(load(6, r.proj_hbm, r.w.at[proj_rows]))
    late2.append(load(0, r.first_hbm, r.s))

    def norm_copy(i, slot):
        return pltpu.make_async_copy(
            r.n2_hbm.at[aligned(i * padded, padded, 16)], r.n2.at[slot], r.n2_sem.at[slot]
        )

    norm_copy(0, 0).start()
    r.b[...] = (r.acc[...] + r.down_b[...]).astype(BF)
    out_copy = pltpu.make_async_copy(r.b, r.out_o, r.load_sem.at[7])
    out_copy.start()
    net.tick()

    def folded(v):
        return v[:8] + v[8:]

    def norm_back(grad, n, rstd, gain):
        t = grad * gain
        centre = t - jnp.mean(t, axis=-1, keepdims=True) - n * jnp.mean(t * n, axis=-1, keepdims=True)
        return jnp.concatenate([rstd] * (width // 128), axis=1) * centre

    def add_vec(first_row, sums):
        for n, value in enumerate(sums):
            r.vec[first_row + n : first_row + n + 1] += jnp.sum(value, axis=0, keepdims=True)

    for copy in late:
        copy.wait()
    for part in range(2):

        @pl.loop(part * images // 2, (part + 1) * images // 2)
        def _(i):
            slot = lax.rem(i, 2)
            norm_copy(i, slot).wait()

            @pl.when(i + 1 < images)
            def _():
                norm_copy(i + 1, 1 - slot).start()

            sums = [0.0] * 4
            for tile in range(padded // 16):
                rows = aligned(i * padded + tile * 16, 16, 16)
                at = slice(tile * 16, tile * 16 + 16)
                n = r.n2[slot, at].astype(F32)
                grad = r.gs[rows]
                cot = r.cot[rows].astype(F32)
                g_res = cot + norm_back(grad, n, r.r2[i, at], r.g2[...])
                r.gs[rows] = g_res
                low = g_res.astype(BF)
                r.a[rows] = low
                terms = (cot, grad * n, grad, low.astype(F32))
                sums = [total + folded(term) for total, term in zip(sums, terms)]
            add_vec(0, sums)

        net.tick()
    for copy in late2:
        copy.wait()
    qkv_at = [r.cot.at[:width], r.cot.at[width : 2 * width], r.w.at[proj_rows]]
    qkv_src = [r.qkv_w_hbm.at[:, b * width : (b + 1) * width] for b in range(3)]
    qkv_loads = [load(3 + b, qkv_src[b], qkv_at[b]) for b in range(2)]
    for n in range(3):
        at = slice(n * 256, n * 256 + 256)
        p_grad = dot(r.h[...], r.a[:, at], 0, 0).astype(BF)
        r.u_stage[n // 2, :, n % 2 * 256 : n % 2 * 256 + 256] = p_grad
    net.tail(6)
    net.tick()
    out_copy.wait()
    n1_copy = load(8, r.n1_hbm, r.h)
    for n in range(3):
        proj_at = slice(3 * rows_all + n * 256, 3 * rows_all + n * 256 + 256)
        g_heads = dot(r.a[...], r.w[proj_at], 1, 1)
        for i in range(images):
            rows = slice(i * padded, (i + 1) * padded)
            t = jnp.concatenate([r.tb[i]] * 2, axis=1)
            r.b[rows, n * 256 : n * 256 + 256] = (g_heads[rows] * t).astype(BF)
    qkv_loads.append(load(5, qkv_src[2], qkv_at[2]))
    net.tick()

    scaled = head_masks(0.125)
    ones = head_masks(1.0)
    stage = 1
    filled = 1
    for g in range(3):
        for half in range(2):
            it = 2 * g + half
            slot = it % 2
            pt_copy(it, slot).wait()
            if it < 5:
                pt_copy(it + 1, 1 - slot).start()
            for n in range(images // 2):
                i = half * (images // 2) + n
                for p in range(2):
                    cols = slice((2 * g + p) * 128, (2 * g + p + 1) * 128)
                    at = [slice(b * rows_all + i * padded, b * rows_all + (i + 1) * padded) for b in range(3)]
                    q, k, v = r.w[at[0], cols], r.w[at[1], cols], r.w[at[2], cols]
                    gh = r.b[i * padded : (i + 1) * padded, cols]
                    gq = gk = gv = None
                    for h in range(2):
                        low = r.pt[slot, n, 2 * p + h]
                        probs = low.astype(F32)
                        g_probs = dot(v * ones[h], gh, 1, 1)
                        row_dot = jnp.sum(probs * g_probs, axis=0, keepdims=True)
                        g_scores = (probs * (g_probs - row_dot)).astype(BF)
                        parts = (
                            dot(g_scores, k * scaled[h], 0, 0),
                            dot(g_scores, q * scaled[h], 1, 0),
                            dot(low, gh * ones[h], 1, 0),
                        )
                        gq, gk, gv = parts if gq is None else (gq + parts[0], gk + parts[1], gv + parts[2])
                    r.w[at[0], cols] = gq.astype(BF)
                    r.w[at[1], cols] = gk.astype(BF)
                    r.w[at[2], cols] = gv.astype(BF)
            net.tick()
        cols = slice(g * 256, (g + 1) * 256)
        for b in range(3):
            grads = r.w[b * rows_all : (b + 1) * rows_all, cols]
            r.u_stage[stage, :, filled * 256 : (filled + 1) * 256] = dot(r.s[...], grads, 0, 0).astype(BF)
            if b != 1:
                r.vec[4 + b // 2 : 5 + b // 2, cols] = jnp.sum(grads.astype(F32), axis=0, keepdims=True)
            filled += 1
            if filled == 2:
                net.tail(6 + (3 * g + b + 3) // 2)
                stage, filled = 1 - stage, 0
        net.tick()

    n1_copy.wait()
    r1_copy = load(10, r.r1_hbm, r.tb)
    for b in range(3):
        qkv_loads[b].wait()
        part = dot(r.w[b * rows_all : (b + 1) * rows_all], qkv_at[b][...], 1, 1)
        if b == 0:
            r.acc[...] = part
        else:
            r.acc[...] += part
        net.tick()

    r1_copy.wait()
    for part in range(2):

        @pl.loop(part * images // 2, (part + 1) * images // 2)
        def _(i):
            sums = [0.0] * 2
            for tile in range(padded // 16):
                rows = aligned(i * padded + tile * 16, 16, 16)
                at = slice(tile * 16, tile * 16 + 16)
                n = r.h[rows].astype(F32)
                grad = r.acc[rows]
                r.a[rows] = (r.gs[rows] + norm_back(grad, n, r.tb[i, at], r.g1[...])).astype(BF)
                sums = [total + folded(term) for total, term in zip(sums, (grad * n, grad))]
            add_vec(6, sums)

        if part == 0:
            net.tick()

    dx_copy = pltpu.make_async_copy(r.a, r.dx_o, r.load_sem.at[9])
    dx_copy.start()
    if exchange:
        r.v_sum[0] = r.vec[...]
    net.tick()
    net.drain()
    r.vec_o[...] = r.v_sum[5] if exchange else r.vec[...]
    dx_copy.wait()


def back(exchange, s2, res, cot, up, down, ho, proj_w, qkv, pt, first, qkv_w, n1, n2, r1, r2, tb, vecs):
    rows, width = s2.shape
    images, padded = tb.shape[:2]
    hidden = up.shape[1]
    vm = pl.BlockSpec(memory_space=pltpu.VMEM)
    hbm = pl.BlockSpec(memory_space=pl.ANY)
    sds = jax.ShapeDtypeStruct
    half = width // 2
    if exchange:
        d_shape, u_shape = (hidden // 2, width), (half, 2 * hidden)
    else:
        d_shape, u_shape = (hidden, width), (width, 2 * hidden)
    ins = dict(
        s2_hbm=s2, res_hbm=res, cot_hbm=cot, up_hbm=up, down_hbm=down, ho_hbm=ho, proj_hbm=proj_w,
        qkv_hbm=qkv, pt_hbm=pt, first_hbm=first, qkv_w_hbm=qkv_w, n1_hbm=n1, n2_hbm=n2, r1_hbm=r1,
        r2_hbm=r2, tb_hbm=tb,
        vecs=vecs,
    )
    outs = dict(
        out_o=sds((rows, width), BF), dx_o=sds((rows, width), BF), d_out=sds(d_shape, BF),
        u_out=sds(u_shape, BF), vec_o=sds((16, width), F32),
    )
    dma = pltpu.SemaphoreType.DMA
    scratch = dict(
        s=pltpu.VMEM((rows, width), BF), cot=pltpu.VMEM((rows, width), BF), a=pltpu.VMEM((rows, width), BF),
        b=pltpu.VMEM((rows, width), BF), h=pltpu.VMEM((rows, width), BF), w=pltpu.VMEM((8 * width, width), BF),
        acc=pltpu.VMEM((rows, width), F32), gs=pltpu.VMEM((rows, width), F32),
        n2=pltpu.VMEM((2, padded, width), BF), r2=pltpu.VMEM((images, padded, 128), F32),
        tb=pltpu.VMEM((images, padded, 128), F32), pt=pltpu.VMEM((2, images // 2, 4, padded, padded), BF),
        up_b=pltpu.VMEM((1, hidden), F32), down_b=pltpu.VMEM((1, width), F32), g1=pltpu.VMEM((1, width), F32),
        g2=pltpu.VMEM((1, width), F32), vec=pltpu.VMEM((16, width), F32), d_stage=pltpu.VMEM((2, 512, width), BF),
        u_stage=pltpu.VMEM((2, width, 512), BF), load_sem=dma((11,)), n2_sem=dma((2,)), pt_sem=dma((2,)),
    )
    if exchange:
        scratch.update(
            d_core=pltpu.VMEM((2, 256, width), BF), u_core=pltpu.VMEM((3, half, 512), BF),
            d_in0=pltpu.VMEM((6, 128, width), BF), d_in1=pltpu.VMEM((6, 64, width), BF),
            d_in2=pltpu.VMEM((6, 32, width), BF), d_in3=pltpu.VMEM((6, 16, width), BF),
            u_in0=pltpu.VMEM((12, half, 256), BF), u_in1=pltpu.VMEM((12, half, 128), BF),
            u_in2=pltpu.VMEM((12, half // 2, 128), BF), u_in3=pltpu.VMEM((12, half // 4, 128), BF),
            d_work=pltpu.VMEM((6, 256, width), BF), u_work=pltpu.VMEM((WORK, half, 512), BF),
            v_sum=pltpu.VMEM((6, 16, width), F32), v_in=pltpu.VMEM((5, 16, width), F32),
            d_send=dma((9, 6)), d_recv=dma((9, 6)), u_send=dma((9, 12)), u_recv=dma((9, 12)),
            v_send=dma((5,)), v_recv=dma((5,)), d_done=dma((6,)), u_done=dma((12,)),
        )
    else:
        scratch.update(d_done=dma((2,)), u_done=dma((2,)))
    small = {"vecs"}
    params = dict(vmem_limit_bytes=63 << 20)
    if exchange:
        params.update(collective_id=1, has_side_effects=True)
    names = [*ins, *outs, *scratch]
    return pl.pallas_call(
        functools.partial(back_kernel, names, exchange),
        out_shape=list(outs.values()),
        in_specs=[vm if name in small else hbm for name in ins],
        out_specs=[hbm] * 4 + [vm],
        scratch_shapes=list(scratch.values()),
        compiler_params=pltpu.CompilerParams(**params),
        cost_estimate=pl.CostEstimate(flops=60_000_000_000, bytes_accessed=60_000_000, transcendentals=0),
        name="back",
    )(*ins.values())


def on_device(n_dp, n_fsdp, *args):
    names = (
        "tokens", "tissue", "norm1_gain", "norm1_shift", "qkv_matrix", "qkv_shift", "proj_matrix", "proj_shift",
        "norm2_gain", "norm2_shift", "up_matrix", "up_shift", "down_matrix", "down_shift", "cotangent",
    )
    arg = dict(zip(names, args, strict=True))
    images, slots, width = arg["tokens"].shape
    exchange = n_dp == 16 and n_fsdp == 2
    packed = jnp.concatenate([arg[name] for name in VECTORS]).astype(F32)
    packed = jnp.broadcast_to(packed, (8, packed.shape[0]))
    mats = [arg[name] for name in ("qkv_matrix", "proj_matrix", "up_matrix", "down_matrix")]
    if not exchange:
        packed = lax.all_gather(packed, "fsdp", axis=0)
        mats = [lax.all_gather(mat, "fsdp", axis=0, tiled=True) for mat in mats]
    n1, r1, cotp, first, qkv, pt, ho, res, s2, n2, r2, tb, qkv_w, proj_w, up, down, vecs = front(
        exchange, arg["tokens"], arg["cotangent"], arg["tissue"], packed, *mats
    )
    out_p, dx_p, d_sum, u_sum, v_sum = back(
        exchange, s2, res, cotp, up, down, ho, proj_w, qkv, pt, first, qkv_w, n1, n2, r1, r2, tb, vecs
    )
    hidden = arg["up_matrix"].shape[1]
    if not exchange:
        d_sum = lax.psum_scatter(d_sum, "fsdp", scatter_dimension=0, tiled=True)
        u_sum = lax.psum_scatter(u_sum, "fsdp", scatter_dimension=0, tiled=True)
        d_sum, u_sum = lax.psum((d_sum, u_sum), "dp")
        v_sum = lax.psum(v_sum, ("dp", "fsdp"))

    def own(v):
        size = v.shape[0] // n_fsdp
        return lax.dynamic_slice(v, (lax.axis_index("fsdp") * size,), (size,))

    def unpad(rows):
        return rows.reshape(images, -1, width)[:, :slots]

    return (
        unpad(out_p),
        unpad(dx_p),
        own(v_sum[6]),
        own(v_sum[7]),
        u_sum[:, hidden : hidden + 3 * width].astype(F32),
        own(v_sum[4:6].reshape(-1)),
        u_sum[:, hidden + 3 * width :].astype(F32),
        own(v_sum[3]),
        own(v_sum[1]),
        own(v_sum[2]),
        u_sum[:, :hidden].astype(F32),
        own(v_sum[8:12].reshape(-1)),
        d_sum.astype(F32),
        own(v_sum[0]),
    )


def solution(mesh):
    rows = P(("dp", "fsdp"), None, None)
    vec, mat = P("fsdp"), P("fsdp", None)
    weights = (vec, vec, mat, vec, mat, vec, vec, vec, mat, vec, mat, vec)
    return jax.shard_map(
        functools.partial(on_device, mesh.shape["dp"], mesh.shape["fsdp"]),
        mesh=mesh,
        in_specs=(rows, P(("dp", "fsdp"), None)) + weights + (rows,),
        out_specs=(rows, rows) + weights,
        check_vma=False,
    )
```

```python
import functools

import jax
import jax.numpy as jnp
from jax import lax
from jax.experimental import pallas as pl
from jax.experimental.pallas import tpu as pltpu
from jax.sharding import PartitionSpec as P

HEADS = 12
EPS = 1e-06
BF = jnp.bfloat16
F32 = jnp.float32
MESH = pl.DeviceIdType.MESH
ERF = (0.254829592, -0.284496736, 1.421413741, -1.453152027, 1.061405429)


def dot(a, b, ca, cb):
    return lax.dot_general(a, b, (((ca,), (cb,)), ((), ())), preferred_element_type=F32)


def aligned(start, size, step):
    if isinstance(start, int):
        return pl.ds(start, size)
    return pl.ds(pl.multiple_of(start, step), size)


def gelu_both(h):
    t = 1.0 / (1.0 + (0.3275911 * 0.7071067811865476) * jnp.abs(h))
    e = jnp.exp(-0.5 * h * h)
    tail = t * (ERF[0] + t * (ERF[1] + t * (ERF[2] + t * (ERF[3] + t * ERF[4])))) * (0.5 * e)
    cdf = jnp.where(h >= 0, 1.0 - tail, tail)
    return h * cdf, cdf + h * e * 0.3989422804014327


def normalized(v):
    mean = jnp.mean(v, axis=-1, keepdims=True)
    centred = v - mean
    var = jnp.mean(centred * centred, axis=-1, keepdims=True)
    rstd = lax.rsqrt(var + EPS)
    return centred * rstd, rstd


VECTORS = (
    "norm1_gain", "norm1_shift", "qkv_shift", "proj_shift", "norm2_gain", "norm2_shift", "up_shift", "down_shift",
)


def unpack(vecs, width, hidden):
    cores = vecs.shape[0]
    sizes = dict(qkv_shift=2 * width, up_shift=hidden)
    out, at = {}, 0
    for name in VECTORS:
        size = sizes.get(name, width) // cores
        out[name] = jnp.concatenate([vecs[core, 0:1, at : at + size] for core in range(cores)], axis=1)
        at += size
    return out


def head_masks(scale):
    lane = lax.broadcasted_iota(jnp.int32, (1, 128), 1)
    return [
        jnp.where(lane < 64, scale, 0.0).astype(BF),
        jnp.where(lane >= 64, scale, 0.0).astype(BF),
    ]


def front_kernel(
    remote, n_vec, *refs
):
    vec_in, refs = refs[:n_vec], refs[n_vec:]
    (
    x_hbm, cot_hbm, tissue, qkv_s, proj_s, up_s, down_s,
    n1_o, r1_o, cotp_o, first_o, qkv_o, pt_o, ho_o, res_o, s2_o, n2_o, r2_o, tb_o, qkv_wo, proj_wo, up_wo, down_wo,
    vecs_o, raw, wide, xp, cotp, first, qkv_w, qkv, pt, ho, proj_w, res, s2, tb, n1, r1, n2, r2, vecs, g1, b1, qkv_b,
    proj_b, g2, b2, packed_v, sem, osem, psem, send_sem, recv_sem, *ff_w,
    ) = refs
    images, slots = tissue.shape
    width = xp.shape[1]
    padded = xp.shape[0] // images
    scores_w = pt.shape[-1]
    hidden = up_s.shape[1]

    loads = {
        "x": pltpu.make_async_copy(x_hbm, raw, sem.at[0]),
        "cot": pltpu.make_async_copy(cot_hbm, raw, sem.at[3]),
    }
    loads["x"].start()
    sends = {}
    if remote:
        up, down = ff_w
        at = 0
        for ref in vec_in:
            size = ref.shape[0]
            packed_v[0:1, at : at + size] = ref[...].astype(F32).reshape(1, size)
            at += size
        dp, core = lax.axis_index("dp"), lax.axis_index("fsdp")
        barrier = pltpu.get_barrier_semaphore()
        pl.semaphore_signal(barrier, inc=1, device_id=(dp, 1 - core), device_id_type=MESH)
        pl.semaphore_wait(barrier, 1)
        parts = (("vecs", packed_v, vecs), ("qkv_w", qkv_s, qkv_w), ("proj_w", proj_s, proj_w), ("up", up_s, up), ("down", down_s, down))
        for n, (name, src, dst) in enumerate(parts):
            if name == "vecs":
                here = dst.at[core]
            else:
                share = src.shape[0]
                here = dst.at[aligned(core * share, share, share)]
            sends[name] = pltpu.make_async_remote_copy(
                src_ref=src, dst_ref=here, send_sem=send_sem.at[n], recv_sem=recv_sem.at[n],
                device_id=(dp, 1 - core), device_id_type=MESH,
            )
            sends[name].start()
            loads[name] = pltpu.make_async_copy(src, here, sem.at[4 + n])
            loads[name].start()
    else:
        loads["vecs"] = pltpu.make_async_copy(vec_in[0], vecs, sem.at[4])
        loads["qkv_w"] = pltpu.make_async_copy(qkv_s, qkv_w, sem.at[1])
        loads["proj_w"] = pltpu.make_async_copy(proj_s, proj_w, sem.at[2])
        for name in ("vecs", "qkv_w", "proj_w"):
            loads[name].start()

    def arrive(name):
        loads[name].wait()
        if remote:
            sends[name].wait()

    arrive("vecs")
    vec = unpack(vecs, width, hidden)
    for ref, name in (
        (g1, "norm1_gain"), (b1, "norm1_shift"), (qkv_b, "qkv_shift"), (proj_b, "proj_shift"), (g2, "norm2_gain"), (b2, "norm2_shift"),
    ):
        ref[...] = vec[name]
    stores = []

    def store(n, src, dst):
        copy = pltpu.make_async_copy(src, dst, osem.at[n])
        copy.start()
        stores.append(copy)

    pad_rows = jnp.zeros((padded - slots, width), F32)

    def widen():
        step = raw.shape[0] // 14

        @pl.loop(0, 14)
        def _(n):
            rows = aligned(n * step, step, step)
            for t in range(width // 128):
                wide[t, rows] = raw[rows, t * 128 : (t + 1) * 128].astype(F32)

    def image(i):
        parts = [wide[t, pl.ds(i, slots, stride=images)] for t in range(width // 128)]
        return jnp.concatenate([jnp.concatenate(parts, axis=1), pad_rows], axis=0)

    loads["x"].wait()
    widen()
    loads["cot"].start()

    @pl.loop(0, images)
    def _(i):
        rows = aligned(i * padded, padded, 16)
        block = image(i)
        xp[rows] = block.astype(BF)
        n, rstd = normalized(block)
        n1[rows] = n.astype(BF)
        r1[i] = jnp.broadcast_to(rstd, (padded, 128))
        first[rows] = (n * g1[...] + b1[...]).astype(BF)
        t_row = jnp.concatenate(
            [tissue[pl.ds(i, 1)].astype(F32), jnp.zeros((1, padded - slots), F32)], axis=1
        )
        tb[i] = jnp.broadcast_to(t_row, (128, padded)).T

    store(0, n1, n1_o)
    store(8, r1, r1_o)
    loads["cot"].wait()
    widen()

    @pl.loop(0, images)
    def _(i):
        cotp[aligned(i * padded, padded, 16)] = image(i).astype(BF)

    store(7, cotp, cotp_o)
    store(1, first, first_o)
    store(2, tb, tb_o)
    arrive("qkv_w")
    if remote:
        store(11, qkv_w, qkv_wo)
        store(12, vecs, vecs_o)
    for part in range(3):
        cols = slice(part * width, (part + 1) * width)
        prod = dot(first[...], qkv_w[:, cols], 1, 0)
        if part == 0:
            prod = prod + qkv_b[:, :width]
        if part == 2:
            prod = prod + qkv_b[:, width:]
        qkv[:, cols] = prod.astype(BF)
    store(3, qkv, qkv_o)

    scaled = head_masks(0.125)
    ones = head_masks(1.0)

    @pl.loop(0, images)
    def _(i):
        rows = aligned(i * padded, padded, 16)
        slot = lax.rem(i, 2)
        out = pltpu.make_async_copy(pt.at[slot], pt_o.at[i], psem.at[slot])

        @pl.when(i >= 2)
        def _():
            out.wait()

        t = tb[i]
        valid = jnp.concatenate([t, t[:, : scores_w - 128]], axis=1) > 0
        for pair in range(HEADS // 2):
            cols = [slice(b * width + pair * 128, b * width + pair * 128 + 128) for b in range(3)]
            q, k, v = qkv[rows, cols[0]], qkv[rows, cols[1]], qkv[rows, cols[2]]
            mixed = None
            for h in range(2):
                st = jnp.where(valid, dot(k * scaled[h], q, 1, 1), -1e30)
                e = jnp.exp(st - jnp.max(st, axis=0, keepdims=True))
                probs = (e * (1.0 / jnp.sum(e, axis=0, keepdims=True))).astype(BF)
                pt[slot, pair * 2 + h] = probs
                part = dot(probs, v * ones[h], 0, 0)
                mixed = part if mixed is None else mixed + part
            ho[rows, cols[0]] = (mixed * t).astype(BF)
        out.start()

    store(4, ho, ho_o)
    arrive("proj_w")
    if remote:
        store(13, proj_w, proj_wo)
    res[...] = dot(ho[...], proj_w[...], 1, 0)

    @pl.loop(0, images)
    def _(i):
        rows = aligned(i * padded, padded, 16)
        total = xp[rows].astype(F32) + res[rows] + proj_b[...]
        res[rows] = total
        n, rstd = normalized(total)
        n2[rows] = n.astype(BF)
        r2[i] = jnp.broadcast_to(rstd, (padded, 128))
        s2[rows] = (n * g2[...] + b2[...]).astype(BF)

    if remote:
        arrive("up")
        store(14, up, up_wo)
        arrive("down")
        store(15, down, down_wo)
    store(5, s2, s2_o)
    store(6, res, res_o)
    store(9, n2, n2_o)
    store(10, r2, r2_o)
    for slot in range(2):
        pltpu.make_async_copy(pt.at[slot], pt_o.at[0], psem.at[slot]).wait()
    for copy in stores:
        copy.wait()


def front(remote, tokens, cot, tissue, vectors, qkv_w, proj_w, up, down):
    images, slots, width = tokens.shape
    tokens, cot = (v.transpose(1, 0, 2).reshape(slots * images, width) for v in (tokens, cot))
    padded = -(-slots // 16) * 16
    rows = images * padded
    cores = 2 if remote else vectors[0].shape[0]
    hidden = up.shape[1]
    vm = pl.BlockSpec(memory_space=pltpu.VMEM)
    hbm = pl.BlockSpec(memory_space=pl.ANY)
    sds = jax.ShapeDtypeStruct
    flat, col = sds((rows, width), BF), sds((images, padded, 128), F32)
    vecs_shape = (cores, 8, sum(v.shape[-1] for v in vectors))
    outs = [
        flat, col, flat, flat, sds((rows, 3 * width), BF), sds((images, HEADS, padded, padded), BF), flat,
        sds((rows, width), F32), flat, flat, col, col, sds((width, 3 * width), BF), sds((width, width), BF),
        sds((width, hidden), BF), sds((hidden, width), BF), sds(vecs_shape, F32),
    ]
    flat_v, col_v = pltpu.VMEM((rows, width), BF), pltpu.VMEM((images, padded, 128), F32)
    row_v = pltpu.VMEM((1, width), F32)
    dma = pltpu.SemaphoreType.DMA
    params = dict(collective_id=2, has_side_effects=True) if remote else {}
    got = pl.pallas_call(
        functools.partial(front_kernel, remote, len(vectors)),
        out_shape=outs,
        in_specs=[vm if remote else hbm] * len(vectors) + [hbm, hbm, vm, hbm, hbm, hbm, hbm],
        out_specs=[hbm] * len(outs),
        scratch_shapes=[
            pltpu.VMEM((slots * images, width), BF), pltpu.VMEM((width // 128, slots * images, 128), F32), flat_v, flat_v,
            flat_v,
            pltpu.VMEM((width, 3 * width), BF), pltpu.VMEM((rows, 3 * width), BF),
            pltpu.VMEM((2, HEADS, padded, padded), BF), flat_v, pltpu.VMEM((width, width), BF),
            pltpu.VMEM((rows, width), F32), flat_v, col_v, flat_v, col_v, flat_v, col_v, pltpu.VMEM(vecs_shape, F32),
            row_v, row_v, pltpu.VMEM((1, 2 * width), F32), row_v, row_v, row_v,
            pltpu.VMEM(vecs_shape[1:], F32), dma((9,)), dma((16,)), dma((2,)),
            dma((5,)), dma((5,)),
        ] + ([pltpu.VMEM((width, hidden), BF), pltpu.VMEM((hidden, width), BF)] if remote else []),
        compiler_params=pltpu.CompilerParams(vmem_limit_bytes=62 << 20, **params),
        cost_estimate=pl.CostEstimate(flops=13_000_000_000, bytes_accessed=40_000_000, transcendentals=0),
        name="front",
    )(*vectors, tokens, cot, tissue, qkv_w, proj_w, up, down)
    if not remote:
        got = [*got[:12], qkv_w, proj_w, up, down, vectors[0]]
    return got


D_ORDER = ((1, 2, 4), (2, 4, 1), (4, 1, 2), (1, 2, 4), (2, 4, 1), (4, 1, 2))
U_ORDER = ((4, 1, 2), (1, 2, 4), (2, 4, 1), (4, 1, 2), (1, 2, 4), (2, 4, 1), (4, 1, 2), (1, 2, 4), (2, 4, 1), (4, 1, 2), (1, 2, 4), (2, 4, 1))
D_TICKS = (
    (1, 2, 4, 6, 7, 8, 9, 10, 13, 15),
    (3, 4, 6, 8, 9, 10, 11, 13, 16, 19),
    (5, 6, 8, 10, 12, 14, 16, 18, 20, 23),
    (7, 8, 10, 13, 15, 17, 20, 22, 24, 27),
    (9, 10, 14, 17, 19, 21, 23, 24, 27, 35),
    (11, 12, 15, 17, 19, 21, 23, 25, 27, 36),
)
U_TICKS = (
    (1, 2, 4, 6, 7, 8, 10, 12, 14, 20),
    (3, 4, 6, 8, 10, 11, 13, 15, 16, 19),
    (5, 6, 8, 10, 11, 13, 15, 16, 20, 23),
    (7, 8, 10, 12, 14, 16, 19, 20, 22, 25),
    (9, 10, 13, 15, 17, 20, 22, 24, 26, 32),
    (11, 12, 15, 19, 20, 22, 24, 26, 28, 44),
    (15, 16, 21, 23, 25, 27, 30, 39, 52, 63),
    (19, 20, 23, 25, 27, 30, 40, 47, 54, 61),
    (19, 20, 23, 26, 28, 31, 42, 49, 59, 67),
    (22, 23, 27, 33, 43, 51, 57, 62, 66, 71),
    (25, 26, 34, 46, 53, 58, 65, 68, 70, 73),
    (25, 26, 29, 38, 48, 55, 60, 64, 69, 72),
)
V_TICKS = (30, 31, 34, 37, 40, 43)
WORK = 7


class Exchange:
    def __init__(self, r):
        self.r = r
        self.dp = lax.axis_index("dp")
        self.core = lax.axis_index("fsdp")
        self.due = self.plan()
        self.now = 0
        self.sides = {bit: (self.dp // bit) % 2 for bit in (1, 2, 4, 8)}
        self.peers = {bit: self.dp + bit * (1 - 2 * self.sides[bit]) for bit in (1, 2, 4, 8)}

    def other_core(self):
        return (self.dp, 1 - self.core)

    def greet(self):
        barrier = pltpu.get_barrier_semaphore()
        peers = [self.other_core()] + [(self.peers[bit], self.core) for bit in (1, 2, 4, 8)]
        for peer in peers:
            pl.semaphore_signal(barrier, inc=1, device_id=peer, device_id_type=MESH)
        pl.semaphore_wait(barrier, len(peers))

    def at_stage(self, order, k):
        bit = (*order, 8)[k]
        return self.sides[bit], self.peers[bit]

    def d_regions(self, u):
        start, size, out = 0, 256, []
        for k in range(4):
            side, peer = self.at_stage(D_ORDER[u], k)
            size //= 2
            out.append((peer, start + side * size, start + (1 - side) * size, size))
            start = start + side * size
        return out

    def d_copy(self, e, u):
        r = self.r
        sems = dict(send_sem=r.d_send.at[e, u], recv_sem=r.d_recv.at[e, u], device_id_type=MESH)
        if e == 0:
            src = r.d_stage.at[u % 2, aligned((1 - self.core) * 256, 256, 256)]
            return pltpu.make_async_remote_copy(
                src_ref=src, dst_ref=r.d_core.at[u % 2], device_id=self.other_core(), **sems
            )
        k = e - 1 if e <= 4 else 8 - e
        peer, kept, sent, size = self.d_regions(u)[k]
        if e <= 4:
            src, dst = r.d_work.at[u, aligned(sent, size, 16)], r.d_in[k].at[u]
        else:
            src = dst = r.d_out.at[aligned(u * 256 + kept, size, 16)]
            if e == 5:
                src = r.d_work.at[u, aligned(kept, size, 16)]
        return pltpu.make_async_remote_copy(
            src_ref=src, dst_ref=dst, device_id=(peer, self.core), **sems
        )

    def d_event(self, e, u):
        r = self.r
        if e >= 1:
            self.d_copy(e - 1, u).wait()
        if e == 1:
            r.d_work[u] = r.d_stage[u % 2, aligned(self.core * 256, 256, 256)] + r.d_core[u % 2]
        elif 2 <= e <= 5:
            _, kept, _, size = self.d_regions(u)[e - 2]
            r.d_work[u, aligned(kept, size, 16)] += r.d_in[e - 2][u]
        if e == 5:
            self.d_own(u).start()
        if e == 6:
            self.d_own(u).wait()
        if e < 9:
            self.d_copy(e, u).start()

    def d_own(self, u):
        _, kept, _, size = self.d_regions(u)[3]
        return pltpu.make_async_copy(
            self.r.d_work.at[u, aligned(kept, size, 16)],
            self.r.d_out.at[aligned(u * 256 + kept, size, 16)],
            self.r.d_done.at[u],
        )

    def u_blocks(self, u):
        width = self.r.width
        if u < 6:
            return u * 256, 2 * width + u * 256
        tail = [4 * width + b * width + g * 256 for g in range(3) for b in range(3)]
        tail = [7 * width, 7 * width + 256, 7 * width + 512] + tail
        return tail[2 * (u - 6)], tail[2 * (u - 6) + 1]

    def u_regions(self, u):
        height = self.r.width // 2
        sides, peers = zip(*(self.at_stage(U_ORDER[u], k) for k in range(4)))
        block, col, row = sides[0], sides[1] * 128, 0
        out = [
            (peers[0], (0, height, block, 0, 256), (0, height, 1 - block, 0, 256)),
            (peers[1], (0, height, block, col, 128), (0, height, block, 128 - col, 128)),
        ]
        for k in (2, 3):
            height //= 2
            kept, sent = row + sides[k] * height, row + (1 - sides[k]) * height
            out.append((peers[k], (kept, height, block, col, 128), (sent, height, block, col, 128)))
            row = kept
        return out

    @staticmethod
    def u_work(region):
        row, rows, block, col, cols = region
        return aligned(row, rows, 32), aligned(block * 256 + col, cols, 128)

    def u_place(self, u, region):
        row, rows, block, col, cols = region
        first, second = self.u_blocks(u)
        return aligned(row, rows, 32), aligned(first + block * (second - first) + col, cols, 128)

    def u_copy(self, e, u):
        r = self.r
        sems = dict(send_sem=r.u_send.at[e, u], recv_sem=r.u_recv.at[e, u], device_id_type=MESH)
        half = r.width // 2
        if e == 0:
            src = r.u_stage.at[u % 2, aligned((1 - self.core) * half, half, half)]
            return pltpu.make_async_remote_copy(
                src_ref=src, dst_ref=r.u_core.at[u % 3], device_id=self.other_core(), **sems
            )
        k = e - 1 if e <= 4 else 8 - e
        peer, kept, sent = self.u_regions(u)[k]
        if e <= 4:
            rows, cols = self.u_work(sent)
            src, dst = r.u_work.at[u % WORK, rows, cols], r.u_in[k].at[u]
        else:
            src = dst = r.u_out.at[self.u_place(u, kept)]
            if e == 5:
                rows, cols = self.u_work(kept)
                src = r.u_work.at[u % WORK, rows, cols]
        return pltpu.make_async_remote_copy(
            src_ref=src, dst_ref=dst, device_id=(peer, self.core), **sems
        )

    def u_event(self, e, u):
        r = self.r
        half = r.width // 2
        if e >= 1:
            self.u_copy(e - 1, u).wait()
        if e == 1:
            r.u_work[u % WORK] = r.u_stage[u % 2, aligned(self.core * half, half, half)] + r.u_core[u % 3]
        elif 2 <= e <= 5:
            rows, cols = self.u_work(self.u_regions(u)[e - 2][1])
            r.u_work[u % WORK, rows, cols] += r.u_in[e - 2][u]
        if e == 5:
            self.u_own(u).start()
        if e == 6:
            self.u_own(u).wait()
        if e < 9:
            self.u_copy(e, u).start()

    def u_own(self, u):
        kept = self.u_regions(u)[3][1]
        rows, cols = self.u_work(kept)
        return pltpu.make_async_copy(
            self.r.u_work.at[u % WORK, rows, cols], self.r.u_out.at[self.u_place(u, kept)], self.r.u_done.at[u]
        )

    def v_copy(self, e):
        r = self.r
        peer = self.other_core() if e == 0 else (self.peers[1 << (e - 1)], self.core)
        return pltpu.make_async_remote_copy(
            src_ref=r.v_sum.at[e], dst_ref=r.v_in.at[e], send_sem=r.v_send.at[e],
            recv_sem=r.v_recv.at[e], device_id=peer, device_id_type=MESH,
        )

    def v_event(self, e, u=0):
        r = self.r
        if e >= 1:
            self.v_copy(e - 1).wait()
            r.v_sum[e] = r.v_sum[e - 1] + r.v_in[e - 1]
        if e < 5:
            self.v_copy(e).start()

    def plan(self):
        due = {}
        for event, table in ((self.d_event, D_TICKS), (self.u_event, U_TICKS), (self.v_event, (V_TICKS,))):
            for u, ticks in enumerate(table):
                for e, tick in enumerate(ticks):
                    due.setdefault(tick, []).append((-e, u, event))
        return due

    def run(self, tick):
        for e, u, event in sorted(self.due.pop(tick, []), key=lambda item: item[:2]):
            event(-e, u)

    def loop_tick(self, c, chunks, j):
        for k in range(chunks):
            if self.due.get(2 * k + j):

                @pl.when(c == k)
                def _(k=k):
                    self.run(2 * k + j)

        self.now = 2 * chunks - 1

    def tick(self):
        self.now += 1
        self.run(self.now)

    def tail(self, u):
        pass

    def drain(self):
        while self.due:
            self.tick()


class Local:
    def __init__(self, r):
        self.r = r
        self.copies = []

    def greet(self):
        pass

    def d_store(self, u):
        r = self.r
        outs = []
        for half in range(2):
            rows = aligned(half * 2 * r.width + u * 256, 256, 256)
            outs.append(
                pltpu.make_async_copy(r.d_stage.at[lax.rem(u, 2), half * 256 : half * 256 + 256], r.d_out.at[rows], r.d_done.at[half])
            )
        return outs

    def d_event(self, e, u):
        for copy in self.d_store(u):
            copy.start()
        for copy in self.d_store(u):
            copy.wait()

    def blocks(self, u):
        if isinstance(u, int):
            return Exchange.u_blocks(self, u)
        return u * 256, 2 * self.r.width + u * 256

    def u_event(self, e, u):
        r = self.r
        for n, col in enumerate(self.blocks(u)):
            copy = pltpu.make_async_copy(
                r.u_stage.at[lax.rem(u, 2), :, n * 256 : n * 256 + 256],
                r.u_out.at[:, aligned(col, 256, 256)],
                r.u_done.at[n],
            )
            copy.start()
            copy.wait()

    def loop_tick(self, c, chunks, j):
        if j == 1:
            self.d_event(0, c)
            self.u_event(0, c)

    def tick(self):
        pass

    def tail(self, u):
        self.u_event(0, u)

    def drain(self):
        pass


class Refs:
    def __init__(self, names, refs):
        self.__dict__.update(zip(names, refs, strict=True))


def back_kernel(names, exchange, *refs):
    r = Refs(names, refs)
    rows_all, width = r.gs.shape
    r.width = width
    images = r.tb_hbm.shape[0]
    padded = rows_all // images
    chunks = r.up_b.shape[1] // 512
    if exchange:
        r.d_in = [r.d_in0, r.d_in1, r.d_in2, r.d_in3]
        r.u_in = [r.u_in0, r.u_in1, r.u_in2, r.u_in3]
    net = Exchange(r) if exchange else Local(r)

    def load(n, src, dst):
        copy = pltpu.make_async_copy(src, dst, r.load_sem.at[n])
        copy.start()
        return copy

    early = [load(0, r.s2_hbm, r.s), load(1, r.cot_hbm, r.cot), load(2, r.res_hbm, r.acc)]
    for b in range(4):
        src = r.up_hbm.at[:, b * width : (b + 1) * width]
        early.append(load(3 + b, src, r.w.at[b * width : (b + 1) * width]))
    early.append(load(7, r.down_hbm, r.w.at[4 * width : 8 * width]))
    late = [load(8, r.ho_hbm, r.h), load(10, r.tb_hbm, r.tb), load(9, r.r2_hbm, r.r2)]
    net.greet()
    vec = unpack(r.vecs, width, r.up_b.shape[1])
    for ref, name in ((r.up_b, "up_shift"), (r.down_b, "down_shift"), (r.g1, "norm1_gain"), (r.g2, "norm2_gain")):
        ref[...] = vec[name]
    r.gs[...] = jnp.zeros_like(r.gs)
    r.vec[...] = jnp.zeros_like(r.vec)
    for copy in early:
        copy.wait()

    def pt_copy(it, slot):
        g, half = it // 2, it % 2
        count = images // 2
        return pltpu.make_async_copy(
            r.pt_hbm.at[half * count : (half + 1) * count, g * 4 : g * 4 + 4],
            r.pt.at[slot],
            r.pt_sem.at[slot],
        )

    pt_copy(0, 0).start()

    def part_of(c, half):
        upper = jnp.where(c >= 3, 1, 0)
        block = (2 * half + upper) * width
        cols = aligned((c - 3 * upper) * 256, 256, 256)
        down = aligned(4 * width + half * 2 * width + c * 256, 256, 256)
        return block, cols, down, 8 + 2 * half + upper

    def ff_in(c, half):
        block, cols, down, row = part_of(c, half)
        at = slice(half * 256, half * 256 + 256)
        bias = r.up_b[:, aligned(half * 2 * width + c * 256, 256, 256)]
        hidden = dot(r.s[...], r.w[aligned(block, width, width), cols], 1, 0) + bias
        g_active = dot(r.cot[...], r.w[down], 1, 1)
        active, slope = gelu_both(hidden)
        r.a[:, at] = active.astype(BF)
        g_hidden = (g_active * slope).astype(BF)
        r.b[:, at] = g_hidden
        r.vec[pl.ds(row, 1), cols] = jnp.sum(g_hidden.astype(F32), axis=0, keepdims=True)

    def ff_out(c):
        (block0, cols, down0, _), (block1, _, down1, _) = part_of(c, 0), part_of(c, 1)
        for n in range(width // 256):
            to = slice(n * 256, n * 256 + 256)
            up0, up1 = aligned(block0 + n * 256, 256, 256), aligned(block1 + n * 256, 256, 256)
            r.acc[:, to] += dot(r.a[:, :256], r.w[down0, to], 1, 0) + dot(r.a[:, 256:512], r.w[down1, to], 1, 0)
            r.gs[:, to] += dot(r.b[:, :256], r.w[up0, cols], 1, 1) + dot(r.b[:, 256:512], r.w[up1, cols], 1, 1)

    @pl.loop(0, chunks)
    def _(c):
        ff_in(c, 0)
        ff_in(c, 1)
        ff_out(c)
        net.loop_tick(c, chunks, 0)
        r.d_stage[lax.rem(c, 2)] = dot(r.a[:, :512], r.cot[...], 0, 0).astype(BF)
        r.u_stage[lax.rem(c, 2)] = dot(r.s[...], r.b[:, :512], 0, 0).astype(BF)
        net.loop_tick(c, chunks, 1)

    late2 = []
    for b in range(3):
        src = r.qkv_hbm.at[:, b * width : (b + 1) * width]
        late2.append(load(3 + b, src, r.w.at[b * rows_all : (b + 1) * rows_all]))
    proj_rows = slice(3 * rows_all, 3 * rows_all + width)
    late2.append(load(6, r.proj_hbm, r.w.at[proj_rows]))
    late2.append(load(0, r.first_hbm, r.s))

    def norm_copy(i, slot):
        return pltpu.make_async_copy(
            r.n2_hbm.at[aligned(i * padded, padded, 16)], r.n2.at[slot], r.n2_sem.at[slot]
        )

    norm_copy(0, 0).start()
    r.b[...] = (r.acc[...] + r.down_b[...]).astype(BF)
    out_copy = pltpu.make_async_copy(r.b, r.out_o, r.load_sem.at[7])
    out_copy.start()
    net.tick()

    def folded(v):
        return v[:8] + v[8:]

    def norm_back(grad, n, rstd, gain):
        t = grad * gain
        centre = t - jnp.mean(t, axis=-1, keepdims=True) - n * jnp.mean(t * n, axis=-1, keepdims=True)
        return jnp.concatenate([rstd] * (width // 128), axis=1) * centre

    def add_vec(first_row, sums):
        for n, value in enumerate(sums):
            r.vec[first_row + n : first_row + n + 1] += jnp.sum(value, axis=0, keepdims=True)

    for copy in late:
        copy.wait()
    for part in range(2):

        @pl.loop(part * images // 2, (part + 1) * images // 2)
        def _(i):
            slot = lax.rem(i, 2)
            norm_copy(i, slot).wait()

            @pl.when(i + 1 < images)
            def _():
                norm_copy(i + 1, 1 - slot).start()

            sums = [0.0] * 4
            for tile in range(padded // 16):
                rows = aligned(i * padded + tile * 16, 16, 16)
                at = slice(tile * 16, tile * 16 + 16)
                n = r.n2[slot, at].astype(F32)
                grad = r.gs[rows]
                cot = r.cot[rows].astype(F32)
                g_res = cot + norm_back(grad, n, r.r2[i, at], r.g2[...])
                r.gs[rows] = g_res
                low = g_res.astype(BF)
                r.a[rows] = low
                terms = (cot, grad * n, grad, low.astype(F32))
                sums = [total + folded(term) for total, term in zip(sums, terms)]
            add_vec(0, sums)

        net.tick()
    for copy in late2:
        copy.wait()
    qkv_at = [r.cot.at[:width], r.cot.at[width : 2 * width], r.w.at[proj_rows]]
    qkv_src = [r.qkv_w_hbm.at[:, b * width : (b + 1) * width] for b in range(3)]
    qkv_loads = [load(3 + b, qkv_src[b], qkv_at[b]) for b in range(2)]
    for n in range(3):
        at = slice(n * 256, n * 256 + 256)
        p_grad = dot(r.h[...], r.a[:, at], 0, 0).astype(BF)
        r.u_stage[n // 2, :, n % 2 * 256 : n % 2 * 256 + 256] = p_grad
    net.tail(6)
    net.tick()
    out_copy.wait()
    n1_copy = load(8, r.n1_hbm, r.h)
    for n in range(3):
        proj_at = slice(3 * rows_all + n * 256, 3 * rows_all + n * 256 + 256)
        g_heads = dot(r.a[...], r.w[proj_at], 1, 1)
        for i in range(images):
            rows = slice(i * padded, (i + 1) * padded)
            t = jnp.concatenate([r.tb[i]] * 2, axis=1)
            r.b[rows, n * 256 : n * 256 + 256] = (g_heads[rows] * t).astype(BF)
    qkv_loads.append(load(5, qkv_src[2], qkv_at[2]))
    net.tick()

    scaled = head_masks(0.125)
    ones = head_masks(1.0)
    stage = 1
    filled = 1
    for g in range(3):
        for half in range(2):
            it = 2 * g + half
            slot = it % 2
            pt_copy(it, slot).wait()
            if it < 5:
                pt_copy(it + 1, 1 - slot).start()
            for n in range(images // 2):
                i = half * (images // 2) + n
                for p in range(2):
                    cols = slice((2 * g + p) * 128, (2 * g + p + 1) * 128)
                    at = [slice(b * rows_all + i * padded, b * rows_all + (i + 1) * padded) for b in range(3)]
                    q, k, v = r.w[at[0], cols], r.w[at[1], cols], r.w[at[2], cols]
                    gh = r.b[i * padded : (i + 1) * padded, cols]
                    gq = gk = gv = None
                    for h in range(2):
                        low = r.pt[slot, n, 2 * p + h]
                        probs = low.astype(F32)
                        g_probs = dot(v * ones[h], gh, 1, 1)
                        row_dot = jnp.sum(probs * g_probs, axis=0, keepdims=True)
                        g_scores = (probs * (g_probs - row_dot)).astype(BF)
                        parts = (
                            dot(g_scores, k * scaled[h], 0, 0),
                            dot(g_scores, q * scaled[h], 1, 0),
                            dot(low, gh * ones[h], 1, 0),
                        )
                        gq, gk, gv = parts if gq is None else (gq + parts[0], gk + parts[1], gv + parts[2])
                    r.w[at[0], cols] = gq.astype(BF)
                    r.w[at[1], cols] = gk.astype(BF)
                    r.w[at[2], cols] = gv.astype(BF)
            net.tick()
        cols = slice(g * 256, (g + 1) * 256)
        for b in range(3):
            grads = r.w[b * rows_all : (b + 1) * rows_all, cols]
            r.u_stage[stage, :, filled * 256 : (filled + 1) * 256] = dot(r.s[...], grads, 0, 0).astype(BF)
            if b != 1:
                r.vec[4 + b // 2 : 5 + b // 2, cols] = jnp.sum(grads.astype(F32), axis=0, keepdims=True)
            filled += 1
            if filled == 2:
                net.tail(6 + (3 * g + b + 3) // 2)
                stage, filled = 1 - stage, 0
        net.tick()

    n1_copy.wait()
    r1_copy = load(10, r.r1_hbm, r.tb)
    for b in range(3):
        qkv_loads[b].wait()
        part = dot(r.w[b * rows_all : (b + 1) * rows_all], qkv_at[b][...], 1, 1)
        if b == 0:
            r.acc[...] = part
        else:
            r.acc[...] += part
        net.tick()

    r1_copy.wait()
    for part in range(2):

        @pl.loop(part * images // 2, (part + 1) * images // 2)
        def _(i):
            sums = [0.0] * 2
            for tile in range(padded // 16):
                rows = aligned(i * padded + tile * 16, 16, 16)
                at = slice(tile * 16, tile * 16 + 16)
                n = r.h[rows].astype(F32)
                grad = r.acc[rows]
                r.a[rows] = (r.gs[rows] + norm_back(grad, n, r.tb[i, at], r.g1[...])).astype(BF)
                sums = [total + folded(term) for total, term in zip(sums, (grad * n, grad))]
            add_vec(6, sums)

        if part == 0:
            net.tick()

    dx_copy = pltpu.make_async_copy(r.a, r.dx_o, r.load_sem.at[9])
    dx_copy.start()
    if exchange:
        r.v_sum[0] = r.vec[...]
    net.tick()
    net.drain()
    r.vec_o[...] = r.v_sum[5] if exchange else r.vec[...]
    dx_copy.wait()


def back(exchange, s2, res, cot, up, down, ho, proj_w, qkv, pt, first, qkv_w, n1, n2, r1, r2, tb, vecs):
    rows, width = s2.shape
    images, padded = tb.shape[:2]
    hidden = up.shape[1]
    vm = pl.BlockSpec(memory_space=pltpu.VMEM)
    hbm = pl.BlockSpec(memory_space=pl.ANY)
    sds = jax.ShapeDtypeStruct
    half = width // 2
    if exchange:
        d_shape, u_shape = (hidden // 2, width), (half, 2 * hidden)
    else:
        d_shape, u_shape = (hidden, width), (width, 2 * hidden)
    ins = dict(
        s2_hbm=s2, res_hbm=res, cot_hbm=cot, up_hbm=up, down_hbm=down, ho_hbm=ho, proj_hbm=proj_w,
        qkv_hbm=qkv, pt_hbm=pt, first_hbm=first, qkv_w_hbm=qkv_w, n1_hbm=n1, n2_hbm=n2, r1_hbm=r1,
        r2_hbm=r2, tb_hbm=tb,
        vecs=vecs,
    )
    outs = dict(
        out_o=sds((rows, width), BF), dx_o=sds((rows, width), BF), d_out=sds(d_shape, BF),
        u_out=sds(u_shape, BF), vec_o=sds((16, width), F32),
    )
    dma = pltpu.SemaphoreType.DMA
    scratch = dict(
        s=pltpu.VMEM((rows, width), BF), cot=pltpu.VMEM((rows, width), BF), a=pltpu.VMEM((rows, width), BF),
        b=pltpu.VMEM((rows, width), BF), h=pltpu.VMEM((rows, width), BF), w=pltpu.VMEM((8 * width, width), BF),
        acc=pltpu.VMEM((rows, width), F32), gs=pltpu.VMEM((rows, width), F32),
        n2=pltpu.VMEM((2, padded, width), BF), r2=pltpu.VMEM((images, padded, 128), F32),
        tb=pltpu.VMEM((images, padded, 128), F32), pt=pltpu.VMEM((2, images // 2, 4, padded, padded), BF),
        up_b=pltpu.VMEM((1, hidden), F32), down_b=pltpu.VMEM((1, width), F32), g1=pltpu.VMEM((1, width), F32),
        g2=pltpu.VMEM((1, width), F32), vec=pltpu.VMEM((16, width), F32), d_stage=pltpu.VMEM((2, 512, width), BF),
        u_stage=pltpu.VMEM((2, width, 512), BF), load_sem=dma((11,)), n2_sem=dma((2,)), pt_sem=dma((2,)),
    )
    if exchange:
        scratch.update(
            d_core=pltpu.VMEM((2, 256, width), BF), u_core=pltpu.VMEM((3, half, 512), BF),
            d_in0=pltpu.VMEM((6, 128, width), BF), d_in1=pltpu.VMEM((6, 64, width), BF),
            d_in2=pltpu.VMEM((6, 32, width), BF), d_in3=pltpu.VMEM((6, 16, width), BF),
            u_in0=pltpu.VMEM((12, half, 256), BF), u_in1=pltpu.VMEM((12, half, 128), BF),
            u_in2=pltpu.VMEM((12, half // 2, 128), BF), u_in3=pltpu.VMEM((12, half // 4, 128), BF),
            d_work=pltpu.VMEM((6, 256, width), BF), u_work=pltpu.VMEM((WORK, half, 512), BF),
            v_sum=pltpu.VMEM((6, 16, width), F32), v_in=pltpu.VMEM((5, 16, width), F32),
            d_send=dma((9, 6)), d_recv=dma((9, 6)), u_send=dma((9, 12)), u_recv=dma((9, 12)),
            v_send=dma((5,)), v_recv=dma((5,)), d_done=dma((6,)), u_done=dma((12,)),
        )
    else:
        scratch.update(d_done=dma((2,)), u_done=dma((2,)))
    small = {"vecs"}
    params = dict(vmem_limit_bytes=63 << 20)
    if exchange:
        params.update(collective_id=1, has_side_effects=True)
    names = [*ins, *outs, *scratch]
    return pl.pallas_call(
        functools.partial(back_kernel, names, exchange),
        out_shape=list(outs.values()),
        in_specs=[vm if name in small else hbm for name in ins],
        out_specs=[hbm] * 4 + [vm],
        scratch_shapes=list(scratch.values()),
        compiler_params=pltpu.CompilerParams(**params),
        cost_estimate=pl.CostEstimate(flops=60_000_000_000, bytes_accessed=60_000_000, transcendentals=0),
        name="back",
    )(*ins.values())


def finish_kernel(
    with_vec, images, d, u, out_p, dx_p, vec, d_o, up_o, qkv_o, proj_o, out_o, dx_o, *rest
):
    vec_o, (d_v, u_v, out_v, dx_v, d_f, up_f, qkv_f, proj_f, wide, out_r, dx_r, sem, osem) = rest[:-13], rest[-13:]
    width = d.shape[1]
    hidden = up_o.shape[1]
    slots_images = out_o.shape[0]
    parts, u_parts = 4, 3
    loads, stores = [], []

    def load(src, dst):
        copy = pltpu.make_async_copy(src, dst, sem.at[len(loads)])
        copy.start()
        loads.append(copy)

    def store(src, dst):
        copy = pltpu.make_async_copy(src, dst, osem.at[len(stores)])
        copy.start()
        stores.append(copy)

    step, u_step = d.shape[0] // parts, u.shape[0] // u_parts
    for n in range(parts):
        load(d.at[n * step : (n + 1) * step], d_v.at[n * step : (n + 1) * step])
    for n in range(u_parts):
        load(u.at[n * u_step : (n + 1) * u_step], u_v.at[n * u_step : (n + 1) * u_step])
    load(out_p, out_v)
    load(dx_p, dx_v)
    for n in range(parts):
        rows = slice(n * step, (n + 1) * step)
        loads[n].wait()
        d_f[rows] = d_v[rows].astype(F32)
        store(d_f.at[rows], d_o.at[rows])
    for n in range(u_parts):
        rows = slice(n * u_step, (n + 1) * u_step)
        loads[parts + n].wait()
        up_f[rows] = u_v[rows, :hidden].astype(F32)
        qkv_f[rows] = u_v[rows, hidden : hidden + 3 * width].astype(F32)
        proj_f[rows] = u_v[rows, hidden + 3 * width :].astype(F32)
        for src, dst in ((up_f, up_o), (qkv_f, qkv_o), (proj_f, proj_o)):
            store(src.at[rows], dst.at[rows])
    padded = out_p.shape[0] // images
    slots = slots_images // images
    for n, (src, dst, final) in enumerate(((out_v, out_r, out_o), (dx_v, dx_r, dx_o))):
        loads[parts + u_parts + n].wait()
        for i in range(images):
            block = src[i * padded : i * padded + padded].astype(F32)[:slots]
            for t in range(width // 128):
                wide[t, pl.ds(i, slots, stride=images)] = block[:, t * 128 : (t + 1) * 128]
        for t in range(width // 128):
            dst[:, t * 128 : (t + 1) * 128] = wide[t].astype(BF)
        store(dst, final)
    if with_vec:
        core = lax.axis_index("fsdp")
        half = width // 2
        own = aligned(core * half, half, half)
        for ref, row in zip(vec_o[:6], (6, 7, 3, 1, 2, 0)):
            ref[...] = vec[row : row + 1, own].reshape(half)
        vec_o[6][...] = vec[pl.ds(4 + core, 1)].reshape(width)
        for n in range(2):
            vec_o[7][n * width : (n + 1) * width] = vec[pl.ds(8 + 2 * core + n, 1)].reshape(width)
    for copy in stores:
        copy.wait()


def finish(with_vec, images, slots, hidden, d, u, out_p, dx_p, vec):
    width = d.shape[1]
    vm = pl.BlockSpec(memory_space=pltpu.VMEM)
    hbm = pl.BlockSpec(memory_space=pl.ANY)
    sds = jax.ShapeDtypeStruct
    rows = u.shape[0]
    outs = [
        sds(d.shape, F32), sds((rows, hidden), F32), sds((rows, 3 * width), F32), sds((rows, width), F32),
        sds((slots * images, width), BF), sds((slots * images, width), BF),
    ]
    small = [sds((width // 2,), F32)] * 6 + [sds((width,), F32), sds((2 * width,), F32)] if with_vec else []
    return pl.pallas_call(
        functools.partial(finish_kernel, with_vec, images),
        out_shape=outs + small,
        in_specs=[hbm] * 4 + [vm],
        out_specs=[hbm] * 6 + [vm] * len(small),
        scratch_shapes=[
            pltpu.VMEM(d.shape, BF), pltpu.VMEM(u.shape, BF), pltpu.VMEM(out_p.shape, BF), pltpu.VMEM(out_p.shape, BF),
            *(pltpu.VMEM(out.shape, out.dtype) for out in outs[:4]), pltpu.VMEM((width // 128, slots * images, 128), F32),
            *(pltpu.VMEM(out.shape, out.dtype) for out in outs[4:]),
            pltpu.SemaphoreType.DMA((10,)), pltpu.SemaphoreType.DMA((18,)),
        ],
        compiler_params=pltpu.CompilerParams(vmem_limit_bytes=60 << 20),
        cost_estimate=pl.CostEstimate(flops=0, bytes_accessed=31_000_000, transcendentals=0),
        name="finish",
    )(d, u, out_p, dx_p, vec)


def on_device(n_dp, n_fsdp, *args):
    names = (
        "tokens", "tissue", "norm1_gain", "norm1_shift", "qkv_matrix", "qkv_shift", "proj_matrix", "proj_shift",
        "norm2_gain", "norm2_shift", "up_matrix", "up_shift", "down_matrix", "down_shift", "cotangent",
    )
    arg = dict(zip(names, args, strict=True))
    images, slots, width = arg["tokens"].shape
    exchange = n_dp == 16 and n_fsdp == 2
    vectors = [arg[name] for name in VECTORS]
    mats = [arg[name] for name in ("qkv_matrix", "proj_matrix", "up_matrix", "down_matrix")]
    if not exchange:
        packed = jnp.concatenate(vectors).astype(F32)
        vectors = [lax.all_gather(jnp.broadcast_to(packed, (8, packed.shape[0])), "fsdp", axis=0)]
        mats = [lax.all_gather(mat, "fsdp", axis=0, tiled=True) for mat in mats]
    n1, r1, cotp, first, qkv, pt, ho, res, s2, n2, r2, tb, qkv_w, proj_w, up, down, vecs = front(
        exchange, arg["tokens"], arg["cotangent"], arg["tissue"], vectors, *mats
    )
    out_p, dx_p, d_sum, u_sum, v_sum = back(
        exchange, s2, res, cotp, up, down, ho, proj_w, qkv, pt, first, qkv_w, n1, n2, r1, r2, tb, vecs
    )
    hidden = arg["up_matrix"].shape[1]
    if not exchange:
        d_sum = lax.psum_scatter(d_sum, "fsdp", scatter_dimension=0, tiled=True)
        u_sum = lax.psum_scatter(u_sum, "fsdp", scatter_dimension=0, tiled=True)
        d_sum, u_sum = lax.psum((d_sum, u_sum), "dp")
        v_sum = lax.psum(v_sum, ("dp", "fsdp"))

    d_f, up_f, qkv_f, proj_f, out_r, dx_r, *small = finish(
        exchange, images, slots, hidden, d_sum, u_sum, out_p, dx_p, v_sum
    )

    def own(v):
        size = v.shape[0] // n_fsdp
        return lax.dynamic_slice(v, (lax.axis_index("fsdp") * size,), (size,))

    def rows_of(v):
        return v.reshape(slots, images, width).transpose(1, 0, 2)

    if not exchange:
        small = [own(v_sum[row]) for row in (6, 7, 3, 1, 2, 0)]
        small += [own(v_sum[4:6].reshape(-1)), own(v_sum[8:12].reshape(-1))]
    n1_g, n1_b, proj_b, n2_g, n2_b, down_b, qkv_b, up_b = small
    return (
        rows_of(out_r), rows_of(dx_r), n1_g, n1_b, qkv_f, qkv_b, proj_f, proj_b, n2_g, n2_b, up_f, up_b, d_f, down_b,
    )


def solution(mesh):
    rows = P(("dp", "fsdp"), None, None)
    vec, mat = P("fsdp"), P("fsdp", None)
    weights = (vec, vec, mat, vec, mat, vec, vec, vec, mat, vec, mat, vec)
    return jax.shard_map(
        functools.partial(on_device, mesh.shape["dp"], mesh.shape["fsdp"]),
        mesh=mesh,
        in_specs=(rows, P(("dp", "fsdp"), None)) + weights + (rows,),
        out_specs=(rows, rows) + weights,
        check_vma=False,
    )
```

```python
import functools

import jax
import jax.numpy as jnp
from jax import lax
from jax.experimental import pallas as pl
from jax.experimental.pallas import tpu as pltpu
from jax.sharding import PartitionSpec as P

HEADS = 12
EPS = 1e-06
BF = jnp.bfloat16
F32 = jnp.float32
MESH = pl.DeviceIdType.MESH
ERF = (0.254829592, -0.284496736, 1.421413741, -1.453152027, 1.061405429)


def dot(a, b, ca, cb):
    return lax.dot_general(a, b, (((ca,), (cb,)), ((), ())), preferred_element_type=F32)


def aligned(start, size, step):
    if isinstance(start, int):
        return pl.ds(start, size)
    return pl.ds(pl.multiple_of(start, step), size)


def gelu_both(h):
    t = 1.0 / (1.0 + (0.3275911 * 0.7071067811865476) * jnp.abs(h))
    e = jnp.exp(-0.5 * h * h)
    tail = t * (ERF[0] + t * (ERF[1] + t * (ERF[2] + t * (ERF[3] + t * ERF[4])))) * (0.5 * e)
    cdf = jnp.where(h >= 0, 1.0 - tail, tail)
    return h * cdf, cdf + h * e * 0.3989422804014327


def normalized(v):
    mean = jnp.mean(v, axis=-1, keepdims=True)
    centred = v - mean
    var = jnp.mean(centred * centred, axis=-1, keepdims=True)
    rstd = lax.rsqrt(var + EPS)
    return centred * rstd, rstd


VECTORS = (
    "norm1_gain", "norm1_shift", "qkv_shift", "proj_shift", "norm2_gain", "norm2_shift", "up_shift", "down_shift",
)


def unpack(vecs, width, hidden):
    cores = vecs.shape[0]
    sizes = dict(qkv_shift=2 * width, up_shift=hidden)
    out, at = {}, 0
    for name in VECTORS:
        size = sizes.get(name, width) // cores
        out[name] = jnp.concatenate([vecs[core, 0:1, at : at + size] for core in range(cores)], axis=1)
        at += size
    return out


def head_masks(scale):
    lane = lax.broadcasted_iota(jnp.int32, (1, 128), 1)
    return [
        jnp.where(lane < 64, scale, 0.0).astype(BF),
        jnp.where(lane >= 64, scale, 0.0).astype(BF),
    ]


def front_kernel(
    remote, n_vec, *refs
):
    vec_in, refs = refs[:n_vec], refs[n_vec:]
    (
    x_hbm, cot_hbm, tissue, qkv_s, proj_s, up_s, down_s,
    n1_o, r1_o, cotp_o, first_o, qkv_o, pt_o, ho_o, res_o, s2_o, n2_o, r2_o, tb_o, qkv_wo, proj_wo, up_wo, down_wo,
    vecs_o, raw, wide, xp, cotp, first, qkv_w, qkv, pt, ho, proj_w, res, s2, tb, n1, r1, n2, r2, vecs, g1, b1, qkv_b,
    proj_b, g2, b2, packed_v, sem, osem, psem, send_sem, recv_sem, *ff_w,
    ) = refs
    images, slots = tissue.shape
    width = xp.shape[1]
    padded = xp.shape[0] // images
    scores_w = pt.shape[-1]
    hidden = up_s.shape[1]

    loads = {
        "x": pltpu.make_async_copy(x_hbm, raw, sem.at[0]),
        "cot": pltpu.make_async_copy(cot_hbm, raw, sem.at[3]),
    }
    loads["x"].start()
    sends = {}
    if remote:
        up, down = ff_w
        at = 0
        for ref in vec_in:
            size = ref.shape[0]
            packed_v[0:1, at : at + size] = ref[...].astype(F32).reshape(1, size)
            at += size
        dp, core = lax.axis_index("dp"), lax.axis_index("fsdp")
        barrier = pltpu.get_barrier_semaphore()
        pl.semaphore_signal(barrier, inc=1, device_id=(dp, 1 - core), device_id_type=MESH)
        pl.semaphore_wait(barrier, 1)
        parts = (("vecs", packed_v, vecs), ("qkv_w", qkv_s, qkv_w), ("proj_w", proj_s, proj_w), ("up", up_s, up), ("down", down_s, down))
        for n, (name, src, dst) in enumerate(parts):
            if name == "vecs":
                here = dst.at[core]
            else:
                share = src.shape[0]
                here = dst.at[aligned(core * share, share, share)]
            sends[name] = pltpu.make_async_remote_copy(
                src_ref=src, dst_ref=here, send_sem=send_sem.at[n], recv_sem=recv_sem.at[n],
                device_id=(dp, 1 - core), device_id_type=MESH,
            )
            sends[name].start()
            loads[name] = pltpu.make_async_copy(src, here, sem.at[4 + n])
            loads[name].start()
    else:
        loads["vecs"] = pltpu.make_async_copy(vec_in[0], vecs, sem.at[4])
        loads["qkv_w"] = pltpu.make_async_copy(qkv_s, qkv_w, sem.at[1])
        loads["proj_w"] = pltpu.make_async_copy(proj_s, proj_w, sem.at[2])
        for name in ("vecs", "qkv_w", "proj_w"):
            loads[name].start()

    def arrive(name):
        loads[name].wait()
        if remote:
            sends[name].wait()

    arrive("vecs")
    vec = unpack(vecs, width, hidden)
    for ref, name in (
        (g1, "norm1_gain"), (b1, "norm1_shift"), (qkv_b, "qkv_shift"), (proj_b, "proj_shift"), (g2, "norm2_gain"), (b2, "norm2_shift"),
    ):
        ref[...] = vec[name]
    stores = []

    def store(n, src, dst):
        copy = pltpu.make_async_copy(src, dst, osem.at[n])
        copy.start()
        stores.append(copy)

    pad_rows = jnp.zeros((padded - slots, width), F32)

    def widen():
        step = raw.shape[0] // 14

        @pl.loop(0, 14)
        def _(n):
            rows = aligned(n * step, step, step)
            for t in range(width // 128):
                wide[t, rows] = raw[rows, t * 128 : (t + 1) * 128].astype(F32)

    def image(i):
        parts = [wide[t, pl.ds(i, slots, stride=images)] for t in range(width // 128)]
        return jnp.concatenate([jnp.concatenate(parts, axis=1), pad_rows], axis=0)

    loads["x"].wait()
    widen()
    loads["cot"].start()

    @pl.loop(0, images)
    def _(i):
        rows = aligned(i * padded, padded, 16)
        block = image(i)
        xp[rows] = block.astype(BF)
        n, rstd = normalized(block)
        n1[rows] = n.astype(BF)
        r1[i] = jnp.broadcast_to(rstd, (padded, 128))
        first[rows] = (n * g1[...] + b1[...]).astype(BF)
        t_row = jnp.concatenate(
            [tissue[pl.ds(i, 1)].astype(F32), jnp.zeros((1, padded - slots), F32)], axis=1
        )
        tb[i] = jnp.broadcast_to(t_row, (128, padded)).T

    store(0, n1, n1_o)
    store(8, r1, r1_o)
    loads["cot"].wait()
    widen()

    @pl.loop(0, images)
    def _(i):
        cotp[aligned(i * padded, padded, 16)] = image(i).astype(BF)

    store(7, cotp, cotp_o)
    store(1, first, first_o)
    store(2, tb, tb_o)
    arrive("qkv_w")
    if remote:
        store(11, qkv_w, qkv_wo)
        store(12, vecs, vecs_o)
    for part in range(3):
        cols = slice(part * width, (part + 1) * width)
        prod = dot(first[...], qkv_w[:, cols], 1, 0)
        if part == 0:
            prod = prod + qkv_b[:, :width]
        if part == 2:
            prod = prod + qkv_b[:, width:]
        qkv[:, cols] = prod.astype(BF)
    store(3, qkv, qkv_o)

    scaled = head_masks(0.125)
    ones = head_masks(1.0)

    @pl.loop(0, images)
    def _(i):
        rows = aligned(i * padded, padded, 16)
        slot = lax.rem(i, 2)
        out = pltpu.make_async_copy(pt.at[slot], pt_o.at[i], psem.at[slot])

        @pl.when(i >= 2)
        def _():
            out.wait()

        t = tb[i]
        valid = jnp.concatenate([t, t[:, : scores_w - 128]], axis=1) > 0
        for pair in range(HEADS // 2):
            cols = [slice(b * width + pair * 128, b * width + pair * 128 + 128) for b in range(3)]
            q, k, v = qkv[rows, cols[0]], qkv[rows, cols[1]], qkv[rows, cols[2]]
            mixed = None
            for h in range(2):
                st = jnp.where(valid, dot(k * scaled[h], q, 1, 1), -1e30)
                e = jnp.exp(st - jnp.max(st, axis=0, keepdims=True))
                probs = (e * (1.0 / jnp.sum(e, axis=0, keepdims=True))).astype(BF)
                pt[slot, pair * 2 + h] = probs
                part = dot(probs, v * ones[h], 0, 0)
                mixed = part if mixed is None else mixed + part
            ho[rows, cols[0]] = (mixed * t).astype(BF)
        out.start()

    if remote:
        arrive("up")
        store(14, up, up_wo)
        arrive("down")
        store(15, down, down_wo)
    store(4, ho, ho_o)
    arrive("proj_w")
    if remote:
        store(13, proj_w, proj_wo)
    res[...] = dot(ho[...], proj_w[...], 1, 0)

    half = images // 2
    for part in range(2):

        @pl.loop(part * half, (part + 1) * half)
        def _(i):
            rows = aligned(i * padded, padded, 16)
            total = xp[rows].astype(F32) + res[rows] + proj_b[...]
            res[rows] = total
            n, rstd = normalized(total)
            n2[rows] = n.astype(BF)
            r2[i] = jnp.broadcast_to(rstd, (padded, 128))
            s2[rows] = (n * g2[...] + b2[...]).astype(BF)

        done = slice(part * half * padded, (part + 1) * half * padded)
        for n, (src, dst) in enumerate(((s2, s2_o), (res, res_o), (n2, n2_o))):
            store(16 + 3 * part + n, src.at[done], dst.at[done])
    store(10, r2, r2_o)
    for slot in range(2):
        pltpu.make_async_copy(pt.at[slot], pt_o.at[0], psem.at[slot]).wait()
    for copy in stores:
        copy.wait()


def front(remote, tokens, cot, tissue, vectors, qkv_w, proj_w, up, down):
    images, slots, width = tokens.shape
    tokens, cot = (v.transpose(1, 0, 2).reshape(slots * images, width) for v in (tokens, cot))
    padded = -(-slots // 16) * 16
    rows = images * padded
    cores = 2 if remote else vectors[0].shape[0]
    hidden = up.shape[1]
    vm = pl.BlockSpec(memory_space=pltpu.VMEM)
    hbm = pl.BlockSpec(memory_space=pl.ANY)
    sds = jax.ShapeDtypeStruct
    flat, col = sds((rows, width), BF), sds((images, padded, 128), F32)
    vecs_shape = (cores, 8, sum(v.shape[-1] for v in vectors))
    outs = [
        flat, col, flat, flat, sds((rows, 3 * width), BF), sds((images, HEADS, padded, padded), BF), flat,
        sds((rows, width), F32), flat, flat, col, col, sds((width, 3 * width), BF), sds((width, width), BF),
        sds((width, hidden), BF), sds((hidden, width), BF), sds(vecs_shape, F32),
    ]
    flat_v, col_v = pltpu.VMEM((rows, width), BF), pltpu.VMEM((images, padded, 128), F32)
    row_v = pltpu.VMEM((1, width), F32)
    dma = pltpu.SemaphoreType.DMA
    params = dict(collective_id=2, has_side_effects=True) if remote else {}
    got = pl.pallas_call(
        functools.partial(front_kernel, remote, len(vectors)),
        out_shape=outs,
        in_specs=[vm if remote else hbm] * len(vectors) + [hbm, hbm, vm, hbm, hbm, hbm, hbm],
        out_specs=[hbm] * len(outs),
        scratch_shapes=[
            pltpu.VMEM((slots * images, width), BF), pltpu.VMEM((width // 128, slots * images, 128), F32), flat_v, flat_v,
            flat_v,
            pltpu.VMEM((width, 3 * width), BF), pltpu.VMEM((rows, 3 * width), BF),
            pltpu.VMEM((2, HEADS, padded, padded), BF), flat_v, pltpu.VMEM((width, width), BF),
            pltpu.VMEM((rows, width), F32), flat_v, col_v, flat_v, col_v, flat_v, col_v, pltpu.VMEM(vecs_shape, F32),
            row_v, row_v, pltpu.VMEM((1, 2 * width), F32), row_v, row_v, row_v,
            pltpu.VMEM(vecs_shape[1:], F32), dma((9,)), dma((22,)), dma((2,)),
            dma((5,)), dma((5,)),
        ] + ([pltpu.VMEM((width, hidden), BF), pltpu.VMEM((hidden, width), BF)] if remote else []),
        compiler_params=pltpu.CompilerParams(vmem_limit_bytes=62 << 20, **params),
        cost_estimate=pl.CostEstimate(flops=13_000_000_000, bytes_accessed=40_000_000, transcendentals=0),
        name="front",
    )(*vectors, tokens, cot, tissue, qkv_w, proj_w, up, down)
    if not remote:
        got = [*got[:12], qkv_w, proj_w, up, down, vectors[0]]
    return got


D_ORDER = ((1, 2, 4), (2, 4, 1), (4, 1, 2), (1, 2, 4), (2, 4, 1), (4, 1, 2))
U_ORDER = ((4, 1, 2), (1, 2, 4), (2, 4, 1), (4, 1, 2), (1, 2, 4), (2, 4, 1), (4, 1, 2), (1, 2, 4), (2, 4, 1), (4, 1, 2), (1, 2, 4), (2, 4, 1))
D_TICKS = (
    (1, 2, 4, 6, 7, 8, 9, 10, 13, 15),
    (3, 4, 6, 8, 9, 10, 11, 13, 16, 19),
    (5, 6, 8, 10, 12, 14, 16, 18, 20, 23),
    (7, 8, 10, 13, 15, 17, 20, 22, 24, 27),
    (9, 10, 14, 17, 19, 21, 23, 24, 27, 35),
    (11, 12, 15, 17, 19, 21, 23, 25, 27, 36),
)
U_TICKS = (
    (1, 2, 4, 6, 7, 8, 10, 12, 14, 20),
    (3, 4, 6, 8, 10, 11, 13, 15, 16, 19),
    (5, 6, 8, 10, 11, 13, 15, 16, 20, 23),
    (7, 8, 10, 12, 14, 16, 19, 20, 22, 25),
    (9, 10, 13, 15, 17, 20, 22, 24, 26, 32),
    (11, 12, 15, 19, 20, 22, 24, 26, 28, 44),
    (15, 16, 21, 23, 25, 27, 30, 39, 52, 63),
    (19, 20, 23, 25, 27, 30, 40, 47, 54, 61),
    (19, 20, 23, 26, 28, 31, 42, 49, 59, 67),
    (22, 23, 27, 33, 43, 51, 57, 62, 66, 71),
    (25, 26, 34, 46, 53, 58, 65, 68, 70, 73),
    (25, 26, 29, 38, 48, 55, 60, 64, 69, 72),
)
V_TICKS = (30, 31, 34, 37, 40, 43)
WORK = 7


class Exchange:
    def __init__(self, r):
        self.r = r
        self.dp = lax.axis_index("dp")
        self.core = lax.axis_index("fsdp")
        self.due = self.plan()
        self.now = 0
        self.sides = {bit: (self.dp // bit) % 2 for bit in (1, 2, 4, 8)}
        self.peers = {bit: self.dp + bit * (1 - 2 * self.sides[bit]) for bit in (1, 2, 4, 8)}

    def other_core(self):
        return (self.dp, 1 - self.core)

    def greet(self):
        barrier = pltpu.get_barrier_semaphore()
        peers = [self.other_core()] + [(self.peers[bit], self.core) for bit in (1, 2, 4, 8)]
        for peer in peers:
            pl.semaphore_signal(barrier, inc=1, device_id=peer, device_id_type=MESH)
        pl.semaphore_wait(barrier, len(peers))

    def at_stage(self, order, k):
        bit = (*order, 8)[k]
        return self.sides[bit], self.peers[bit]

    def d_regions(self, u):
        start, size, out = 0, 256, []
        for k in range(4):
            side, peer = self.at_stage(D_ORDER[u], k)
            size //= 2
            out.append((peer, start + side * size, start + (1 - side) * size, size))
            start = start + side * size
        return out

    def d_copy(self, e, u):
        r = self.r
        sems = dict(send_sem=r.d_send.at[e, u], recv_sem=r.d_recv.at[e, u], device_id_type=MESH)
        if e == 0:
            src = r.d_stage.at[u % 2, aligned((1 - self.core) * 256, 256, 256)]
            return pltpu.make_async_remote_copy(
                src_ref=src, dst_ref=r.d_core.at[u % 2], device_id=self.other_core(), **sems
            )
        k = e - 1 if e <= 4 else 8 - e
        peer, kept, sent, size = self.d_regions(u)[k]
        if e <= 4:
            src, dst = r.d_work.at[u, aligned(sent, size, 16)], r.d_in[k].at[u]
        else:
            src = dst = r.d_out.at[aligned(u * 256 + kept, size, 16)]
            if e == 5:
                src = r.d_work.at[u, aligned(kept, size, 16)]
        return pltpu.make_async_remote_copy(
            src_ref=src, dst_ref=dst, device_id=(peer, self.core), **sems
        )

    def d_event(self, e, u):
        r = self.r
        if e >= 1:
            self.d_copy(e - 1, u).wait()
        if e == 1:
            r.d_work[u] = r.d_stage[u % 2, aligned(self.core * 256, 256, 256)] + r.d_core[u % 2]
        elif 2 <= e <= 5:
            _, kept, _, size = self.d_regions(u)[e - 2]
            r.d_work[u, aligned(kept, size, 16)] += r.d_in[e - 2][u]
        if e == 5:
            self.d_own(u).start()
        if e == 6:
            self.d_own(u).wait()
        if e < 9:
            self.d_copy(e, u).start()

    def d_own(self, u):
        _, kept, _, size = self.d_regions(u)[3]
        return pltpu.make_async_copy(
            self.r.d_work.at[u, aligned(kept, size, 16)],
            self.r.d_out.at[aligned(u * 256 + kept, size, 16)],
            self.r.d_done.at[u],
        )

    def u_blocks(self, u):
        width = self.r.width
        if u < 6:
            return u * 256, 2 * width + u * 256
        tail = [4 * width + b * width + g * 256 for g in range(3) for b in range(3)]
        tail = [7 * width, 7 * width + 256, 7 * width + 512] + tail
        return tail[2 * (u - 6)], tail[2 * (u - 6) + 1]

    def u_regions(self, u):
        height = self.r.width // 2
        sides, peers = zip(*(self.at_stage(U_ORDER[u], k) for k in range(4)))
        block, col, row = sides[0], sides[1] * 128, 0
        out = [
            (peers[0], (0, height, block, 0, 256), (0, height, 1 - block, 0, 256)),
            (peers[1], (0, height, block, col, 128), (0, height, block, 128 - col, 128)),
        ]
        for k in (2, 3):
            height //= 2
            kept, sent = row + sides[k] * height, row + (1 - sides[k]) * height
            out.append((peers[k], (kept, height, block, col, 128), (sent, height, block, col, 128)))
            row = kept
        return out

    @staticmethod
    def u_work(region):
        row, rows, block, col, cols = region
        return aligned(row, rows, 32), aligned(block * 256 + col, cols, 128)

    def u_place(self, u, region):
        row, rows, block, col, cols = region
        first, second = self.u_blocks(u)
        return aligned(row, rows, 32), aligned(first + block * (second - first) + col, cols, 128)

    def u_copy(self, e, u):
        r = self.r
        sems = dict(send_sem=r.u_send.at[e, u], recv_sem=r.u_recv.at[e, u], device_id_type=MESH)
        half = r.width // 2
        if e == 0:
            src = r.u_stage.at[u % 2, aligned((1 - self.core) * half, half, half)]
            return pltpu.make_async_remote_copy(
                src_ref=src, dst_ref=r.u_core.at[u % 3], device_id=self.other_core(), **sems
            )
        k = e - 1 if e <= 4 else 8 - e
        peer, kept, sent = self.u_regions(u)[k]
        if e <= 4:
            rows, cols = self.u_work(sent)
            src, dst = r.u_work.at[u % WORK, rows, cols], r.u_in[k].at[u]
        else:
            src = dst = r.u_out.at[self.u_place(u, kept)]
            if e == 5:
                rows, cols = self.u_work(kept)
                src = r.u_work.at[u % WORK, rows, cols]
        return pltpu.make_async_remote_copy(
            src_ref=src, dst_ref=dst, device_id=(peer, self.core), **sems
        )

    def u_event(self, e, u):
        r = self.r
        half = r.width // 2
        if e >= 1:
            self.u_copy(e - 1, u).wait()
        if e == 1:
            r.u_work[u % WORK] = r.u_stage[u % 2, aligned(self.core * half, half, half)] + r.u_core[u % 3]
        elif 2 <= e <= 5:
            rows, cols = self.u_work(self.u_regions(u)[e - 2][1])
            r.u_work[u % WORK, rows, cols] += r.u_in[e - 2][u]
        if e == 5:
            self.u_own(u).start()
        if e == 6:
            self.u_own(u).wait()
        if e < 9:
            self.u_copy(e, u).start()

    def u_own(self, u):
        kept = self.u_regions(u)[3][1]
        rows, cols = self.u_work(kept)
        return pltpu.make_async_copy(
            self.r.u_work.at[u % WORK, rows, cols], self.r.u_out.at[self.u_place(u, kept)], self.r.u_done.at[u]
        )

    def v_copy(self, e):
        r = self.r
        peer = self.other_core() if e == 0 else (self.peers[1 << (e - 1)], self.core)
        return pltpu.make_async_remote_copy(
            src_ref=r.v_sum.at[e], dst_ref=r.v_in.at[e], send_sem=r.v_send.at[e],
            recv_sem=r.v_recv.at[e], device_id=peer, device_id_type=MESH,
        )

    def v_event(self, e, u=0):
        r = self.r
        if e >= 1:
            self.v_copy(e - 1).wait()
            r.v_sum[e] = r.v_sum[e - 1] + r.v_in[e - 1]
        if e < 5:
            self.v_copy(e).start()

    def plan(self):
        due = {}
        for event, table in ((self.d_event, D_TICKS), (self.u_event, U_TICKS), (self.v_event, (V_TICKS,))):
            for u, ticks in enumerate(table):
                for e, tick in enumerate(ticks):
                    due.setdefault(tick, []).append((-e, u, event))
        return due

    def run(self, tick):
        for e, u, event in sorted(self.due.pop(tick, []), key=lambda item: item[:2]):
            event(-e, u)

    def loop_tick(self, c, chunks, j):
        for k in range(chunks):
            if self.due.get(2 * k + j):

                @pl.when(c == k)
                def _(k=k):
                    self.run(2 * k + j)

        self.now = 2 * chunks - 1

    def tick(self):
        self.now += 1
        self.run(self.now)

    def tail(self, u):
        pass

    def drain(self):
        while self.due:
            self.tick()


class Local:
    def __init__(self, r):
        self.r = r
        self.copies = []

    def greet(self):
        pass

    def d_store(self, u):
        r = self.r
        outs = []
        for half in range(2):
            rows = aligned(half * 2 * r.width + u * 256, 256, 256)
            outs.append(
                pltpu.make_async_copy(r.d_stage.at[lax.rem(u, 2), half * 256 : half * 256 + 256], r.d_out.at[rows], r.d_done.at[half])
            )
        return outs

    def d_event(self, e, u):
        for copy in self.d_store(u):
            copy.start()
        for copy in self.d_store(u):
            copy.wait()

    def blocks(self, u):
        if isinstance(u, int):
            return Exchange.u_blocks(self, u)
        return u * 256, 2 * self.r.width + u * 256

    def u_event(self, e, u):
        r = self.r
        for n, col in enumerate(self.blocks(u)):
            copy = pltpu.make_async_copy(
                r.u_stage.at[lax.rem(u, 2), :, n * 256 : n * 256 + 256],
                r.u_out.at[:, aligned(col, 256, 256)],
                r.u_done.at[n],
            )
            copy.start()
            copy.wait()

    def loop_tick(self, c, chunks, j):
        if j == 1:
            self.d_event(0, c)
            self.u_event(0, c)

    def tick(self):
        pass

    def tail(self, u):
        self.u_event(0, u)

    def drain(self):
        pass


class Refs:
    def __init__(self, names, refs):
        self.__dict__.update(zip(names, refs, strict=True))


def back_kernel(names, exchange, *refs):
    r = Refs(names, refs)
    rows_all, width = r.gs.shape
    r.width = width
    images = r.tb_hbm.shape[0]
    padded = rows_all // images
    chunks = r.up_b.shape[1] // 512
    if exchange:
        r.d_in = [r.d_in0, r.d_in1, r.d_in2, r.d_in3]
        r.u_in = [r.u_in0, r.u_in1, r.u_in2, r.u_in3]
    net = Exchange(r) if exchange else Local(r)

    def load(n, src, dst):
        copy = pltpu.make_async_copy(src, dst, r.load_sem.at[n])
        copy.start()
        return copy

    def up_load(b):
        return load(3 + b, r.up_hbm.at[:, b * width : (b + 1) * width], r.w.at[b * width : (b + 1) * width])

    early = [load(0, r.s2_hbm, r.s), up_load(0), up_load(2), load(1, r.cot_hbm, r.cot)]
    early += [load(7, r.down_hbm, r.w.at[4 * width : 8 * width]), load(2, r.res_hbm, r.acc)]
    up_late = [up_load(1), up_load(3)]
    net.greet()
    vec = unpack(r.vecs, width, r.up_b.shape[1])
    for ref, name in ((r.up_b, "up_shift"), (r.down_b, "down_shift"), (r.g1, "norm1_gain"), (r.g2, "norm2_gain")):
        ref[...] = vec[name]
    r.gs[...] = jnp.zeros_like(r.gs)
    r.vec[...] = jnp.zeros_like(r.vec)
    for copy in early:
        copy.wait()
    late = [load(8, r.ho_hbm, r.h), load(10, r.tb_hbm, r.tb), load(9, r.r2_hbm, r.r2)]

    def pt_copy(it, slot):
        g, half = it // 2, it % 2
        count = images // 2
        return pltpu.make_async_copy(
            r.pt_hbm.at[half * count : (half + 1) * count, g * 4 : g * 4 + 4],
            r.pt.at[slot],
            r.pt_sem.at[slot],
        )

    pt_copy(0, 0).start()

    def part_of(c, half):
        upper = jnp.where(c >= 3, 1, 0)
        block = (2 * half + upper) * width
        cols = aligned((c - 3 * upper) * 256, 256, 256)
        down = aligned(4 * width + half * 2 * width + c * 256, 256, 256)
        return block, cols, down, 8 + 2 * half + upper

    def ff_in(c, half):
        block, cols, down, row = part_of(c, half)
        at = slice(half * 256, half * 256 + 256)
        bias = r.up_b[:, aligned(half * 2 * width + c * 256, 256, 256)]
        hidden = dot(r.s[...], r.w[aligned(block, width, width), cols], 1, 0) + bias
        g_active = dot(r.cot[...], r.w[down], 1, 1)
        active, slope = gelu_both(hidden)
        r.a[:, at] = active.astype(BF)
        g_hidden = (g_active * slope).astype(BF)
        r.b[:, at] = g_hidden
        r.vec[pl.ds(row, 1), cols] = jnp.sum(g_hidden.astype(F32), axis=0, keepdims=True)

    def ff_out(c):
        (block0, cols, down0, _), (block1, _, down1, _) = part_of(c, 0), part_of(c, 1)
        for n in range(width // 256):
            to = slice(n * 256, n * 256 + 256)
            up0, up1 = aligned(block0 + n * 256, 256, 256), aligned(block1 + n * 256, 256, 256)
            r.acc[:, to] += dot(r.a[:, :256], r.w[down0, to], 1, 0) + dot(r.a[:, 256:512], r.w[down1, to], 1, 0)
            r.gs[:, to] += dot(r.b[:, :256], r.w[up0, cols], 1, 1) + dot(r.b[:, 256:512], r.w[up1, cols], 1, 1)

    @pl.loop(0, chunks)
    def _(c):
        @pl.when(c == 3)
        def _():
            for copy in up_late:
                copy.wait()

        ff_in(c, 0)
        ff_in(c, 1)
        ff_out(c)
        net.loop_tick(c, chunks, 0)
        r.d_stage[lax.rem(c, 2)] = dot(r.a[:, :512], r.cot[...], 0, 0).astype(BF)
        r.u_stage[lax.rem(c, 2)] = dot(r.s[...], r.b[:, :512], 0, 0).astype(BF)
        net.loop_tick(c, chunks, 1)

    late2 = []
    for b in range(3):
        src = r.qkv_hbm.at[:, b * width : (b + 1) * width]
        late2.append(load(3 + b, src, r.w.at[b * rows_all : (b + 1) * rows_all]))
    proj_rows = slice(3 * rows_all, 3 * rows_all + width)
    late2.append(load(6, r.proj_hbm, r.w.at[proj_rows]))
    late2.append(load(0, r.first_hbm, r.s))

    def norm_copy(i, slot):
        return pltpu.make_async_copy(
            r.n2_hbm.at[aligned(i * padded, padded, 16)], r.n2.at[slot], r.n2_sem.at[slot]
        )

    norm_copy(0, 0).start()
    net.tick()

    def folded(v):
        return v[:8] + v[8:]

    def norm_back(grad, n, rstd, gain):
        t = grad * gain
        centre = t - jnp.mean(t, axis=-1, keepdims=True) - n * jnp.mean(t * n, axis=-1, keepdims=True)
        return jnp.concatenate([rstd] * (width // 128), axis=1) * centre

    def add_vec(first_row, sums):
        for n, value in enumerate(sums):
            r.vec[first_row + n : first_row + n + 1] += jnp.sum(value, axis=0, keepdims=True)

    for copy in late:
        copy.wait()
    for part in range(2):

        @pl.loop(part * images // 2, (part + 1) * images // 2)
        def _(i):
            slot = lax.rem(i, 2)
            norm_copy(i, slot).wait()

            @pl.when(i + 1 < images)
            def _():
                norm_copy(i + 1, 1 - slot).start()

            sums = [0.0] * 4
            for tile in range(padded // 16):
                rows = aligned(i * padded + tile * 16, 16, 16)
                at = slice(tile * 16, tile * 16 + 16)
                n = r.n2[slot, at].astype(F32)
                grad = r.gs[rows]
                cot = r.cot[rows].astype(F32)
                g_res = cot + norm_back(grad, n, r.r2[i, at], r.g2[...])
                r.gs[rows] = g_res
                low = g_res.astype(BF)
                r.a[rows] = low
                terms = (cot, grad * n, grad, low.astype(F32))
                sums = [total + folded(term) for total, term in zip(sums, terms)]
            add_vec(0, sums)

        net.tick()
    for copy in late2:
        copy.wait()
    qkv_at = [r.cot.at[:width], r.cot.at[width : 2 * width], r.w.at[proj_rows]]
    qkv_src = [r.qkv_w_hbm.at[:, b * width : (b + 1) * width] for b in range(3)]
    qkv_loads = [load(3 + b, qkv_src[b], qkv_at[b]) for b in range(2)]
    p_grad = dot(r.h[...], r.a[...], 0, 0).astype(BF)
    r.u_stage[0] = p_grad[:, :512]
    r.u_stage[1, :, :256] = p_grad[:, 512:]
    net.tail(6)
    net.tick()
    n1_copy = load(8, r.n1_hbm, r.h)
    for n in range(3):
        proj_at = slice(3 * rows_all + n * 256, 3 * rows_all + n * 256 + 256)
        g_heads = dot(r.a[...], r.w[proj_at], 1, 1)
        for i in range(images):
            rows = slice(i * padded, (i + 1) * padded)
            t = jnp.concatenate([r.tb[i]] * 2, axis=1)
            r.b[rows, n * 256 : n * 256 + 256] = (g_heads[rows] * t).astype(BF)
    qkv_loads.append(load(5, qkv_src[2], qkv_at[2]))
    net.tick()

    scaled = head_masks(0.125)
    ones = head_masks(1.0)
    stage = 1
    filled = 1
    for g in range(3):
        for half in range(2):
            it = 2 * g + half
            slot = it % 2
            pt_copy(it, slot).wait()
            if it < 5:
                pt_copy(it + 1, 1 - slot).start()
            for n in range(images // 2):
                i = half * (images // 2) + n
                for p in range(2):
                    cols = slice((2 * g + p) * 128, (2 * g + p + 1) * 128)
                    at = [slice(b * rows_all + i * padded, b * rows_all + (i + 1) * padded) for b in range(3)]
                    q, k, v = r.w[at[0], cols], r.w[at[1], cols], r.w[at[2], cols]
                    gh = r.b[i * padded : (i + 1) * padded, cols]
                    gq = gk = gv = None
                    for h in range(2):
                        low = r.pt[slot, n, 2 * p + h]
                        probs = low.astype(F32)
                        g_probs = dot(v * ones[h], gh, 1, 1)
                        row_dot = jnp.sum(probs * g_probs, axis=0, keepdims=True)
                        g_scores = (probs * (g_probs - row_dot)).astype(BF)
                        parts = (
                            dot(g_scores, k * scaled[h], 0, 0),
                            dot(g_scores, q * scaled[h], 1, 0),
                            dot(low, gh * ones[h], 1, 0),
                        )
                        gq, gk, gv = parts if gq is None else (gq + parts[0], gk + parts[1], gv + parts[2])
                    r.w[at[0], cols] = gq.astype(BF)
                    r.w[at[1], cols] = gk.astype(BF)
                    r.w[at[2], cols] = gv.astype(BF)
            net.tick()
        cols = slice(g * 256, (g + 1) * 256)
        parts = [r.w[b * rows_all : (b + 1) * rows_all, cols] for b in range(3)]
        grads = dot(r.s[...], jnp.concatenate(parts, axis=1), 0, 0).astype(BF)
        for b in range(3):
            r.u_stage[stage, :, filled * 256 : (filled + 1) * 256] = grads[:, b * 256 : (b + 1) * 256]
            if b != 1:
                r.vec[4 + b // 2 : 5 + b // 2, cols] = jnp.sum(parts[b].astype(F32), axis=0, keepdims=True)
            filled += 1
            if filled == 2:
                net.tail(6 + (3 * g + b + 3) // 2)
                stage, filled = 1 - stage, 0
        net.tick()

    r.b[...] = (r.acc[...] + r.down_b[...]).astype(BF)
    out_copy = pltpu.make_async_copy(r.b, r.out_o, r.load_sem.at[7])
    out_copy.start()
    n1_copy.wait()
    r1_copy = load(10, r.r1_hbm, r.tb)
    for b in range(3):
        qkv_loads[b].wait()
        part = dot(r.w[b * rows_all : (b + 1) * rows_all], qkv_at[b][...], 1, 1)
        if b == 0:
            r.acc[...] = part
        else:
            r.acc[...] += part
        net.tick()

    r1_copy.wait()
    for part in range(2):

        @pl.loop(part * images // 2, (part + 1) * images // 2)
        def _(i):
            sums = [0.0] * 2
            for tile in range(padded // 16):
                rows = aligned(i * padded + tile * 16, 16, 16)
                at = slice(tile * 16, tile * 16 + 16)
                n = r.h[rows].astype(F32)
                grad = r.acc[rows]
                r.a[rows] = (r.gs[rows] + norm_back(grad, n, r.tb[i, at], r.g1[...])).astype(BF)
                sums = [total + folded(term) for total, term in zip(sums, (grad * n, grad))]
            add_vec(6, sums)

        if part == 0:
            net.tick()

    dx_copy = pltpu.make_async_copy(r.a, r.dx_o, r.load_sem.at[9])
    dx_copy.start()
    if exchange:
        r.v_sum[0] = r.vec[...]
    net.tick()
    net.drain()
    r.vec_o[...] = r.v_sum[5] if exchange else r.vec[...]
    dx_copy.wait()
    out_copy.wait()


def back(exchange, s2, res, cot, up, down, ho, proj_w, qkv, pt, first, qkv_w, n1, n2, r1, r2, tb, vecs):
    rows, width = s2.shape
    images, padded = tb.shape[:2]
    hidden = up.shape[1]
    vm = pl.BlockSpec(memory_space=pltpu.VMEM)
    hbm = pl.BlockSpec(memory_space=pl.ANY)
    sds = jax.ShapeDtypeStruct
    half = width // 2
    if exchange:
        d_shape, u_shape = (hidden // 2, width), (half, 2 * hidden)
    else:
        d_shape, u_shape = (hidden, width), (width, 2 * hidden)
    ins = dict(
        s2_hbm=s2, res_hbm=res, cot_hbm=cot, up_hbm=up, down_hbm=down, ho_hbm=ho, proj_hbm=proj_w,
        qkv_hbm=qkv, pt_hbm=pt, first_hbm=first, qkv_w_hbm=qkv_w, n1_hbm=n1, n2_hbm=n2, r1_hbm=r1,
        r2_hbm=r2, tb_hbm=tb,
        vecs=vecs,
    )
    outs = dict(
        out_o=sds((rows, width), BF), dx_o=sds((rows, width), BF), d_out=sds(d_shape, BF),
        u_out=sds(u_shape, BF), vec_o=sds((16, width), F32),
    )
    dma = pltpu.SemaphoreType.DMA
    scratch = dict(
        s=pltpu.VMEM((rows, width), BF), cot=pltpu.VMEM((rows, width), BF), a=pltpu.VMEM((rows, width), BF),
        b=pltpu.VMEM((rows, width), BF), h=pltpu.VMEM((rows, width), BF), w=pltpu.VMEM((8 * width, width), BF),
        acc=pltpu.VMEM((rows, width), F32), gs=pltpu.VMEM((rows, width), F32),
        n2=pltpu.VMEM((2, padded, width), BF), r2=pltpu.VMEM((images, padded, 128), F32),
        tb=pltpu.VMEM((images, padded, 128), F32), pt=pltpu.VMEM((2, images // 2, 4, padded, padded), BF),
        up_b=pltpu.VMEM((1, hidden), F32), down_b=pltpu.VMEM((1, width), F32), g1=pltpu.VMEM((1, width), F32),
        g2=pltpu.VMEM((1, width), F32), vec=pltpu.VMEM((16, width), F32), d_stage=pltpu.VMEM((2, 512, width), BF),
        u_stage=pltpu.VMEM((2, width, 512), BF), load_sem=dma((11,)), n2_sem=dma((2,)), pt_sem=dma((2,)),
    )
    if exchange:
        scratch.update(
            d_core=pltpu.VMEM((2, 256, width), BF), u_core=pltpu.VMEM((3, half, 512), BF),
            d_in0=pltpu.VMEM((6, 128, width), BF), d_in1=pltpu.VMEM((6, 64, width), BF),
            d_in2=pltpu.VMEM((6, 32, width), BF), d_in3=pltpu.VMEM((6, 16, width), BF),
            u_in0=pltpu.VMEM((12, half, 256), BF), u_in1=pltpu.VMEM((12, half, 128), BF),
            u_in2=pltpu.VMEM((12, half // 2, 128), BF), u_in3=pltpu.VMEM((12, half // 4, 128), BF),
            d_work=pltpu.VMEM((6, 256, width), BF), u_work=pltpu.VMEM((WORK, half, 512), BF),
            v_sum=pltpu.VMEM((6, 16, width), F32), v_in=pltpu.VMEM((5, 16, width), F32),
            d_send=dma((9, 6)), d_recv=dma((9, 6)), u_send=dma((9, 12)), u_recv=dma((9, 12)),
            v_send=dma((5,)), v_recv=dma((5,)), d_done=dma((6,)), u_done=dma((12,)),
        )
    else:
        scratch.update(d_done=dma((2,)), u_done=dma((2,)))
    small = {"vecs"}
    params = dict(vmem_limit_bytes=63 << 20)
    if exchange:
        params.update(collective_id=1, has_side_effects=True)
    names = [*ins, *outs, *scratch]
    return pl.pallas_call(
        functools.partial(back_kernel, names, exchange),
        out_shape=list(outs.values()),
        in_specs=[vm if name in small else hbm for name in ins],
        out_specs=[hbm] * 4 + [vm],
        scratch_shapes=list(scratch.values()),
        compiler_params=pltpu.CompilerParams(**params),
        cost_estimate=pl.CostEstimate(flops=60_000_000_000, bytes_accessed=60_000_000, transcendentals=0),
        name="back",
    )(*ins.values())


def finish_kernel(
    with_vec, images, d, u, out_p, dx_p, vec, d_o, up_o, qkv_o, proj_o, out_o, dx_o, *rest
):
    vec_o, (d_v, u_v, out_v, dx_v, d_f, up_f, qkv_f, proj_f, wide, out_r, dx_r, sem, osem) = rest[:-13], rest[-13:]
    width = d.shape[1]
    hidden = up_o.shape[1]
    slots_images = out_o.shape[0]
    parts, u_parts = 4, 3
    loads, stores = [], []

    def load(src, dst):
        copy = pltpu.make_async_copy(src, dst, sem.at[len(loads)])
        copy.start()
        loads.append(copy)

    def store(src, dst):
        copy = pltpu.make_async_copy(src, dst, osem.at[len(stores)])
        copy.start()
        stores.append(copy)

    step, u_step = d.shape[0] // parts, u.shape[0] // u_parts
    for n in range(parts):
        load(d.at[n * step : (n + 1) * step], d_v.at[n * step : (n + 1) * step])
    for n in range(u_parts):
        load(u.at[n * u_step : (n + 1) * u_step], u_v.at[n * u_step : (n + 1) * u_step])
    load(out_p, out_v)
    load(dx_p, dx_v)
    for n in range(parts):
        rows = slice(n * step, (n + 1) * step)
        loads[n].wait()
        d_f[rows] = d_v[rows].astype(F32)
        store(d_f.at[rows], d_o.at[rows])
    for n in range(u_parts):
        rows = slice(n * u_step, (n + 1) * u_step)
        loads[parts + n].wait()
        up_f[rows] = u_v[rows, :hidden].astype(F32)
        qkv_f[rows] = u_v[rows, hidden : hidden + 3 * width].astype(F32)
        proj_f[rows] = u_v[rows, hidden + 3 * width :].astype(F32)
        for src, dst in ((up_f, up_o), (qkv_f, qkv_o), (proj_f, proj_o)):
            store(src.at[rows], dst.at[rows])
    padded = out_p.shape[0] // images
    slots = slots_images // images
    for n, (src, dst, final) in enumerate(((out_v, out_r, out_o), (dx_v, dx_r, dx_o))):
        loads[parts + u_parts + n].wait()
        for i in range(images):
            block = src[i * padded : i * padded + padded].astype(F32)[:slots]
            for t in range(width // 128):
                wide[t, pl.ds(i, slots, stride=images)] = block[:, t * 128 : (t + 1) * 128]
        for t in range(width // 128):
            dst[:, t * 128 : (t + 1) * 128] = wide[t].astype(BF)
        store(dst, final)
    if with_vec:
        core = lax.axis_index("fsdp")
        half = width // 2
        own = aligned(core * half, half, half)
        for ref, row in zip(vec_o[:6], (6, 7, 3, 1, 2, 0)):
            ref[...] = vec[row : row + 1, own].reshape(half)
        vec_o[6][...] = vec[pl.ds(4 + core, 1)].reshape(width)
        for n in range(2):
            vec_o[7][n * width : (n + 1) * width] = vec[pl.ds(8 + 2 * core + n, 1)].reshape(width)
    for copy in stores:
        copy.wait()


def finish(with_vec, images, slots, hidden, d, u, out_p, dx_p, vec):
    width = d.shape[1]
    vm = pl.BlockSpec(memory_space=pltpu.VMEM)
    hbm = pl.BlockSpec(memory_space=pl.ANY)
    sds = jax.ShapeDtypeStruct
    rows = u.shape[0]
    outs = [
        sds(d.shape, F32), sds((rows, hidden), F32), sds((rows, 3 * width), F32), sds((rows, width), F32),
        sds((slots * images, width), BF), sds((slots * images, width), BF),
    ]
    small = [sds((width // 2,), F32)] * 6 + [sds((width,), F32), sds((2 * width,), F32)] if with_vec else []
    return pl.pallas_call(
        functools.partial(finish_kernel, with_vec, images),
        out_shape=outs + small,
        in_specs=[hbm] * 4 + [vm],
        out_specs=[hbm] * 6 + [vm] * len(small),
        scratch_shapes=[
            pltpu.VMEM(d.shape, BF), pltpu.VMEM(u.shape, BF), pltpu.VMEM(out_p.shape, BF), pltpu.VMEM(out_p.shape, BF),
            *(pltpu.VMEM(out.shape, out.dtype) for out in outs[:4]), pltpu.VMEM((width // 128, slots * images, 128), F32),
            *(pltpu.VMEM(out.shape, out.dtype) for out in outs[4:]),
            pltpu.SemaphoreType.DMA((10,)), pltpu.SemaphoreType.DMA((18,)),
        ],
        compiler_params=pltpu.CompilerParams(vmem_limit_bytes=60 << 20),
        cost_estimate=pl.CostEstimate(flops=0, bytes_accessed=31_000_000, transcendentals=0),
        name="finish",
    )(d, u, out_p, dx_p, vec)


def on_device(n_dp, n_fsdp, *args):
    names = (
        "tokens", "tissue", "norm1_gain", "norm1_shift", "qkv_matrix", "qkv_shift", "proj_matrix", "proj_shift",
        "norm2_gain", "norm2_shift", "up_matrix", "up_shift", "down_matrix", "down_shift", "cotangent",
    )
    arg = dict(zip(names, args, strict=True))
    images, slots, width = arg["tokens"].shape
    exchange = n_dp == 16 and n_fsdp == 2
    vectors = [arg[name] for name in VECTORS]
    mats = [arg[name] for name in ("qkv_matrix", "proj_matrix", "up_matrix", "down_matrix")]
    if not exchange:
        packed = jnp.concatenate(vectors).astype(F32)
        vectors = [lax.all_gather(jnp.broadcast_to(packed, (8, packed.shape[0])), "fsdp", axis=0)]
        mats = [lax.all_gather(mat, "fsdp", axis=0, tiled=True) for mat in mats]
    n1, r1, cotp, first, qkv, pt, ho, res, s2, n2, r2, tb, qkv_w, proj_w, up, down, vecs = front(
        exchange, arg["tokens"], arg["cotangent"], arg["tissue"], vectors, *mats
    )
    out_p, dx_p, d_sum, u_sum, v_sum = back(
        exchange, s2, res, cotp, up, down, ho, proj_w, qkv, pt, first, qkv_w, n1, n2, r1, r2, tb, vecs
    )
    hidden = arg["up_matrix"].shape[1]
    if not exchange:
        d_sum = lax.psum_scatter(d_sum, "fsdp", scatter_dimension=0, tiled=True)
        u_sum = lax.psum_scatter(u_sum, "fsdp", scatter_dimension=0, tiled=True)
        d_sum, u_sum = lax.psum((d_sum, u_sum), "dp")
        v_sum = lax.psum(v_sum, ("dp", "fsdp"))

    d_f, up_f, qkv_f, proj_f, out_r, dx_r, *small = finish(
        exchange, images, slots, hidden, d_sum, u_sum, out_p, dx_p, v_sum
    )

    def own(v):
        size = v.shape[0] // n_fsdp
        return lax.dynamic_slice(v, (lax.axis_index("fsdp") * size,), (size,))

    def rows_of(v):
        return v.reshape(slots, images, width).transpose(1, 0, 2)

    if not exchange:
        small = [own(v_sum[row]) for row in (6, 7, 3, 1, 2, 0)]
        small += [own(v_sum[4:6].reshape(-1)), own(v_sum[8:12].reshape(-1))]
    n1_g, n1_b, proj_b, n2_g, n2_b, down_b, qkv_b, up_b = small
    return (
        rows_of(out_r), rows_of(dx_r), n1_g, n1_b, qkv_f, qkv_b, proj_f, proj_b, n2_g, n2_b, up_f, up_b, d_f, down_b,
    )


def solution(mesh):
    rows = P(("dp", "fsdp"), None, None)
    vec, mat = P("fsdp"), P("fsdp", None)
    weights = (vec, vec, mat, vec, mat, vec, vec, vec, mat, vec, mat, vec)
    return jax.shard_map(
        functools.partial(on_device, mesh.shape["dp"], mesh.shape["fsdp"]),
        mesh=mesh,
        in_specs=(rows, P(("dp", "fsdp"), None)) + weights + (rows,),
        out_specs=(rows, rows) + weights,
        check_vma=False,
    )
```

```python
import functools

import jax
import jax.numpy as jnp
from jax import lax
from jax.experimental import pallas as pl
from jax.experimental.pallas import tpu as pltpu
from jax.sharding import PartitionSpec as P

HEADS = 12
EPS = 1e-06
BF = jnp.bfloat16
F32 = jnp.float32
MESH = pl.DeviceIdType.MESH
ERF = (0.254829592, -0.284496736, 1.421413741, -1.453152027, 1.061405429)


def dot(a, b, ca, cb):
    return lax.dot_general(a, b, (((ca,), (cb,)), ((), ())), preferred_element_type=F32)


def aligned(start, size, step):
    if isinstance(start, int):
        return pl.ds(start, size)
    return pl.ds(pl.multiple_of(start, step), size)


def gelu_both(h):
    t = 1.0 / (1.0 + (0.3275911 * 0.7071067811865476) * jnp.abs(h))
    e = jnp.exp(-0.5 * h * h)
    tail = t * (ERF[0] + t * (ERF[1] + t * (ERF[2] + t * (ERF[3] + t * ERF[4])))) * (0.5 * e)
    cdf = jnp.where(h >= 0, 1.0 - tail, tail)
    return h * cdf, cdf + h * e * 0.3989422804014327


def normalized(v):
    mean = jnp.mean(v, axis=-1, keepdims=True)
    centred = v - mean
    var = jnp.mean(centred * centred, axis=-1, keepdims=True)
    rstd = lax.rsqrt(var + EPS)
    return centred * rstd, rstd


VECTORS = (
    "norm1_gain", "norm1_shift", "qkv_shift", "proj_shift", "norm2_gain", "norm2_shift", "up_shift", "down_shift",
)


def unpack(vecs, width, hidden):
    cores = vecs.shape[0]
    sizes = dict(qkv_shift=2 * width, up_shift=hidden)
    out, at = {}, 0
    for name in VECTORS:
        size = sizes.get(name, width) // cores
        out[name] = jnp.concatenate([vecs[core, 0:1, at : at + size] for core in range(cores)], axis=1)
        at += size
    return out


def head_masks(scale):
    lane = lax.broadcasted_iota(jnp.int32, (1, 128), 1)
    return [
        jnp.where(lane < 64, scale, 0.0).astype(BF),
        jnp.where(lane >= 64, scale, 0.0).astype(BF),
    ]


def front_kernel(
    remote, n_vec, *refs
):
    vec_in, refs = refs[:n_vec], refs[n_vec:]
    (
    x_hbm, cot_hbm, tissue, qkv_s, proj_s, up_s, down_s,
    n1_o, r1_o, cotp_o, first_o, qkv_o, pt_o, ho_o, res_o, s2_o, n2_o, r2_o, tb_o, qkv_wo, proj_wo, up_wo, down_wo,
    vecs_o, raw, wide, xp, cotp, first, qkv_w, qkv, pt, ho, proj_w, res, s2, tb, n1, r1, n2, r2, vecs, g1, b1, qkv_b,
    proj_b, g2, b2, packed_v, sem, osem, psem, send_sem, recv_sem, *ff_w,
    ) = refs
    images, slots = tissue.shape
    width = xp.shape[1]
    padded = xp.shape[0] // images
    scores_w = pt.shape[-1]
    hidden = up_s.shape[1]

    loads = {
        "x": pltpu.make_async_copy(x_hbm, raw, sem.at[0]),
        "cot": pltpu.make_async_copy(cot_hbm, raw, sem.at[3]),
    }
    loads["x"].start()
    sends = {}
    if remote:
        up, down = ff_w
        at = 0
        for ref in vec_in:
            size = ref.shape[0]
            packed_v[0:1, at : at + size] = ref[...].astype(F32).reshape(1, size)
            at += size
        dp, core = lax.axis_index("dp"), lax.axis_index("fsdp")
        barrier = pltpu.get_barrier_semaphore()
        pl.semaphore_signal(barrier, inc=1, device_id=(dp, 1 - core), device_id_type=MESH)
        pl.semaphore_wait(barrier, 1)
        parts = (("vecs", packed_v, vecs), ("qkv_w", qkv_s, qkv_w), ("proj_w", proj_s, proj_w), ("up", up_s, up), ("down", down_s, down))
        for n, (name, src, dst) in enumerate(parts):
            if name == "vecs":
                here = dst.at[core]
            else:
                share = src.shape[0]
                here = dst.at[aligned(core * share, share, share)]
            sends[name] = pltpu.make_async_remote_copy(
                src_ref=src, dst_ref=here, send_sem=send_sem.at[n], recv_sem=recv_sem.at[n],
                device_id=(dp, 1 - core), device_id_type=MESH,
            )
            sends[name].start()
            loads[name] = pltpu.make_async_copy(src, here, sem.at[4 + n])
            loads[name].start()
    else:
        loads["vecs"] = pltpu.make_async_copy(vec_in[0], vecs, sem.at[4])
        loads["qkv_w"] = pltpu.make_async_copy(qkv_s, qkv_w, sem.at[1])
        loads["proj_w"] = pltpu.make_async_copy(proj_s, proj_w, sem.at[2])
        for name in ("vecs", "qkv_w", "proj_w"):
            loads[name].start()

    def arrive(name):
        loads[name].wait()
        if remote:
            sends[name].wait()

    arrive("vecs")
    vec = unpack(vecs, width, hidden)
    for ref, name in (
        (g1, "norm1_gain"), (b1, "norm1_shift"), (qkv_b, "qkv_shift"), (proj_b, "proj_shift"), (g2, "norm2_gain"), (b2, "norm2_shift"),
    ):
        ref[...] = vec[name]
    stores = []

    def store(n, src, dst):
        copy = pltpu.make_async_copy(src, dst, osem.at[n])
        copy.start()
        stores.append(copy)

    pad_rows = jnp.zeros((padded - slots, width), F32)

    def widen():
        step = raw.shape[0] // 14

        @pl.loop(0, 14)
        def _(n):
            rows = aligned(n * step, step, step)
            for t in range(width // 128):
                wide[t, rows] = raw[rows, t * 128 : (t + 1) * 128].astype(F32)

    def image(i):
        parts = [wide[t, pl.ds(i, slots, stride=images)] for t in range(width // 128)]
        return jnp.concatenate([jnp.concatenate(parts, axis=1), pad_rows], axis=0)

    loads["x"].wait()
    widen()
    loads["cot"].start()

    @pl.loop(0, images)
    def _(i):
        rows = aligned(i * padded, padded, 16)
        block = image(i)
        xp[rows] = block.astype(BF)
        n, rstd = normalized(block)
        n1[rows] = n.astype(BF)
        r1[i] = jnp.broadcast_to(rstd, (padded, 128))
        first[rows] = (n * g1[...] + b1[...]).astype(BF)
        t_row = jnp.concatenate(
            [tissue[pl.ds(i, 1)].astype(F32), jnp.zeros((1, padded - slots), F32)], axis=1
        )
        tb[i] = jnp.broadcast_to(t_row, (128, padded)).T

    store(0, n1, n1_o)
    store(8, r1, r1_o)
    loads["cot"].wait()
    widen()

    @pl.loop(0, images)
    def _(i):
        cotp[aligned(i * padded, padded, 16)] = image(i).astype(BF)

    store(7, cotp, cotp_o)
    store(1, first, first_o)
    store(2, tb, tb_o)
    arrive("qkv_w")
    if remote:
        store(11, qkv_w, qkv_wo)
        store(12, vecs, vecs_o)
    for part in range(3):
        cols = slice(part * width, (part + 1) * width)
        prod = dot(first[...], qkv_w[:, cols], 1, 0)
        if part == 0:
            prod = prod + qkv_b[:, :width]
        if part == 2:
            prod = prod + qkv_b[:, width:]
        qkv[:, cols] = prod.astype(BF)
    store(3, qkv, qkv_o)

    scaled = head_masks(0.125)
    ones = head_masks(1.0)

    @pl.loop(0, images)
    def _(i):
        rows = aligned(i * padded, padded, 16)
        slot = lax.rem(i, 2)
        out = pltpu.make_async_copy(pt.at[slot], pt_o.at[i], psem.at[slot])

        @pl.when(i >= 2)
        def _():
            out.wait()

        t = tb[i]
        valid = jnp.concatenate([t, t[:, : scores_w - 128]], axis=1) > 0
        for pair in range(HEADS // 2):
            cols = [slice(b * width + pair * 128, b * width + pair * 128 + 128) for b in range(3)]
            q, k, v = qkv[rows, cols[0]], qkv[rows, cols[1]], qkv[rows, cols[2]]
            mixed = None
            for h in range(2):
                st = jnp.where(valid, dot(k * scaled[h], q, 1, 1), -1e30)
                e = jnp.exp(st - jnp.max(st, axis=0, keepdims=True))
                probs = (e * (1.0 / jnp.sum(e, axis=0, keepdims=True))).astype(BF)
                pt[slot, pair * 2 + h] = probs
                part = dot(probs, v * ones[h], 0, 0)
                mixed = part if mixed is None else mixed + part
            ho[rows, cols[0]] = (mixed * t).astype(BF)
        out.start()

    if remote:
        arrive("up")
        store(14, up, up_wo)
        arrive("down")
        store(15, down, down_wo)
    store(4, ho, ho_o)
    arrive("proj_w")
    if remote:
        store(13, proj_w, proj_wo)
    res[...] = dot(ho[...], proj_w[...], 1, 0)

    half = images // 2
    for part in range(2):

        @pl.loop(part * half, (part + 1) * half)
        def _(i):
            rows = aligned(i * padded, padded, 16)
            total = xp[rows].astype(F32) + res[rows] + proj_b[...]
            res[rows] = total
            n, rstd = normalized(total)
            n2[rows] = n.astype(BF)
            r2[i] = jnp.broadcast_to(rstd, (padded, 128))
            s2[rows] = (n * g2[...] + b2[...]).astype(BF)

        done = slice(part * half * padded, (part + 1) * half * padded)
        for n, (src, dst) in enumerate(((s2, s2_o), (res, res_o), (n2, n2_o))):
            store(16 + 3 * part + n, src.at[done], dst.at[done])
    store(10, r2, r2_o)
    for slot in range(2):
        pltpu.make_async_copy(pt.at[slot], pt_o.at[0], psem.at[slot]).wait()
    for copy in stores:
        copy.wait()


def front(remote, tokens, cot, tissue, vectors, qkv_w, proj_w, up, down):
    images, slots, width = tokens.shape
    tokens, cot = (v.transpose(1, 0, 2).reshape(slots * images, width) for v in (tokens, cot))
    padded = -(-slots // 16) * 16
    rows = images * padded
    cores = 2 if remote else vectors[0].shape[0]
    hidden = up.shape[1]
    vm = pl.BlockSpec(memory_space=pltpu.VMEM)
    hbm = pl.BlockSpec(memory_space=pl.ANY)
    sds = jax.ShapeDtypeStruct
    flat, col = sds((rows, width), BF), sds((images, padded, 128), F32)
    vecs_shape = (cores, 8, sum(v.shape[-1] for v in vectors))
    outs = [
        flat, col, flat, flat, sds((rows, 3 * width), BF), sds((images, HEADS, padded, padded), BF), flat,
        sds((rows, width), F32), flat, flat, col, col, sds((width, 3 * width), BF), sds((width, width), BF),
        sds((width, hidden), BF), sds((hidden, width), BF), sds(vecs_shape, F32),
    ]
    flat_v, col_v = pltpu.VMEM((rows, width), BF), pltpu.VMEM((images, padded, 128), F32)
    row_v = pltpu.VMEM((1, width), F32)
    dma = pltpu.SemaphoreType.DMA
    params = dict(collective_id=2, has_side_effects=True) if remote else {}
    got = pl.pallas_call(
        functools.partial(front_kernel, remote, len(vectors)),
        out_shape=outs,
        in_specs=[vm if remote else hbm] * len(vectors) + [hbm, hbm, vm, hbm, hbm, hbm, hbm],
        out_specs=[hbm] * len(outs),
        scratch_shapes=[
            pltpu.VMEM((slots * images, width), BF), pltpu.VMEM((width // 128, slots * images, 128), F32), flat_v, flat_v,
            flat_v,
            pltpu.VMEM((width, 3 * width), BF), pltpu.VMEM((rows, 3 * width), BF),
            pltpu.VMEM((2, HEADS, padded, padded), BF), flat_v, pltpu.VMEM((width, width), BF),
            pltpu.VMEM((rows, width), F32), flat_v, col_v, flat_v, col_v, flat_v, col_v, pltpu.VMEM(vecs_shape, F32),
            row_v, row_v, pltpu.VMEM((1, 2 * width), F32), row_v, row_v, row_v,
            pltpu.VMEM(vecs_shape[1:], F32), dma((9,)), dma((22,)), dma((2,)),
            dma((5,)), dma((5,)),
        ] + ([pltpu.VMEM((width, hidden), BF), pltpu.VMEM((hidden, width), BF)] if remote else []),
        compiler_params=pltpu.CompilerParams(vmem_limit_bytes=62 << 20, **params),
        cost_estimate=pl.CostEstimate(flops=13_000_000_000, bytes_accessed=40_000_000, transcendentals=0),
        name="front",
    )(*vectors, tokens, cot, tissue, qkv_w, proj_w, up, down)
    if not remote:
        got = [*got[:12], qkv_w, proj_w, up, down, vectors[0]]
    return got


D_ORDER = ((1, 2, 4), (2, 4, 1), (4, 1, 2), (1, 2, 4), (2, 4, 1), (4, 1, 2))
U_ORDER = ((4, 1, 2), (1, 2, 4), (2, 4, 1), (4, 1, 2), (1, 2, 4), (2, 4, 1), (4, 1, 2), (1, 2, 4), (2, 4, 1), (4, 1, 2), (1, 2, 4), (2, 4, 1))
D_TICKS = (
    (1, 2, 4, 6, 7, 8, 10, 11, 14, 16),
    (3, 4, 6, 8, 9, 10, 12, 14, 16, 20),
    (5, 6, 8, 10, 12, 14, 16, 19, 22, 25),
    (7, 8, 10, 13, 15, 17, 20, 22, 24, 27),
    (9, 10, 14, 16, 18, 21, 23, 25, 28, 31),
    (11, 12, 15, 17, 19, 21, 23, 25, 28, 41),
)
U_TICKS = (
    (1, 2, 4, 6, 7, 8, 10, 11, 15, 21),
    (3, 4, 6, 8, 10, 12, 14, 16, 19, 23),
    (5, 6, 8, 10, 11, 13, 15, 16, 20, 24),
    (7, 8, 10, 13, 15, 17, 20, 22, 25, 29),
    (9, 10, 14, 15, 17, 20, 22, 24, 27, 34),
    (11, 12, 15, 19, 21, 23, 25, 27, 30, 48),
    (15, 16, 21, 24, 26, 28, 31, 42, 53, 67),
    (19, 20, 24, 27, 29, 35, 45, 55, 62, 68),
    (19, 20, 24, 27, 30, 39, 50, 57, 66, 72),
    (22, 23, 27, 30, 36, 44, 52, 59, 63, 69),
    (25, 26, 29, 33, 40, 49, 56, 61, 64, 70),
    (25, 26, 28, 32, 38, 47, 54, 60, 65, 71),
)
V_TICKS = (31, 32, 35, 38, 41, 44)
WORK = 7


class Exchange:
    def __init__(self, r):
        self.r = r
        self.dp = lax.axis_index("dp")
        self.core = lax.axis_index("fsdp")
        self.due = self.plan()
        self.now = 0
        self.sides = {bit: (self.dp // bit) % 2 for bit in (1, 2, 4, 8)}
        self.peers = {bit: self.dp + bit * (1 - 2 * self.sides[bit]) for bit in (1, 2, 4, 8)}

    def other_core(self):
        return (self.dp, 1 - self.core)

    def greet(self):
        barrier = pltpu.get_barrier_semaphore()
        peers = [self.other_core()] + [(self.peers[bit], self.core) for bit in (1, 2, 4, 8)]
        for peer in peers:
            pl.semaphore_signal(barrier, inc=1, device_id=peer, device_id_type=MESH)
        pl.semaphore_wait(barrier, len(peers))

    def at_stage(self, order, k):
        bit = (*order, 8)[k]
        return self.sides[bit], self.peers[bit]

    def d_regions(self, u):
        start, size, out = 0, 256, []
        for k in range(4):
            side, peer = self.at_stage(D_ORDER[u], k)
            size //= 2
            out.append((peer, start + side * size, start + (1 - side) * size, size))
            start = start + side * size
        return out

    def d_copy(self, e, u):
        r = self.r
        sems = dict(send_sem=r.d_send.at[e, u], recv_sem=r.d_recv.at[e, u], device_id_type=MESH)
        if e == 0:
            src = r.d_stage.at[u % 2, aligned((1 - self.core) * 256, 256, 256)]
            return pltpu.make_async_remote_copy(
                src_ref=src, dst_ref=r.d_core.at[u % 2], device_id=self.other_core(), **sems
            )
        k = e - 1 if e <= 4 else 8 - e
        peer, kept, sent, size = self.d_regions(u)[k]
        if e <= 4:
            src, dst = r.d_work.at[u, aligned(sent, size, 16)], r.d_in[k].at[u]
        else:
            src = dst = r.d_out.at[aligned(u * 256 + kept, size, 16)]
            if e == 5:
                src = r.d_work.at[u, aligned(kept, size, 16)]
        return pltpu.make_async_remote_copy(
            src_ref=src, dst_ref=dst, device_id=(peer, self.core), **sems
        )

    def d_event(self, e, u):
        r = self.r
        if e >= 1:
            self.d_copy(e - 1, u).wait()
        if e == 1:
            r.d_work[u] = r.d_stage[u % 2, aligned(self.core * 256, 256, 256)] + r.d_core[u % 2]
        elif 2 <= e <= 5:
            _, kept, _, size = self.d_regions(u)[e - 2]
            r.d_work[u, aligned(kept, size, 16)] += r.d_in[e - 2][u]
        if e == 5:
            self.d_own(u).start()
        if e == 6:
            self.d_own(u).wait()
        if e < 9:
            self.d_copy(e, u).start()

    def d_own(self, u):
        _, kept, _, size = self.d_regions(u)[3]
        return pltpu.make_async_copy(
            self.r.d_work.at[u, aligned(kept, size, 16)],
            self.r.d_out.at[aligned(u * 256 + kept, size, 16)],
            self.r.d_done.at[u],
        )

    def u_blocks(self, u):
        width = self.r.width
        if u < 6:
            return u * 256, 2 * width + u * 256
        tail = [4 * width + b * width + g * 256 for g in range(3) for b in range(3)]
        tail = [7 * width, 7 * width + 256, 7 * width + 512] + tail
        return tail[2 * (u - 6)], tail[2 * (u - 6) + 1]

    def u_regions(self, u):
        height = self.r.width // 2
        sides, peers = zip(*(self.at_stage(U_ORDER[u], k) for k in range(4)))
        block, col, row = sides[0], sides[1] * 128, 0
        out = [
            (peers[0], (0, height, block, 0, 256), (0, height, 1 - block, 0, 256)),
            (peers[1], (0, height, block, col, 128), (0, height, block, 128 - col, 128)),
        ]
        for k in (2, 3):
            height //= 2
            kept, sent = row + sides[k] * height, row + (1 - sides[k]) * height
            out.append((peers[k], (kept, height, block, col, 128), (sent, height, block, col, 128)))
            row = kept
        return out

    @staticmethod
    def u_work(region):
        row, rows, block, col, cols = region
        return aligned(row, rows, 32), aligned(block * 256 + col, cols, 128)

    def u_place(self, u, region):
        row, rows, block, col, cols = region
        first, second = self.u_blocks(u)
        return aligned(row, rows, 32), aligned(first + block * (second - first) + col, cols, 128)

    def u_copy(self, e, u):
        r = self.r
        sems = dict(send_sem=r.u_send.at[e, u], recv_sem=r.u_recv.at[e, u], device_id_type=MESH)
        half = r.width // 2
        if e == 0:
            src = r.u_stage.at[u % 2, aligned((1 - self.core) * half, half, half)]
            return pltpu.make_async_remote_copy(
                src_ref=src, dst_ref=r.u_core.at[u % 3], device_id=self.other_core(), **sems
            )
        k = e - 1 if e <= 4 else 8 - e
        peer, kept, sent = self.u_regions(u)[k]
        if e <= 4:
            rows, cols = self.u_work(sent)
            src, dst = r.u_work.at[u % WORK, rows, cols], r.u_in[k].at[u]
        else:
            src = dst = r.u_out.at[self.u_place(u, kept)]
            if e == 5:
                rows, cols = self.u_work(kept)
                src = r.u_work.at[u % WORK, rows, cols]
        return pltpu.make_async_remote_copy(
            src_ref=src, dst_ref=dst, device_id=(peer, self.core), **sems
        )

    def u_event(self, e, u):
        r = self.r
        half = r.width // 2
        if e >= 1:
            self.u_copy(e - 1, u).wait()
        if e == 1:
            r.u_work[u % WORK] = r.u_stage[u % 2, aligned(self.core * half, half, half)] + r.u_core[u % 3]
        elif 2 <= e <= 5:
            rows, cols = self.u_work(self.u_regions(u)[e - 2][1])
            r.u_work[u % WORK, rows, cols] += r.u_in[e - 2][u]
        if e == 5:
            self.u_own(u).start()
        if e == 6:
            self.u_own(u).wait()
        if e < 9:
            self.u_copy(e, u).start()

    def u_own(self, u):
        kept = self.u_regions(u)[3][1]
        rows, cols = self.u_work(kept)
        return pltpu.make_async_copy(
            self.r.u_work.at[u % WORK, rows, cols], self.r.u_out.at[self.u_place(u, kept)], self.r.u_done.at[u]
        )

    def v_copy(self, e):
        r = self.r
        peer = self.other_core() if e == 0 else (self.peers[1 << (e - 1)], self.core)
        return pltpu.make_async_remote_copy(
            src_ref=r.v_sum.at[e], dst_ref=r.v_in.at[e], send_sem=r.v_send.at[e],
            recv_sem=r.v_recv.at[e], device_id=peer, device_id_type=MESH,
        )

    def v_event(self, e, u=0):
        r = self.r
        if e >= 1:
            self.v_copy(e - 1).wait()
            r.v_sum[e] = r.v_sum[e - 1] + r.v_in[e - 1]
        if e < 5:
            self.v_copy(e).start()

    def plan(self):
        due = {}
        for event, table in ((self.d_event, D_TICKS), (self.u_event, U_TICKS), (self.v_event, (V_TICKS,))):
            for u, ticks in enumerate(table):
                for e, tick in enumerate(ticks):
                    due.setdefault(tick, []).append((-e, u, event))
        return due

    def run(self, tick):
        for e, u, event in sorted(self.due.pop(tick, []), key=lambda item: item[:2]):
            event(-e, u)

    def loop_tick(self, c, chunks, j):
        for k in range(chunks):
            if self.due.get(2 * k + j):

                @pl.when(c == k)
                def _(k=k):
                    self.run(2 * k + j)

        self.now = 2 * chunks - 1

    def tick(self):
        self.now += 1
        self.run(self.now)

    def tail(self, u):
        pass

    def drain(self):
        while self.due:
            self.tick()


class Local:
    def __init__(self, r):
        self.r = r
        self.copies = []

    def greet(self):
        pass

    def d_store(self, u):
        r = self.r
        outs = []
        for half in range(2):
            rows = aligned(half * 2 * r.width + u * 256, 256, 256)
            outs.append(
                pltpu.make_async_copy(r.d_stage.at[lax.rem(u, 2), half * 256 : half * 256 + 256], r.d_out.at[rows], r.d_done.at[half])
            )
        return outs

    def d_event(self, e, u):
        for copy in self.d_store(u):
            copy.start()
        for copy in self.d_store(u):
            copy.wait()

    def blocks(self, u):
        if isinstance(u, int):
            return Exchange.u_blocks(self, u)
        return u * 256, 2 * self.r.width + u * 256

    def u_event(self, e, u):
        r = self.r
        for n, col in enumerate(self.blocks(u)):
            copy = pltpu.make_async_copy(
                r.u_stage.at[lax.rem(u, 2), :, n * 256 : n * 256 + 256],
                r.u_out.at[:, aligned(col, 256, 256)],
                r.u_done.at[n],
            )
            copy.start()
            copy.wait()

    def loop_tick(self, c, chunks, j):
        if j == 1:
            self.d_event(0, c)
            self.u_event(0, c)

    def tick(self):
        pass

    def tail(self, u):
        self.u_event(0, u)

    def drain(self):
        pass


class Refs:
    def __init__(self, names, refs):
        self.__dict__.update(zip(names, refs, strict=True))


def back_kernel(names, exchange, *refs):
    r = Refs(names, refs)
    rows_all, width = r.gs.shape
    r.width = width
    images = r.tb_hbm.shape[0]
    padded = rows_all // images
    chunks = r.up_b.shape[1] // 512
    if exchange:
        r.d_in = [r.d_in0, r.d_in1, r.d_in2, r.d_in3]
        r.u_in = [r.u_in0, r.u_in1, r.u_in2, r.u_in3]
    net = Exchange(r) if exchange else Local(r)

    def load(n, src, dst):
        copy = pltpu.make_async_copy(src, dst, r.load_sem.at[n])
        copy.start()
        return copy

    def up_load(b):
        return load(3 + b, r.up_hbm.at[:, b * width : (b + 1) * width], r.w.at[b * width : (b + 1) * width])

    early = [load(0, r.s2_hbm, r.s), up_load(0), up_load(2), load(1, r.cot_hbm, r.cot)]
    early += [load(7, r.down_hbm, r.w.at[4 * width : 8 * width]), load(2, r.res_hbm, r.acc)]
    up_late = [up_load(1), up_load(3)]
    net.greet()
    vec = unpack(r.vecs, width, r.up_b.shape[1])
    for ref, name in ((r.up_b, "up_shift"), (r.down_b, "down_shift"), (r.g1, "norm1_gain"), (r.g2, "norm2_gain")):
        ref[...] = vec[name]
    r.gs[...] = jnp.zeros_like(r.gs)
    r.vec[...] = jnp.zeros_like(r.vec)
    for copy in early:
        copy.wait()
    late = [load(8, r.ho_hbm, r.h), load(10, r.tb_hbm, r.tb), load(9, r.r2_hbm, r.r2)]

    def pt_copy(it, slot):
        g, half = it // 2, it % 2
        count = images // 2
        return pltpu.make_async_copy(
            r.pt_hbm.at[half * count : (half + 1) * count, g * 4 : g * 4 + 4],
            r.pt.at[slot],
            r.pt_sem.at[slot],
        )

    pt_copy(0, 0).start()

    def part_of(c, half):
        upper = jnp.where(c >= 3, 1, 0)
        block = (2 * half + upper) * width
        cols = aligned((c - 3 * upper) * 256, 256, 256)
        down = aligned(4 * width + half * 2 * width + c * 256, 256, 256)
        return block, cols, down, 8 + 2 * half + upper

    def ff_in(c, half):
        block, cols, down, row = part_of(c, half)
        at = slice(half * 256, half * 256 + 256)
        bias = r.up_b[:, aligned(half * 2 * width + c * 256, 256, 256)]
        hidden = dot(r.s[...], r.w[aligned(block, width, width), cols], 1, 0) + bias
        g_active = dot(r.cot[...], r.w[down], 1, 1)
        active, slope = gelu_both(hidden)
        r.a[:, at] = active.astype(BF)
        g_hidden = (g_active * slope).astype(BF)
        r.b[:, at] = g_hidden
        r.vec[pl.ds(row, 1), cols] = jnp.sum(g_hidden.astype(F32), axis=0, keepdims=True)

    def ff_out(c):
        (block0, cols, down0, _), (block1, _, down1, _) = part_of(c, 0), part_of(c, 1)
        for n in range(width // 256):
            to = slice(n * 256, n * 256 + 256)
            up0, up1 = aligned(block0 + n * 256, 256, 256), aligned(block1 + n * 256, 256, 256)
            r.acc[:, to] += dot(r.a[:, :256], r.w[down0, to], 1, 0) + dot(r.a[:, 256:512], r.w[down1, to], 1, 0)
            r.gs[:, to] += dot(r.b[:, :256], r.w[up0, cols], 1, 1) + dot(r.b[:, 256:512], r.w[up1, cols], 1, 1)

    @pl.loop(0, chunks)
    def _(c):
        @pl.when(c == 3)
        def _():
            for copy in up_late:
                copy.wait()

        ff_in(c, 0)
        ff_in(c, 1)
        ff_out(c)
        net.loop_tick(c, chunks, 0)
        r.d_stage[lax.rem(c, 2)] = dot(r.a[:, :512], r.cot[...], 0, 0).astype(BF)
        r.u_stage[lax.rem(c, 2)] = dot(r.s[...], r.b[:, :512], 0, 0).astype(BF)
        net.loop_tick(c, chunks, 1)

    late2 = []
    for b in range(3):
        src = r.qkv_hbm.at[:, b * width : (b + 1) * width]
        late2.append(load(3 + b, src, r.w.at[b * rows_all : (b + 1) * rows_all]))
    proj_rows = slice(3 * rows_all, 3 * rows_all + width)
    late2.append(load(6, r.proj_hbm, r.w.at[proj_rows]))
    late2.append(load(0, r.first_hbm, r.s))

    def norm_copy(i, slot):
        return pltpu.make_async_copy(
            r.n2_hbm.at[aligned(i * padded, padded, 16)], r.n2.at[slot], r.n2_sem.at[slot]
        )

    norm_copy(0, 0).start()
    net.tick()

    def folded(v):
        return v[:8] + v[8:]

    def norm_back(grad, n, rstd, gain):
        t = grad * gain
        centre = t - jnp.mean(t, axis=-1, keepdims=True) - n * jnp.mean(t * n, axis=-1, keepdims=True)
        return jnp.concatenate([rstd] * (width // 128), axis=1) * centre

    def add_vec(first_row, sums):
        for n, value in enumerate(sums):
            r.vec[first_row + n : first_row + n + 1] += jnp.sum(value, axis=0, keepdims=True)

    for copy in late:
        copy.wait()
    for part in range(2):

        @pl.loop(part * images // 2, (part + 1) * images // 2)
        def _(i):
            slot = lax.rem(i, 2)
            norm_copy(i, slot).wait()

            @pl.when(i + 1 < images)
            def _():
                norm_copy(i + 1, 1 - slot).start()

            sums = [0.0] * 4
            for tile in range(padded // 16):
                rows = aligned(i * padded + tile * 16, 16, 16)
                at = slice(tile * 16, tile * 16 + 16)
                n = r.n2[slot, at].astype(F32)
                grad = r.gs[rows]
                cot = r.cot[rows].astype(F32)
                g_res = cot + norm_back(grad, n, r.r2[i, at], r.g2[...])
                r.gs[rows] = g_res
                low = g_res.astype(BF)
                r.a[rows] = low
                terms = (cot, grad * n, grad, low.astype(F32))
                sums = [total + folded(term) for total, term in zip(sums, terms)]
            add_vec(0, sums)

        net.tick()
    for copy in late2:
        copy.wait()
    qkv_at = [r.cot.at[:width], r.cot.at[width : 2 * width], r.w.at[proj_rows]]
    qkv_src = [r.qkv_w_hbm.at[:, b * width : (b + 1) * width] for b in range(3)]
    qkv_loads = [load(3 + b, qkv_src[b], qkv_at[b]) for b in range(2)]
    p_grad = dot(r.h[...], r.a[...], 0, 0).astype(BF)
    r.u_stage[0] = p_grad[:, :512]
    r.u_stage[1, :, :256] = p_grad[:, 512:]
    net.tail(6)
    net.tick()
    n1_copy = load(8, r.n1_hbm, r.h)
    for n in range(3):
        proj_at = slice(3 * rows_all + n * 256, 3 * rows_all + n * 256 + 256)
        g_heads = dot(r.a[...], r.w[proj_at], 1, 1)
        for i in range(images):
            rows = slice(i * padded, (i + 1) * padded)
            t = jnp.concatenate([r.tb[i]] * 2, axis=1)
            r.b[rows, n * 256 : n * 256 + 256] = (g_heads[rows] * t).astype(BF)
    qkv_loads.append(load(5, qkv_src[2], qkv_at[2]))
    net.tick()

    scaled = head_masks(0.125)
    ones = head_masks(1.0)
    stage = 1
    filled = 1
    for g in range(3):
        for half in range(2):
            it = 2 * g + half
            slot = it % 2
            pt_copy(it, slot).wait()
            if it < 5:
                pt_copy(it + 1, 1 - slot).start()
            for n in range(images // 2):
                i = half * (images // 2) + n
                for p in range(2):
                    cols = slice((2 * g + p) * 128, (2 * g + p + 1) * 128)
                    at = [slice(b * rows_all + i * padded, b * rows_all + (i + 1) * padded) for b in range(3)]
                    q, k, v = r.w[at[0], cols], r.w[at[1], cols], r.w[at[2], cols]
                    gh = r.b[i * padded : (i + 1) * padded, cols]
                    gq = gk = gv = None
                    for h in range(2):
                        low = r.pt[slot, n, 2 * p + h]
                        probs = low.astype(F32)
                        g_probs = dot(v * ones[h], gh, 1, 1)
                        row_dot = jnp.sum(probs * g_probs, axis=0, keepdims=True)
                        g_scores = (probs * (g_probs - row_dot)).astype(BF)
                        parts = (
                            dot(g_scores, k * scaled[h], 0, 0),
                            dot(g_scores, q * scaled[h], 1, 0),
                            dot(low, gh * ones[h], 1, 0),
                        )
                        gq, gk, gv = parts if gq is None else (gq + parts[0], gk + parts[1], gv + parts[2])
                    r.w[at[0], cols] = gq.astype(BF)
                    r.w[at[1], cols] = gk.astype(BF)
                    r.w[at[2], cols] = gv.astype(BF)
            net.tick()
        cols = slice(g * 256, (g + 1) * 256)
        parts = [r.w[b * rows_all : (b + 1) * rows_all, cols] for b in range(3)]
        grads = dot(r.s[...], jnp.concatenate(parts, axis=1), 0, 0).astype(BF)
        for b in range(3):
            r.u_stage[stage, :, filled * 256 : (filled + 1) * 256] = grads[:, b * 256 : (b + 1) * 256]
            if b != 1:
                r.vec[4 + b // 2 : 5 + b // 2, cols] = jnp.sum(parts[b].astype(F32), axis=0, keepdims=True)
            filled += 1
            if filled == 2:
                net.tail(6 + (3 * g + b + 3) // 2)
                stage, filled = 1 - stage, 0
        net.tick()

    r.b[...] = (r.acc[...] + r.down_b[...]).astype(BF)
    out_copy = pltpu.make_async_copy(r.b, r.out_o, r.load_sem.at[7])
    out_copy.start()
    net.tick()
    n1_copy.wait()
    r1_copy = load(10, r.r1_hbm, r.tb)
    for b in range(3):
        qkv_loads[b].wait()
        part = dot(r.w[b * rows_all : (b + 1) * rows_all], qkv_at[b][...], 1, 1)
        if b == 0:
            r.acc[...] = part
        else:
            r.acc[...] += part
        net.tick()

    r1_copy.wait()
    for part in range(2):

        @pl.loop(part * images // 2, (part + 1) * images // 2)
        def _(i):
            sums = [0.0] * 2
            for tile in range(padded // 16):
                rows = aligned(i * padded + tile * 16, 16, 16)
                at = slice(tile * 16, tile * 16 + 16)
                n = r.h[rows].astype(F32)
                grad = r.acc[rows]
                r.a[rows] = (r.gs[rows] + norm_back(grad, n, r.tb[i, at], r.g1[...])).astype(BF)
                sums = [total + folded(term) for total, term in zip(sums, (grad * n, grad))]
            add_vec(6, sums)

        if part == 0:
            net.tick()

    dx_copy = pltpu.make_async_copy(r.a, r.dx_o, r.load_sem.at[9])
    dx_copy.start()
    if exchange:
        r.v_sum[0] = r.vec[...]
    net.tick()
    net.drain()
    r.vec_o[...] = r.v_sum[5] if exchange else r.vec[...]
    dx_copy.wait()
    out_copy.wait()


def back(exchange, s2, res, cot, up, down, ho, proj_w, qkv, pt, first, qkv_w, n1, n2, r1, r2, tb, vecs):
    rows, width = s2.shape
    images, padded = tb.shape[:2]
    hidden = up.shape[1]
    vm = pl.BlockSpec(memory_space=pltpu.VMEM)
    hbm = pl.BlockSpec(memory_space=pl.ANY)
    sds = jax.ShapeDtypeStruct
    half = width // 2
    if exchange:
        d_shape, u_shape = (hidden // 2, width), (half, 2 * hidden)
    else:
        d_shape, u_shape = (hidden, width), (width, 2 * hidden)
    ins = dict(
        s2_hbm=s2, res_hbm=res, cot_hbm=cot, up_hbm=up, down_hbm=down, ho_hbm=ho, proj_hbm=proj_w,
        qkv_hbm=qkv, pt_hbm=pt, first_hbm=first, qkv_w_hbm=qkv_w, n1_hbm=n1, n2_hbm=n2, r1_hbm=r1,
        r2_hbm=r2, tb_hbm=tb,
        vecs=vecs,
    )
    outs = dict(
        out_o=sds((rows, width), BF), dx_o=sds((rows, width), BF), d_out=sds(d_shape, BF),
        u_out=sds(u_shape, BF), vec_o=sds((16, width), F32),
    )
    dma = pltpu.SemaphoreType.DMA
    scratch = dict(
        s=pltpu.VMEM((rows, width), BF), cot=pltpu.VMEM((rows, width), BF), a=pltpu.VMEM((rows, width), BF),
        b=pltpu.VMEM((rows, width), BF), h=pltpu.VMEM((rows, width), BF), w=pltpu.VMEM((8 * width, width), BF),
        acc=pltpu.VMEM((rows, width), F32), gs=pltpu.VMEM((rows, width), F32),
        n2=pltpu.VMEM((2, padded, width), BF), r2=pltpu.VMEM((images, padded, 128), F32),
        tb=pltpu.VMEM((images, padded, 128), F32), pt=pltpu.VMEM((2, images // 2, 4, padded, padded), BF),
        up_b=pltpu.VMEM((1, hidden), F32), down_b=pltpu.VMEM((1, width), F32), g1=pltpu.VMEM((1, width), F32),
        g2=pltpu.VMEM((1, width), F32), vec=pltpu.VMEM((16, width), F32), d_stage=pltpu.VMEM((2, 512, width), BF),
        u_stage=pltpu.VMEM((2, width, 512), BF), load_sem=dma((11,)), n2_sem=dma((2,)), pt_sem=dma((2,)),
    )
    if exchange:
        scratch.update(
            d_core=pltpu.VMEM((2, 256, width), BF), u_core=pltpu.VMEM((3, half, 512), BF),
            d_in0=pltpu.VMEM((6, 128, width), BF), d_in1=pltpu.VMEM((6, 64, width), BF),
            d_in2=pltpu.VMEM((6, 32, width), BF), d_in3=pltpu.VMEM((6, 16, width), BF),
            u_in0=pltpu.VMEM((12, half, 256), BF), u_in1=pltpu.VMEM((12, half, 128), BF),
            u_in2=pltpu.VMEM((12, half // 2, 128), BF), u_in3=pltpu.VMEM((12, half // 4, 128), BF),
            d_work=pltpu.VMEM((6, 256, width), BF), u_work=pltpu.VMEM((WORK, half, 512), BF),
            v_sum=pltpu.VMEM((6, 16, width), F32), v_in=pltpu.VMEM((5, 16, width), F32),
            d_send=dma((9, 6)), d_recv=dma((9, 6)), u_send=dma((9, 12)), u_recv=dma((9, 12)),
            v_send=dma((5,)), v_recv=dma((5,)), d_done=dma((6,)), u_done=dma((12,)),
        )
    else:
        scratch.update(d_done=dma((2,)), u_done=dma((2,)))
    small = {"vecs"}
    params = dict(vmem_limit_bytes=63 << 20)
    if exchange:
        params.update(collective_id=1, has_side_effects=True)
    names = [*ins, *outs, *scratch]
    return pl.pallas_call(
        functools.partial(back_kernel, names, exchange),
        out_shape=list(outs.values()),
        in_specs=[vm if name in small else hbm for name in ins],
        out_specs=[hbm] * 4 + [vm],
        scratch_shapes=list(scratch.values()),
        compiler_params=pltpu.CompilerParams(**params),
        cost_estimate=pl.CostEstimate(flops=60_000_000_000, bytes_accessed=60_000_000, transcendentals=0),
        name="back",
    )(*ins.values())


def finish_kernel(
    with_vec, images, d, u, out_p, dx_p, vec, d_o, up_o, qkv_o, proj_o, out_o, dx_o, *rest
):
    vec_o, (d_v, u_v, out_v, dx_v, d_f, up_f, qkv_f, proj_f, wide, out_r, dx_r, sem, osem) = rest[:-13], rest[-13:]
    width = d.shape[1]
    hidden = up_o.shape[1]
    slots_images = out_o.shape[0]
    parts, u_parts = 4, 3
    loads, stores = [], []

    def load(src, dst):
        copy = pltpu.make_async_copy(src, dst, sem.at[len(loads)])
        copy.start()
        loads.append(copy)

    def store(src, dst):
        copy = pltpu.make_async_copy(src, dst, osem.at[len(stores)])
        copy.start()
        stores.append(copy)

    step, u_step = d.shape[0] // parts, u.shape[0] // u_parts
    for n in range(parts):
        load(d.at[n * step : (n + 1) * step], d_v.at[n * step : (n + 1) * step])
    for n in range(u_parts):
        load(u.at[n * u_step : (n + 1) * u_step], u_v.at[n * u_step : (n + 1) * u_step])
    load(out_p, out_v)
    load(dx_p, dx_v)
    for n in range(parts):
        rows = slice(n * step, (n + 1) * step)
        loads[n].wait()
        d_f[rows] = d_v[rows].astype(F32)
        store(d_f.at[rows], d_o.at[rows])
    for n in range(u_parts):
        rows = slice(n * u_step, (n + 1) * u_step)
        loads[parts + n].wait()
        up_f[rows] = u_v[rows, :hidden].astype(F32)
        qkv_f[rows] = u_v[rows, hidden : hidden + 3 * width].astype(F32)
        proj_f[rows] = u_v[rows, hidden + 3 * width :].astype(F32)
        for src, dst in ((up_f, up_o), (qkv_f, qkv_o), (proj_f, proj_o)):
            store(src.at[rows], dst.at[rows])
    padded = out_p.shape[0] // images
    slots = slots_images // images
    for n, (src, dst, final) in enumerate(((out_v, out_r, out_o), (dx_v, dx_r, dx_o))):
        loads[parts + u_parts + n].wait()
        for i in range(images):
            block = src[i * padded : i * padded + padded].astype(F32)[:slots]
            for t in range(width // 128):
                wide[t, pl.ds(i, slots, stride=images)] = block[:, t * 128 : (t + 1) * 128]
        for t in range(width // 128):
            dst[:, t * 128 : (t + 1) * 128] = wide[t].astype(BF)
        store(dst, final)
    if with_vec:
        core = lax.axis_index("fsdp")
        half = width // 2
        own = aligned(core * half, half, half)
        for ref, row in zip(vec_o[:6], (6, 7, 3, 1, 2, 0)):
            ref[...] = vec[row : row + 1, own].reshape(half)
        vec_o[6][...] = vec[pl.ds(4 + core, 1)].reshape(width)
        for n in range(2):
            vec_o[7][n * width : (n + 1) * width] = vec[pl.ds(8 + 2 * core + n, 1)].reshape(width)
    for copy in stores:
        copy.wait()


def finish(with_vec, images, slots, hidden, d, u, out_p, dx_p, vec):
    width = d.shape[1]
    vm = pl.BlockSpec(memory_space=pltpu.VMEM)
    hbm = pl.BlockSpec(memory_space=pl.ANY)
    sds = jax.ShapeDtypeStruct
    rows = u.shape[0]
    outs = [
        sds(d.shape, F32), sds((rows, hidden), F32), sds((rows, 3 * width), F32), sds((rows, width), F32),
        sds((slots * images, width), BF), sds((slots * images, width), BF),
    ]
    small = [sds((width // 2,), F32)] * 6 + [sds((width,), F32), sds((2 * width,), F32)] if with_vec else []
    return pl.pallas_call(
        functools.partial(finish_kernel, with_vec, images),
        out_shape=outs + small,
        in_specs=[hbm] * 4 + [vm],
        out_specs=[hbm] * 6 + [vm] * len(small),
        scratch_shapes=[
            pltpu.VMEM(d.shape, BF), pltpu.VMEM(u.shape, BF), pltpu.VMEM(out_p.shape, BF), pltpu.VMEM(out_p.shape, BF),
            *(pltpu.VMEM(out.shape, out.dtype) for out in outs[:4]), pltpu.VMEM((width // 128, slots * images, 128), F32),
            *(pltpu.VMEM(out.shape, out.dtype) for out in outs[4:]),
            pltpu.SemaphoreType.DMA((10,)), pltpu.SemaphoreType.DMA((18,)),
        ],
        compiler_params=pltpu.CompilerParams(vmem_limit_bytes=60 << 20),
        cost_estimate=pl.CostEstimate(flops=0, bytes_accessed=31_000_000, transcendentals=0),
        name="finish",
    )(d, u, out_p, dx_p, vec)


def on_device(n_dp, n_fsdp, *args):
    names = (
        "tokens", "tissue", "norm1_gain", "norm1_shift", "qkv_matrix", "qkv_shift", "proj_matrix", "proj_shift",
        "norm2_gain", "norm2_shift", "up_matrix", "up_shift", "down_matrix", "down_shift", "cotangent",
    )
    arg = dict(zip(names, args, strict=True))
    images, slots, width = arg["tokens"].shape
    exchange = n_dp == 16 and n_fsdp == 2
    vectors = [arg[name] for name in VECTORS]
    mats = [arg[name] for name in ("qkv_matrix", "proj_matrix", "up_matrix", "down_matrix")]
    if not exchange:
        packed = jnp.concatenate(vectors).astype(F32)
        vectors = [lax.all_gather(jnp.broadcast_to(packed, (8, packed.shape[0])), "fsdp", axis=0)]
        mats = [lax.all_gather(mat, "fsdp", axis=0, tiled=True) for mat in mats]
    n1, r1, cotp, first, qkv, pt, ho, res, s2, n2, r2, tb, qkv_w, proj_w, up, down, vecs = front(
        exchange, arg["tokens"], arg["cotangent"], arg["tissue"], vectors, *mats
    )
    out_p, dx_p, d_sum, u_sum, v_sum = back(
        exchange, s2, res, cotp, up, down, ho, proj_w, qkv, pt, first, qkv_w, n1, n2, r1, r2, tb, vecs
    )
    hidden = arg["up_matrix"].shape[1]
    if not exchange:
        d_sum = lax.psum_scatter(d_sum, "fsdp", scatter_dimension=0, tiled=True)
        u_sum = lax.psum_scatter(u_sum, "fsdp", scatter_dimension=0, tiled=True)
        d_sum, u_sum = lax.psum((d_sum, u_sum), "dp")
        v_sum = lax.psum(v_sum, ("dp", "fsdp"))

    d_f, up_f, qkv_f, proj_f, out_r, dx_r, *small = finish(
        exchange, images, slots, hidden, d_sum, u_sum, out_p, dx_p, v_sum
    )

    def own(v):
        size = v.shape[0] // n_fsdp
        return lax.dynamic_slice(v, (lax.axis_index("fsdp") * size,), (size,))

    def rows_of(v):
        return v.reshape(slots, images, width).transpose(1, 0, 2)

    if not exchange:
        small = [own(v_sum[row]) for row in (6, 7, 3, 1, 2, 0)]
        small += [own(v_sum[4:6].reshape(-1)), own(v_sum[8:12].reshape(-1))]
    n1_g, n1_b, proj_b, n2_g, n2_b, down_b, qkv_b, up_b = small
    return (
        rows_of(out_r), rows_of(dx_r), n1_g, n1_b, qkv_f, qkv_b, proj_f, proj_b, n2_g, n2_b, up_f, up_b, d_f, down_b,
    )


def solution(mesh):
    rows = P(("dp", "fsdp"), None, None)
    vec, mat = P("fsdp"), P("fsdp", None)
    weights = (vec, vec, mat, vec, mat, vec, vec, vec, mat, vec, mat, vec)
    return jax.shard_map(
        functools.partial(on_device, mesh.shape["dp"], mesh.shape["fsdp"]),
        mesh=mesh,
        in_specs=(rows, P(("dp", "fsdp"), None)) + weights + (rows,),
        out_specs=(rows, rows) + weights,
        check_vma=False,
    )
```
